128 devices in a mesh: seq: 16 (over y_lo, x, core), fsdp: 8 (over y_hi, z).
Axes of the slice: x: 4, y: 4 (y_hi: 2, y_lo: 2; y = y_hi * 2 + y_lo), z: 4, core: 2. Of those that a mesh axis runs over, the one named last changes fastest.
Arguments:
- hidden: bfloat16 [8, 2048, 2560], P('fsdp', 'seq'), may hold values from -6 to 6
- queries: bfloat16 [8, 2048, 4096], P('fsdp', 'seq'), may hold values from -6 to 6
- doc_ids: int32 [8, 2048], P('fsdp'), may hold values from 0 to 7, never falling along the last dimension, each value on 1 to 1024 neighbouring positions
- kv_weight: bfloat16 [2560, 1024], P('fsdp'), may hold values from -0.125 to 0.125
- q_gain: float32 [128], replicated, may hold values from 0.5 to 1.5
- k_gain: float32 [128], replicated, may hold values from 0.5 to 1.5
- grad_out: bfloat16 [8, 2048, 4096], P('fsdp', 'seq'), may hold values from -6 to 6
Outputs:
- attended: bfloat16 [8, 2048, 4096], P('fsdp', 'seq')
- grad_queries: bfloat16 [8, 2048, 4096], P('fsdp', 'seq')
- grad_hidden: bfloat16 [8, 2048, 2560], P('fsdp', 'seq')
- grad_weight: bfloat16 [2560, 1024], P(('seq', 'fsdp'))
- grad_qgain: float32 [128], replicated
- grad_kgain: float32 [128], replicated
The draws below stay inside these ranges and needn't reach their ends.
Inputs may be any that keep to these rules, and one draw needn't show every extreme that they name: `doc_ids`: rollout numbers never fall along a pack; each of the 8 rollouts has at least one token and one has exactly 1024.
All inputs are finite; a program needn't handle non-finite values.
Results may differ from the reference program's by a relative error of at most 0.017.
Values may be sent and summed in bfloat16 or wider, within the bound.
A program may use at most 128 MiB of HBM per device.

```python
import math
import jax
import jax.numpy as jnp
import numpy as np
from jax import lax

D = 2560
QH = 32
KVH = 4
HD = 128
DOCS = 8
QW = 4096
KW = 512
PACK = 2048
PACKS = 8
LONGEST = 1024


def block_scale(stream_key, shape, pieces, least, high):
    def one(dim, shards_of):
        heights = jax.random.uniform(jax.random.fold_in(jax.random.fold_in(stream_key, 6), dim), (shards_of,), jnp.float32, least / len(pieces), high / len(pieces))
        return jnp.repeat(jnp.exp(heights), shape[dim] // shards_of).reshape((-1,) + (1,) * (len(shape) - dim - 1))

    loudness = one(*pieces[0])
    for cut in pieces[1:]:
        loudness = loudness * one(*cut)
    return loudness


def length_profile(number_of, total, most, lean):
    loads = [(1 << 20) // math.isqrt(standing ** lean) + 1 for standing in range(2, number_of + 1)]
    spare, counts = total - most - (number_of - 1), [1] * (number_of - 1)
    while spare > 0:
        free = [i for i in range(number_of - 1) if counts[i] < most]
        mass, budget = sum([loads[i] for i in free]), spare
        for i in free:
            extra = min(most - counts[i], max(1, budget * loads[i] // mass), spare)
            counts[i] = counts[i] + extra
            spare = spare - extra
    return np.array([most] + counts)


def uneven(rng, count, total, limit, lean):
    if count == 2:
        one = jax.random.randint(rng, (), max(1, total - limit), min(limit, total - 1) + 1)
        return jnp.stack([one, total - one])
    tallies = jnp.asarray(length_profile(count, total, limit, lean), jnp.int32)
    twos = (count - 1) // 2
    source_of, taker = tallies[1:1 + 2 * twos:2], tallies[2:2 + 2 * twos:2]
    room = jnp.minimum(source_of - 1, limit - taker)
    shifted = jax.random.randint(jax.random.fold_in(rng, 1), (twos,), 0, 1 << 20) % (room + 1)
    tallies = tallies.at[1:1 + 2 * twos:2].set(source_of - shifted).at[2:2 + 2 * twos:2].set(taker + shifted)
    return tallies[jax.random.permutation(jax.random.fold_in(rng, 2), count)]


def scatter_about(rng, dims, deviation, limit, shards=(), held_as=jnp.bfloat16):
    level = block_scale(rng, dims, shards, -0.22, 0.18) if shards else 1.0
    entries = jax.random.normal(rng, dims, jnp.float32) * deviation * level
    return jnp.minimum(jnp.maximum(entries, -limit), limit).astype(held_as)


def setup_inputs(seed: int = 0) -> dict:
    splits = jax.random.split(jax.random.key(seed), 8)
    hidden = scatter_about(splits[0], (PACKS, PACK, D), 1.0, 6.0, ((0, 8), (1, 16)))
    queries = scatter_about(splits[1], (PACKS, PACK, QW), 1.0, 6.0, ((0, 8), (1, 16)))
    doc_ids = jax.vmap(lambda own: jnp.searchsorted(jnp.cumsum(uneven(own, DOCS, PACK, LONGEST, 2)), jnp.arange(PACK), side="right"))(jax.random.split(splits[2], PACKS)).reshape((PACKS, PACK)).astype(jnp.int32)
    kv_weight = scatter_about(splits[3], (D, 2 * KW), D ** -0.5, 0.125, ((0, 8),))
    q_gain = jnp.clip(1.0 + 0.1 * jax.random.normal(splits[4], (HD,), jnp.float32), 0.5, 1.5)
    k_gain = jnp.clip(1.0 + 0.1 * jax.random.normal(splits[5], (HD,), jnp.float32), 0.5, 1.5)
    grad_out = scatter_about(splits[6], (PACKS, PACK, QW), 1.0, 6.0, ((0, 8), (1, 16)))
    return {"hidden": hidden, "queries": queries, "doc_ids": doc_ids, "kv_weight": kv_weight, "q_gain": q_gain, "k_gain": k_gain, "grad_out": grad_out}


epsilon = 1e-06

def normalize(values, gain):
    return values * lax.rsqrt(lax.optimization_barrier(jnp.mean(values * values, axis=-1, keepdims=True)) + epsilon) * gain

def rounded(values):
    return lax.optimization_barrier(values.astype(jnp.bfloat16)).astype(jnp.float32)

def one_pack(hidden, queries, docs, grad_out, kv_weight, q_gain, k_gain):
    pack = docs.shape[0]
    group = QH // KVH
    kv_width = KVH * HD
    scale = 1.0 / math.sqrt(HD)
    projected = jnp.dot(hidden, kv_weight, preferred_element_type=jnp.float32)
    k_raw = projected[:, :kv_width].reshape(pack, KVH, HD)
    keys = rounded(normalize(k_raw, k_gain))
    values = rounded(projected[:, kv_width:]).reshape(pack, KVH, HD)
    q_raw = queries.astype(jnp.float32).reshape(pack, QH, HD)
    q_normed = rounded(normalize(q_raw, q_gain)).reshape(pack, KVH, group, HD)
    d_out = grad_out.astype(jnp.float32).reshape(pack, KVH, group, HD)
    positions = jnp.arange(pack, dtype=jnp.int32)
    live = (docs[:, None] == docs[None, :]) & (positions[None, :] <= positions[:, None])

    def per_head(index):
        q_group = q_normed[:, index]
        k_group = keys[:, index]
        v_group = values[:, index]
        d_group = d_out[:, index]
        scores = jnp.einsum('qjd,kd->jqk', q_group, k_group) * scale
        expd = jnp.where(live[None], jnp.exp(scores), 0.0)
        total = lax.optimization_barrier(jnp.sum(expd, axis=-1))
        numer = jnp.einsum('jqk,kd->qjd', rounded(expd), v_group)
        att = rounded(numer / jnp.transpose(total)[:, :, None])
        delta = lax.optimization_barrier(jnp.sum(d_group * att, axis=-1))
        probs = expd / total[..., None]
        grad_values = jnp.einsum('jqk,qjd->kd', rounded(probs), d_group)
        grad_probs = jnp.einsum('qjd,kd->jqk', d_group, v_group)
        grad_scores = rounded(probs * (grad_probs - jnp.transpose(delta)[..., None]))
        grad_qn = jnp.einsum('jqk,kd->qjd', grad_scores, k_group) * scale
        grad_kn = jnp.einsum('jqk,qjd->kd', grad_scores, q_group) * scale
        return (att, grad_qn, grad_kn, grad_values)
    att, grad_qn, grad_kn, grad_values = lax.map(per_head, jnp.arange(KVH, dtype=jnp.int32))
    attended = jnp.transpose(att, (1, 0, 2, 3)).reshape(pack, QH * HD).astype(jnp.bfloat16)
    grad_qn = jnp.transpose(grad_qn, (1, 0, 2, 3)).reshape(pack, QH, HD)
    grad_kn = jnp.transpose(grad_kn, (1, 0, 2))
    grad_values = jnp.transpose(grad_values, (1, 0, 2)).reshape(pack, kv_width)
    q_value, q_pull = jax.vjp(normalize, q_raw, q_gain)
    grad_qraw, grad_qgain = q_pull(grad_qn)
    k_value, k_pull = jax.vjp(normalize, k_raw, k_gain)
    grad_kraw, grad_kgain = k_pull(grad_kn)
    grad_queries = grad_qraw.reshape(pack, QH * HD).astype(jnp.bfloat16)
    grad_kv = jnp.concatenate([grad_kraw.reshape(pack, kv_width), grad_values], axis=1).astype(jnp.bfloat16)
    grad_hidden = jnp.einsum('tk,rk->tr', grad_kv, kv_weight, preferred_element_type=jnp.float32).astype(jnp.bfloat16)
    weight_terms = jnp.einsum('tr,tk->rk', hidden, grad_kv, preferred_element_type=jnp.float32)
    return (attended, grad_queries, grad_hidden, weight_terms, grad_qgain, grad_kgain)

def reference(hidden, queries, doc_ids, kv_weight, q_gain, k_gain, grad_out):

    def run(index):
        return one_pack(hidden[index], queries[index], doc_ids[index], grad_out[index], kv_weight, q_gain, k_gain)
    attended, grad_queries, grad_hidden, weight_terms, grad_qgain, grad_kgain = lax.map(run, jnp.arange(hidden.shape[0], dtype=jnp.int32))
    grad_weight = lax.optimization_barrier(jnp.sum(weight_terms, axis=0)).astype(jnp.bfloat16)
    return (attended, grad_queries, grad_hidden, grad_weight, lax.optimization_barrier(jnp.sum(grad_qgain, axis=0)), lax.optimization_barrier(jnp.sum(grad_kgain, axis=0)))
```

```python
import math

import jax
import jax.numpy as jnp
from jax import lax
from jax.experimental import pallas as pl
from jax.experimental.pallas import tpu as pltpu
from jax.sharding import PartitionSpec as P

MESH = pl.DeviceIdType.MESH
BF = jnp.bfloat16
F32 = jnp.float32
EPS = 1e-06
TOK = 128
HD = 128
KVH = 4
GROUP = 8
D = 2560
ROWS = 320
WIN = 9
SCALE = 1.0 / math.sqrt(HD)
LOG2E = 1.4426950408889634
NT = (((1,), (1,)), ((), ()))


class Place:
    def __init__(self):
        s = lax.axis_index("seq")
        f = lax.axis_index("fsdp")
        self.s, self.f = s, f
        self.c = lax.rem(s, 2)
        self.x = lax.rem(lax.div(s, 2), 4)
        self.yl = lax.div(s, 8)
        self.yh = lax.div(f, 4)
        self.z = lax.rem(f, 4)
        self.k = lax.div(s, 2)

    def at(self, x=None, yl=None, yh=None, z=None, c=None):
        x = self.x if x is None else x
        yl = self.yl if yl is None else yl
        yh = self.yh if yh is None else yh
        z = self.z if z is None else z
        c = self.c if c is None else c
        return ((yl * 4 + x) * 2 + c, yh * 4 + z)

    def xs(self, d):
        return lax.rem(self.x + d, 4)

    def zs(self, d):
        return lax.rem(self.z + d, 4)


class Net:
    def __init__(self, send, recv):
        self.send, self.recv, self.n = send, recv, 0
        self.sent = []

    def copy(self, src, dst, dev):
        i = self.n
        self.n += 1
        return pltpu.make_async_remote_copy(
            src_ref=src,
            dst_ref=dst,
            send_sem=self.send.at[i],
            recv_sem=self.recv.at[i],
            device_id=dev,
            device_id_type=MESH,
        )

    def start(self, copy, cond=None):
        self.sent.append((copy, cond))
        when(cond, copy.start)

    def drain(self):
        for copy, cond in self.sent:
            when(cond, copy.wait_send)


def when(cond, fn):
    if cond is None:
        fn()
    else:
        pl.when(cond)(fn)


def greet(partners):
    barrier = pltpu.get_barrier_semaphore()
    for dev in partners:
        pl.semaphore_signal(barrier, inc=1, device_id=dev, device_id_type=MESH)
    pl.semaphore_wait(barrier, len(partners))


def piece_start(i, c, z):
    return ((i // 8) * 8 + ((i // 2) % 4) * 2 + c) * 160 + ((i % 2) * 4 + z) * 20


N1 = 64


def gather_kernel(
    hid, w, kg,
    wout, kwin, vwin, kraw, hout,
    wbuf, kbuf, vbuf, hT, hs, hpk, hrecv, acc, send, recv, loc,
):
    p = Place()
    net = Net(send, recv)
    c, x, z = p.c, p.x, p.z
    sib = p.at(c=1 - c)
    xp, xm = p.at(x=p.xs(1)), p.at(x=p.xs(3))
    zp, zm = p.at(z=p.zs(1)), p.at(z=p.zs(3))
    far = p.at(yh=1 - p.yh, yl=1 - p.yl)
    near = p.at(yl=1 - p.yl)
    zgroup = [p.at(z=p.zs(d), c=cc) for d in range(4) for cc in (c, 1 - c)][1:]

    loads = [
        pltpu.make_async_copy(w.at[:, pl.ds(j * 128, 128)], wbuf.at[p.f, j], loc.at[j])
        for j in range(8)
    ]
    for l in loads:
        l.start()
    greet([xp, xm, far, near] + zgroup)
    for l in loads:
        l.wait()

    c4 = c * 4
    fo = (1 - p.yh) * 4
    others = [fo + z, fo + p.zs(3), fo + p.zs(1), fo + p.zs(2)]
    home = p.yh * 4
    f_m, f_p, f_2 = home + p.zs(3), home + p.zs(1), home + p.zs(2)

    y_cp = net.copy(wbuf.at[p.f, c4 + x], wbuf.at[p.f, c4 + x], far)
    net.start(y_cp)
    zp_own, zm_own = [None, None], [None, None]
    for q in (0, 1):
        r = pl.ds(c4 + 2 * q, 2)
        zp_own[q] = net.copy(wbuf.at[p.f, r], wbuf.at[p.f, r], zp)
        net.start(zp_own[q])
        r = pl.ds(c4 + 2 * (1 - q), 2)
        zm_own[1 - q] = net.copy(wbuf.at[p.f, r], wbuf.at[p.f, r], zm)
        net.start(zm_own[1 - q])

    for f in range(8):
        hs[f] = hid[:, f * ROWS:(f + 1) * ROWS]
    for b in range(D // 128):
        hT[pl.ds(b * 128, 128), :] = hid[:, b * 128:(b + 1) * 128].astype(F32).T

    xp_cp, xm_cp = [None] * 4, [None] * 4

    def to_x(i):
        ref = wbuf.at[others[i], c4 + x]
        xp_cp[i] = net.copy(ref, ref, xp)
        xm_cp[i] = net.copy(ref, ref, xm)
        net.start(xp_cp[i])
        net.start(xm_cp[i])

    y_cp.wait_recv()
    quarter = wbuf.at[others[0], c4 + x]
    zp_oth = net.copy(quarter, quarter, zp)
    zm_oth = net.copy(quarter, quarter, zm)
    net.start(zp_oth)
    net.start(zm_oth)
    to_x(0)
    zp_own[0].wait_recv()
    r = pl.ds(c4, 2)
    zp_fwd = net.copy(wbuf.at[f_m, r], wbuf.at[f_m, r], zp)
    net.start(zp_fwd)
    zm_own[1].wait_recv()
    r = pl.ds(c4 + 2, 2)
    zm_fwd = net.copy(wbuf.at[f_p, r], wbuf.at[f_p, r], zm)
    net.start(zm_fwd)

    for zc in range(4):
        for cc in range(2):
            for i in range(16):
                hpk[zc * 2 + cc, pl.ds(i * 20, 20), :] = hT[pl.ds(piece_start(i, cc, zc), 20), :].astype(BF)

    zp_oth.wait_recv()
    ref = wbuf.at[others[1], c4 + x]
    zp_ofwd = net.copy(ref, ref, zp)
    net.start(zp_ofwd)
    to_x(1)
    zm_oth.wait_recv()
    to_x(2)
    zp_own[1].wait_recv()
    zm_own[0].wait_recv()

    def to_sib(f):
        r = pl.ds(c4, 4)
        cp = net.copy(wbuf.at[f, r], wbuf.at[f, r], sib)
        net.start(cp)
        return cp

    sib_cps = [(f_m, to_sib(f_m)), (f_p, to_sib(f_p))]
    zp_ofwd.wait_recv()
    to_x(3)
    x_fwd = []
    for i in range(4):
        if i < 2:
            xp_cp[i].wait_recv()
            ref = wbuf.at[others[i], c4 + p.xs(3)]
            cp = net.copy(ref, ref, xp)
        else:
            xm_cp[i].wait_recv()
            ref = wbuf.at[others[i], c4 + p.xs(1)]
            cp = net.copy(ref, ref, xm)
        net.start(cp)
        x_fwd.append(cp)
    zp_fwd.wait_recv()
    zm_fwd.wait_recv()
    sib_cps.append((f_2, to_sib(f_2)))

    mine = z * 2 + c
    h_cps = []
    for d in range(4):
        for e in range(2):
            if d == 0 and e == 0:
                continue
            zc = p.zs(d)
            cc = lax.rem(c + e, 2)
            cp = net.copy(hpk.at[zc * 2 + cc], hrecv.at[mine], p.at(z=zc, c=cc))
            net.start(cp)
            h_cps.append(cp)
    own_h = pltpu.make_async_copy(hpk.at[mine], hrecv.at[mine], loc.at[0])
    own_h.start()

    def shard(f):
        return jnp.concatenate([wbuf[f, j] for j in range(8)], axis=1)

    def project(f):
        return jnp.dot(hs[f], shard(f), preferred_element_type=F32)

    acc[...] = project(p.f)
    for f, cp in sib_cps:
        cp.wait_recv()
        acc[...] += project(f)
    rest = []
    for i in range(4):
        if i < 2:
            xm_cp[i].wait_recv()
        else:
            xp_cp[i].wait_recv()
        x_fwd[i].wait_recv()
        rest.append((others[i], to_sib(others[i])))
    for f, cp in rest:
        cp.wait_recv()
        acc[...] += project(f)
    w_save = pltpu.make_async_copy(wbuf, wout, loc.at[1])
    w_save.start()

    for d in range(1, WIN):
        @pl.when(p.s < d)
        def _():
            kbuf[d] = jnp.zeros((KVH, TOK, HD), BF)
            vbuf[d] = jnp.zeros((KVH, TOK, HD), BF)
    for g in range(KVH):
        raw = acc[:, g * HD:(g + 1) * HD]
        kraw[g] = raw
        r = lax.rsqrt(jnp.mean(raw * raw, axis=1, keepdims=True) + EPS)
        kbuf[0, g] = (raw * r * kg[...]).astype(BF)
        vbuf[0, g] = acc[:, 512 + g * HD:512 + (g + 1) * HD].astype(BF)

    row1 = p.yl == 1
    bufs = (kbuf, vbuf)
    y_c, r_c, l_c, r2_c, l2_c = [], [], [], [], []
    sc = [[None] * 5, [None] * 5]

    def sib_copy(ch, m):
        b = bufs[ch]
        cp = net.copy(b.at[2 * m], b.at[jnp.clip(2 * m + 1 - 2 * c, 0, WIN - 1)], sib)
        cond = p.k >= m
        if m == 4:
            cond = cond & (c == 1)
        if m == 0:
            cond = c == 0
        net.start(cp, cond)
        sc[ch][m] = cp

    for ch in range(2):
        b = bufs[ch]
        cp = net.copy(b.at[0], b.at[8], near)
        net.start(cp, p.yl == 0)
        y_c.append(cp)
        cp = net.copy(b.at[jnp.where(x < 3, 0, 8)], b.at[2], xp)
        net.start(cp, x < 3)
        r_c.append(cp)
        cp = net.copy(b.at[jnp.where(x == 0, 0, 8)], b.at[6], xm)
        net.start(cp, x == 0)
        l_c.append(cp)
        sib_copy(ch, 0)
    for ch in range(2):
        when(row1, y_c[ch].wait_recv)
        net.start(r_c[ch], (x == 3) & row1)
        net.start(l_c[ch], (x > 0) & row1)
    mid = (x == 1) | (x == 2)
    for ch in range(2):
        b = bufs[ch]
        when(p.k >= 1, r_c[ch].wait_recv)
        cp = net.copy(b.at[2], b.at[4], xp)
        net.start(cp, mid)
        r2_c.append(cp)
        sib_copy(ch, 1)
    for ch in range(2):
        b = bufs[ch]
        when(p.k >= 3, l_c[ch].wait_recv)
        cp = net.copy(b.at[6], b.at[4], xm)
        net.start(cp, mid & row1)
        l2_c.append(cp)
        sib_copy(ch, 3)
        sib_copy(ch, 4)
    for ch in range(2):
        when(x >= 2, r2_c[ch].wait_recv)
        when((x < 2) & row1, l2_c[ch].wait_recv)
        sib_copy(ch, 2)
    for ch in range(2):
        for m in range(5):
            cond = p.k >= m
            if m == 0:
                cond = c == 1
            if m == 4:
                cond = cond & (c == 0)
            when(cond, sc[ch][m].wait_recv)
    k_save = pltpu.make_async_copy(kbuf, kwin, loc.at[2])
    v_save = pltpu.make_async_copy(vbuf, vwin, loc.at[3])
    k_save.start()
    v_save.start()
    for cp in h_cps:
        cp.wait_recv()
    own_h.wait()
    h_save = pltpu.make_async_copy(hrecv, hout, loc.at[4])
    h_save.start()
    w_save.wait()
    k_save.wait()
    v_save.wait()
    h_save.wait()
    net.drain()
    assert net.n <= N1


def attend_kernel(
    sref, docs, q, do, kk, vv, qg,
    att, dq, dk, dv, qgain,
    mask, w_s, ds_s, qn_s, do_s, gacc,
):
    g = pl.program_id(0)
    s = sref[0]
    rows = WIN * TOK

    @pl.when(g == 0)
    def _():
        gacc[...] = jnp.zeros_like(gacc)
        qd = docs[pl.ds(s, 1), :].astype(F32)
        tri = (
            lax.broadcasted_iota(jnp.int32, (TOK, TOK), 0)
            <= lax.broadcasted_iota(jnp.int32, (TOK, TOK), 1)
        )
        for d in range(WIN):
            kd = docs[pl.ds(jnp.maximum(s - d, 0), 1), :].astype(F32)
            kd = jnp.broadcast_to(kd, (TOK, TOK)).T
            live = (kd == qd) & (s >= d)
            if d == 0:
                live = live & tri
            mask[pl.ds(d * TOK, TOK), :] = jnp.where(live, 1.0, 0.0).astype(F32)

    kall = kk[...].reshape(rows, HD)
    vall = vv[...].reshape(rows, HD)
    kT = kall.astype(F32).T.astype(BF)
    vT = vall.astype(F32).T.astype(BF)
    gain = jnp.broadcast_to(qg[...], (HD, HD)).T
    gain = jnp.concatenate([gain, gain], axis=1)
    for pair in range(GROUP // 2):
        cols = pl.ds(pair * 256, 256)
        heads = [2 * pair, 2 * pair + 1]

        def turned(ref):
            return jnp.concatenate(
                [ref[:, h * HD:(h + 1) * HD].astype(F32).T for h in heads], axis=1
            )

        qT = turned(q)
        doT = turned(do)
        r = lax.rsqrt(jnp.mean(qT * qT, axis=0, keepdims=True) + EPS)
        xhat = qT * r
        qn = (xhat * gain).astype(BF)
        qn_s[:, cols] = qn
        scores = jnp.dot(kall, qn, preferred_element_type=F32)
        m = mask[...]
        e = jnp.exp2(scores * (SCALE * LOG2E)) * jnp.concatenate([m, m], axis=1)
        total = jnp.sum(e, axis=0, keepdims=True)
        w = e.astype(BF)
        w_s[:, cols] = w
        inv = 1.0 / total
        attT = (jnp.dot(vT, w, preferred_element_type=F32) * inv).astype(BF).astype(F32)
        delta = jnp.sum(doT * attT, axis=0, keepdims=True) * inv
        dos = (doT * inv).astype(BF)
        do_s[:, cols] = dos
        dp = jnp.dot(vall, dos, preferred_element_type=F32)
        ds = (e * (dp - delta)).astype(BF)
        ds_s[:, cols] = ds
        dy = jnp.dot(kT, ds, preferred_element_type=F32) * SCALE
        gacc[...] += dy * xhat
        dxh = dy * gain
        dx = r * (dxh - xhat * jnp.mean(xhat * dxh, axis=0, keepdims=True))
        for n, h in enumerate(heads):
            att[:, h * HD:(h + 1) * HD] = attT[:, n * HD:(n + 1) * HD].T.astype(BF)
            dq[:, h * HD:(h + 1) * HD] = dx[:, n * HD:(n + 1) * HD].T.astype(BF)
    dvv = lax.dot_general(w_s[...], do_s[...], NT, preferred_element_type=F32)
    dv[...] = dvv.astype(BF).reshape(WIN, 1, TOK, HD)
    dkk = lax.dot_general(ds_s[...], qn_s[...], NT, preferred_element_type=F32) * SCALE
    dk[...] = dkk.astype(BF).reshape(WIN, 1, TOK, HD)

    @pl.when(g == KVH - 1)
    def _():
        a = gacc[:, :HD] + gacc[:, HD:]
        qgain[...] = jnp.sum(a.T, axis=0, keepdims=True)


N3 = 96


def reduce_kernel(
    dk, dv, kraw, wfull, hbuf, kg, qgain,
    gh, gw, qgo, kgo,
    pk, pv, sbk, sbv, r2r, r2l, r1, r3, ry, t0,
    wbuf, hb, gk, gv, gf, st, rbs, rbr, stf, gs1, gr1, gs2, gr2, send, recv, loc,
):
    p = Place()
    net = Net(send, recv)
    c, x, z, k = p.c, p.x, p.z, p.k
    row1 = p.yl == 1
    sib = p.at(c=1 - c)
    xp, xm = p.at(x=p.xs(1)), p.at(x=p.xs(3))
    zp, zm = p.at(z=p.zs(1)), p.at(z=p.zs(3))
    near = p.at(yl=1 - p.yl)
    zgroup = [p.at(z=p.zs(d), c=cc) for d in range(4) for cc in (c, 1 - c)][1:]
    me16 = (p.yl * 4 + x) * 2 + p.yh
    peers = []
    for i in range(1, 16):
        o = lax.rem(me16 + i, 16)
        peers.append((o, p.at(x=lax.rem(lax.div(o, 2), 4), yl=lax.div(o, 8), yh=lax.rem(o, 2))))

    parts = (pk, pv)
    sbs = (sbk, sbv)
    loads = [
        pltpu.make_async_copy(dv, pv, loc.at[1]),
        pltpu.make_async_copy(dk, pk, loc.at[0]),
        pltpu.make_async_copy(wfull, wbuf, loc.at[2]),
        pltpu.make_async_copy(hbuf, hb, loc.at[3]),
    ]
    for l in loads:
        l.start()
    greet(zgroup + [d for _, d in peers])
    loads[0].wait()
    loads[1].wait()

    order = (1, 0)
    sc = [[None] * 5, [None] * 5]
    for ch in order:
        for m in (2, 1, 3, 4, 0):
            cp = net.copy(parts[ch].at[jnp.clip(2 * m + 2 * c - 1, 0, WIN - 1)], sbs[ch].at[m], sib)
            cond = k >= m
            if m == 0:
                cond = c == 1
            if m == 4:
                cond = cond & (c == 0)
            net.start(cp, cond)
            sc[ch][m] = cp

    def pair(ch, m):
        cond = k >= m
        if m == 0:
            cond = c == 0
        if m == 4:
            cond = cond & (c == 1)

        def add():
            sc[ch][m].wait_recv()
            if m == 0:
                t0[ch] = t0[ch] + sbs[ch][m].astype(F32)
            else:
                b = parts[ch]
                b[2 * m] = (b[2 * m].astype(F32) + sbs[ch][m].astype(F32)).astype(BF)

        when(cond, add)

    def add_to(ch, slot, ref):
        def add():
            if slot == 0:
                t0[ch] = t0[ch] + ref[ch].astype(F32)
            else:
                b = parts[ch]
                b[slot] = (b[slot].astype(F32) + ref[ch].astype(F32)).astype(BF)
        return add

    def arrive(cond, cp, fn):
        def go():
            cp.wait_recv()
            fn()
        when(cond, go)

    mid = (x == 1) | (x == 2)
    c2r, c2l, c1, c3, cy = [None] * 2, [None] * 2, [None] * 2, [None] * 2, [None] * 2
    for ch in order:
        pair(ch, 2)
        b = parts[ch]
        c2r[ch] = net.copy(b.at[4], r2r.at[ch], xm)
        net.start(c2r[ch], x >= 2)
        c2l[ch] = net.copy(b.at[4], r2l.at[ch], xp)
        net.start(c2l[ch], (x < 2) & row1)
    for ch in order:
        pair(ch, 1)
        pair(ch, 3)
        pair(ch, 4)
    for ch in order:
        b = parts[ch]
        arrive(mid, c2r[ch], add_to(ch, 2, r2r))
        c1[ch] = net.copy(b.at[2], r1.at[ch], xm)
        net.start(c1[ch], k >= 1)
        arrive(mid & row1, c2l[ch], add_to(ch, 6, r2l))
        c3[ch] = net.copy(b.at[6], r3.at[ch], xp)
        net.start(c3[ch], k >= 3)
    for ch in order:
        t0[ch] = parts[ch][0].astype(F32)
        pair(ch, 0)
    for ch in order:
        arrive(x < 3, c1[ch], add_to(ch, 0, r1))
        arrive((x == 3) & row1, c1[ch], add_to(ch, 8, r1))
        arrive(x == 0, c3[ch], add_to(ch, 0, r3))
        arrive((x > 0) & row1, c3[ch], add_to(ch, 8, r3))
        cy[ch] = net.copy(parts[ch].at[8], ry.at[ch], near)
        net.start(cy[ch], row1)

    mine = z * 2 + c
    bufs = (gk, gv)
    zpc, zmc, sibc, fwd = [None] * 2, [None] * 2, [None] * 2, [None] * 2
    for ch in order:
        arrive(p.yl == 0, cy[ch], add_to(ch, 0, ry))
        if ch == 0:
            kga = jnp.zeros((1, HD), F32)
            for g in range(KVH):
                raw = kraw[g]
                r = lax.rsqrt(jnp.mean(raw * raw, axis=1, keepdims=True) + EPS)
                xh = raw * r
                dy = t0[0, g]
                kga = kga + jnp.sum(dy * xh, axis=0, keepdims=True)
                dxh = dy * kg[...]
                dx = r * (dxh - xh * jnp.mean(xh * dxh, axis=1, keepdims=True))
                gk[mine, g] = dx.astype(BF)
            gs1[...] = jnp.concatenate(
                [qgain[...], kga, jnp.zeros((6, HD), F32)], axis=0
            )
        else:
            gv[mine] = t0[1].astype(BF)
        b = bufs[ch]
        zpc[ch] = net.copy(b.at[mine], b.at[mine], zp)
        zmc[ch] = net.copy(b.at[mine], b.at[mine], zm)
        sibc[ch] = net.copy(b.at[mine], b.at[mine], sib)
        net.start(zpc[ch])
        net.start(zmc[ch])
        net.start(sibc[ch])
    g1 = []
    for d in range(4):
        for e in range(2):
            if d == 0 and e == 0:
                continue
            cp = net.copy(gs1, gr1.at[mine], p.at(z=p.zs(d), c=lax.rem(c + e, 2)))
            net.start(cp)
            g1.append(cp)

    def slot(d):
        return p.zs(d) * 2 + c

    def forward(ch, d, dev):
        cp = net.copy(bufs[ch].at[slot(d)], bufs[ch].at[slot(d)], dev)
        net.start(cp)
        return cp

    zmc[1].wait_recv()
    fwd[1] = forward(1, 1, zm)
    s_p1 = forward(1, 1, sib)
    zpc[1].wait_recv()
    s_m1 = forward(1, 3, sib)
    zpc[0].wait_recv()
    fwd[0] = forward(0, 3, zp)
    s_m0 = forward(0, 3, sib)
    zmc[0].wait_recv()
    s_p0 = forward(0, 1, sib)

    loads[2].wait()
    gkv = jnp.concatenate(
        [gk[mine, g] for g in range(KVH)] + [gv[mine, g] for g in range(KVH)], axis=1
    )
    for f in range(8):
        wv = jnp.concatenate([wbuf[f, j] for j in range(8)], axis=1)
        gh[:, f * ROWS:(f + 1) * ROWS] = lax.dot_general(
            gkv, wv, NT, preferred_element_type=F32
        ).astype(BF)

    fwd[1].wait_recv()
    s_f1 = forward(1, 2, sib)
    fwd[0].wait_recv()
    s_f0 = forward(0, 2, sib)
    for cp in g1:
        cp.wait_recv()
    gr1[mine] = gs1[...]
    gs2[...] = jnp.sum(gr1[...], axis=0)
    g2 = []
    for i, (o, dev) in enumerate(peers):
        cp = net.copy(gs2, gr2.at[me16], dev)
        net.start(cp)
        g2.append(cp)
    gr2[me16] = gs2[...]
    loads[3].wait()
    for cp in (sibc[1], s_p1, s_m1, s_f1, sibc[0], s_p0, s_m0, s_f0):
        cp.wait_recv()

    lhs = jnp.concatenate([hb[i] for i in range(8)], axis=1)
    for ch in order:
        for j in range(KVH):
            rhs = bufs[ch][:, j].reshape(8 * TOK, HD)
            gf[:, (ch * 4 + j) * HD:(ch * 4 + j + 1) * HD] = jnp.dot(lhs, rhs, preferred_element_type=F32)
    for i in range(16):
        for j in range(8):
            st[i, pl.ds(j * 20, 20), :] = gf[pl.ds(i * 20, 20), j * HD:(j + 1) * HD]
    for i in range(16):
        rbs[i] = st[i].astype(BF)
    w_c = []
    for i, (o, dev) in enumerate(peers):
        cp = net.copy(rbs.at[o], rbr.at[me16], dev)
        net.start(cp)
        w_c.append(cp)
    rbr[me16] = rbs[me16]
    for cp in w_c:
        cp.wait_recv()
    total = rbr[0].astype(F32)
    for i in range(1, 16):
        total = total + rbr[i].astype(F32)
    stf[...] = total
    for j in range(8):
        gw[:, j * HD:(j + 1) * HD] = stf[pl.ds(j * 20, 20), :].astype(BF)
    for cp in g2:
        cp.wait_recv()
    gsum = jnp.sum(gr2[...], axis=0)
    qgo[...] = gsum[0:1]
    kgo[...] = gsum[1:2]
    net.drain()
    assert net.n <= N3


def shards(hidden, queries, doc_ids, kv_weight, q_gain, k_gain, grad_out):
    hid = hidden[0]
    vm = pl.BlockSpec(memory_space=pltpu.VMEM)
    hbm = pl.BlockSpec(memory_space=pl.ANY)
    kg = k_gain.reshape(1, HD)
    qg = q_gain.reshape(1, HD)
    sds = jax.ShapeDtypeStruct
    win = (WIN, KVH, TOK, HD)
    wfull, kwin, vwin, kraw, hbuf = pl.pallas_call(
        gather_kernel,
        out_shape=(
            sds((8, 8, ROWS, 128), BF),
            sds(win, BF),
            sds(win, BF),
            sds((KVH, TOK, HD), F32),
            sds((8, ROWS, TOK), BF),
        ),
        in_specs=[vm, hbm, vm],
        out_specs=(hbm, hbm, hbm, vm, hbm),
        scratch_shapes=[
            pltpu.VMEM((8, 8, ROWS, 128), BF),
            pltpu.VMEM(win, BF),
            pltpu.VMEM(win, BF),
            pltpu.VMEM((D, TOK), F32),
            pltpu.VMEM((8, TOK, ROWS), BF),
            pltpu.VMEM((8, ROWS, TOK), BF),
            pltpu.VMEM((8, ROWS, TOK), BF),
            pltpu.VMEM((TOK, 1024), F32),
            pltpu.SemaphoreType.DMA((N1,)),
            pltpu.SemaphoreType.DMA((N1,)),
            pltpu.SemaphoreType.DMA((8,)),
        ],
        compiler_params=pltpu.CompilerParams(
            collective_id=0, has_side_effects=True, vmem_limit_bytes=56 * 1024 * 1024
        ),
        name="gather",
    )(hid, kv_weight, kg)

    s = lax.axis_index("seq").astype(jnp.int32).reshape(1)
    docs = doc_ids[0].reshape(16, TOK)
    rows = WIN * TOK
    head = pl.BlockSpec((TOK, GROUP * HD), lambda g: (0, g))
    wspec = pl.BlockSpec((WIN, 1, TOK, HD), lambda g: (0, g, 0, 0))
    fixed = pl.BlockSpec((1, HD), lambda g: (0, 0))
    att, dq, dk, dv, qgain = pl.pallas_call(
        attend_kernel,
        grid=(KVH,),
        out_shape=(
            sds((TOK, 32 * HD), BF),
            sds((TOK, 32 * HD), BF),
            sds(win, BF),
            sds(win, BF),
            sds((1, HD), F32),
        ),
        in_specs=[
            pl.BlockSpec(memory_space=pltpu.SMEM),
            pl.BlockSpec((16, TOK), lambda g: (0, 0)),
            head,
            head,
            wspec,
            wspec,
            fixed,
        ],
        out_specs=(head, head, wspec, wspec, fixed),
        scratch_shapes=[
            pltpu.VMEM((rows, TOK), F32),
            pltpu.VMEM((rows, GROUP * TOK), BF),
            pltpu.VMEM((rows, GROUP * TOK), BF),
            pltpu.VMEM((HD, GROUP * TOK), BF),
            pltpu.VMEM((HD, GROUP * TOK), BF),
            pltpu.VMEM((HD, 256), F32),
        ],
        compiler_params=pltpu.CompilerParams(vmem_limit_bytes=56 * 1024 * 1024),
        name="attend",
    )(s, docs, queries[0], grad_out[0], kwin, vwin, qg)

    unit = (KVH, TOK, HD)
    gh, gw, qgo, kgo = pl.pallas_call(
        reduce_kernel,
        out_shape=(
            sds((TOK, D), BF),
            sds((20, 1024), BF),
            sds((1, HD), F32),
            sds((1, HD), F32),
        ),
        in_specs=[hbm, hbm, vm, hbm, hbm, vm, vm],
        out_specs=(vm, vm, vm, vm),
        scratch_shapes=[
            pltpu.VMEM(win, BF),
            pltpu.VMEM(win, BF),
            pltpu.VMEM((5,) + unit, BF),
            pltpu.VMEM((5,) + unit, BF),
            pltpu.VMEM((2,) + unit, BF),
            pltpu.VMEM((2,) + unit, BF),
            pltpu.VMEM((2,) + unit, BF),
            pltpu.VMEM((2,) + unit, BF),
            pltpu.VMEM((2,) + unit, BF),
            pltpu.VMEM((2,) + unit, F32),
            pltpu.VMEM((8, 8, ROWS, 128), BF),
            pltpu.VMEM((8, ROWS, TOK), BF),
            pltpu.VMEM((8,) + unit, BF),
            pltpu.VMEM((8,) + unit, BF),
            pltpu.VMEM((ROWS, 1024), F32),
            pltpu.VMEM((16, 160, HD), F32),
            pltpu.VMEM((16, 160, HD), BF),
            pltpu.VMEM((16, 160, HD), BF),
            pltpu.VMEM((160, HD), F32),
            pltpu.VMEM((8, HD), F32),
            pltpu.VMEM((8, 8, HD), F32),
            pltpu.VMEM((8, HD), F32),
            pltpu.VMEM((16, 8, HD), F32),
            pltpu.SemaphoreType.DMA((N3,)),
            pltpu.SemaphoreType.DMA((N3,)),
            pltpu.SemaphoreType.DMA((4,)),
        ],
        compiler_params=pltpu.CompilerParams(
            collective_id=1, has_side_effects=True, vmem_limit_bytes=56 * 1024 * 1024
        ),
        name="reduce",
    )(dk, dv, kraw, wfull, hbuf, kg, qgain)
    return (att[None], dq[None], gh[None], gw, qgo.reshape(HD), kgo.reshape(HD))


def solution(mesh):
    return jax.shard_map(
        shards,
        mesh=mesh,
        in_specs=(
            P("fsdp", "seq", None),
            P("fsdp", "seq", None),
            P("fsdp", None),
            P("fsdp", None),
            P(),
            P(),
            P("fsdp", "seq", None),
        ),
        out_specs=(
            P("fsdp", "seq", None),
            P("fsdp", "seq", None),
            P("fsdp", "seq", None),
            P(("seq", "fsdp"), None),
            P(),
            P(),
        ),
        check_vma=False,
    )
```

```python
import math

import jax
import jax.numpy as jnp
from jax import lax
from jax.experimental import pallas as pl
from jax.experimental.pallas import tpu as pltpu
from jax.sharding import PartitionSpec as P

MESH = pl.DeviceIdType.MESH
BF = jnp.bfloat16
F32 = jnp.float32
EPS = 1e-06
TOK = 128
HD = 128
KVH = 4
GROUP = 8
D = 2560
ROWS = 320
WIN = 9
SCALE = 1.0 / math.sqrt(HD)
LOG2E = 1.4426950408889634
NT = (((1,), (1,)), ((), ()))


class Place:
    def __init__(self):
        s = lax.axis_index("seq")
        f = lax.axis_index("fsdp")
        self.s, self.f = s, f
        self.c = lax.rem(s, 2)
        self.x = lax.rem(lax.div(s, 2), 4)
        self.yl = lax.div(s, 8)
        self.yh = lax.div(f, 4)
        self.z = lax.rem(f, 4)
        self.k = lax.div(s, 2)

    def at(self, x=None, yl=None, yh=None, z=None, c=None):
        x = self.x if x is None else x
        yl = self.yl if yl is None else yl
        yh = self.yh if yh is None else yh
        z = self.z if z is None else z
        c = self.c if c is None else c
        return ((yl * 4 + x) * 2 + c, yh * 4 + z)

    def xs(self, d):
        return lax.rem(self.x + d, 4)

    def zs(self, d):
        return lax.rem(self.z + d, 4)


class Net:
    def __init__(self, send, recv):
        self.send, self.recv, self.n = send, recv, 0
        self.sent = []

    def copy(self, src, dst, dev):
        i = self.n
        self.n += 1
        return pltpu.make_async_remote_copy(
            src_ref=src,
            dst_ref=dst,
            send_sem=self.send.at[i],
            recv_sem=self.recv.at[i],
            device_id=dev,
            device_id_type=MESH,
        )

    def start(self, copy, cond=None):
        self.sent.append((copy, cond))
        when(cond, copy.start)

    def drain(self):
        for copy, cond in self.sent:
            when(cond, copy.wait_send)


def when(cond, fn):
    if cond is None:
        fn()
    else:
        pl.when(cond)(fn)


def greet(partners):
    barrier = pltpu.get_barrier_semaphore()
    for dev in partners:
        pl.semaphore_signal(barrier, inc=1, device_id=dev, device_id_type=MESH)
    pl.semaphore_wait(barrier, len(partners))


def piece_start(i, c, z):
    return ((i // 8) * 8 + ((i // 2) % 4) * 2 + c) * 160 + ((i % 2) * 4 + z) * 20


NSEM = 160
WROWS = WIN * TOK
UNIT = 2 * TOK


def mega_kernel(
    w, hid, q, do, docs, qg, kg,
    att, dq, gh, gw, qgo, kgo,
    wbuf, hidv, hs, hT, hpk, hb, acc, kv, kraw, qv, dov, xh, rq, doT, qn, dos, w_s, ds_s, mask,
    attv, dqv, part, sb, xr, yr, t0, gb, gf, st, rbs, rbr, stf, gacc, kacc, gs1, gr1, gs2, gr2,
    send, recv, loc,
):
    p = Place()
    net = Net(send, recv)
    c, x, z, k = p.c, p.x, p.z, p.k
    row1 = p.yl == 1
    sib = p.at(c=1 - c)
    near = p.at(yl=1 - p.yl)
    far = p.at(yh=1 - p.yh, yl=1 - p.yl)
    xd = [None] + [p.at(x=p.xs(d)) for d in (1, 2, 3)]
    zd = [None] + [p.at(z=p.zs(d)) for d in (1, 2, 3)]
    fard = [None] + [p.at(yh=1 - p.yh, yl=1 - p.yl, z=p.zs(d)) for d in (1, 2, 3)]
    zgroup = [(p.zs(d), lax.rem(c + e, 2)) for d in range(4) for e in range(2)][1:]
    me16 = (p.yl * 4 + x) * 2 + p.yh
    peers = []
    for i in range(1, 16):
        o = lax.rem(me16 + i, 16)
        peers.append((o, p.at(x=lax.rem(lax.div(o, 2), 4), yl=lax.div(o, 8), yh=lax.rem(o, 2))))
    c4 = c * 4
    home, away = p.yh * 4, (1 - p.yh) * 4

    own = pl.ds(c4, 4)
    loads = []
    for n in range(8):
        j = lax.rem(c4 + n, 8)
        cols = pl.ds(pl.multiple_of(j * 128, 128), 128)
        loads.append(pltpu.make_async_copy(w.at[:, cols], wbuf.at[p.f, j], loc.at[n]))
    loads.append(pltpu.make_async_copy(hid, hidv, loc.at[8]))
    loads.append(pltpu.make_async_copy(q, qv, loc.at[9]))
    loads.append(pltpu.make_async_copy(do, dov, loc.at[10]))
    for l in loads:
        l.start()
    for m in range(1, 5):
        @pl.when(k < m)
        def _():
            kv[c, :, pl.ds((4 - m) * UNIT, UNIT), :] = jnp.zeros((KVH, UNIT, HD), BF)
    greet([p.at(z=zz, c=cc) for zz, cc in zgroup] + [d for _, d in peers] + fard[1:])
    for l in loads[:4]:
        l.wait()

    def wcopy(f, cols, dev):
        ref = wbuf.at[f, cols]
        cp = net.copy(ref, ref, dev)
        net.start(cp)
        return cp

    quarter = [None] + [wcopy(p.f, c4 + x, fard[d]) for d in (1, 2, 3)]
    first, second = pl.ds(c4, 2), pl.ds(c4 + 2, 2)
    zp0 = wcopy(p.f, first, zd[1])
    zm1 = wcopy(p.f, second, zd[3])
    far_c = wcopy(p.f, own, far)
    zp1 = wcopy(p.f, second, zd[1])
    zm0 = wcopy(p.f, first, zd[3])
    loads[8].wait()
    for f in range(8):
        hs[c, f] = hidv[:, f * ROWS:(f + 1) * ROWS]
    hs_c = net.copy(hs.at[c], hs.at[c], sib)
    net.start(hs_c)

    gain = jnp.broadcast_to(qg[...], (HD, HD)).T

    def prep(g):
        for h in range(g * GROUP, (g + 1) * GROUP):
            cols = slice(h * HD, (h + 1) * HD)
            t = qv[:, cols].astype(F32).T
            r = lax.rsqrt(jnp.mean(t * t, axis=0, keepdims=True) + EPS)
            xhat = t * r
            xh[:, cols] = xhat
            rq[:, cols] = jnp.broadcast_to(r, (8, HD))
            qn[g, :, (h % GROUP) * HD:(h % GROUP + 1) * HD] = (xhat * gain).astype(BF)
            doT[:, cols] = dov[:, cols].astype(F32).T

    loads[9].wait()
    loads[10].wait()
    prep(0)
    zp0.wait_recv()
    zpf = wcopy(home + p.zs(3), first, zd[1])
    zm1.wait_recv()
    zmf = wcopy(home + p.zs(1), second, zd[3])
    xs_c = []
    for d in (1, 3, 2):
        quarter[d].wait_recv()
        f = away + p.zs(4 - d)
        for e in (1, 3, 2):
            xs_c.append(wcopy(f, c4 + x, xd[e]))
    prep(1)

    s = p.s
    gacc[...] = jnp.zeros_like(gacc)
    kacc[...] = jnp.zeros_like(kacc)
    qd = docs[pl.ds(s, 1), :].astype(F32)
    tri = (
        lax.broadcasted_iota(jnp.int32, (TOK, TOK), 0)
        <= lax.broadcasted_iota(jnp.int32, (TOK, TOK), 1)
    )
    for d in range(WIN):
        kd = docs[pl.ds(jnp.maximum(s - d, 0), 1), :].astype(F32)
        kd = jnp.broadcast_to(kd, (TOK, TOK)).T
        live = jnp.where((kd == qd) & (s >= d), 1.0, 0.0)
        if d == 0:
            live = jnp.where(tri, live, 0.0)
        mask[pl.ds((WIN - 1 - d) * TOK, TOK), :] = live
    prep(2)
    prep(3)
    for g in range(KVH):
        for t in range(2):
            part[t, g, pl.ds(pl.multiple_of((1 - c) * WROWS, TOK), TOK), :] = jnp.zeros((TOK, HD), BF)
    for b in range(D // 128):
        hT[pl.ds(b * 128, 128), :] = hidv[:, b * 128:(b + 1) * 128].astype(F32).T
    for zc in range(4):
        for cc in range(2):
            for i in range(16):
                hpk[zc * 2 + cc, pl.ds(i * 20, 20), :] = hT[pl.ds(piece_start(i, cc, zc), 20), :].astype(BF)
    mine = z * 2 + c
    h_cps = []
    for zc, cc in zgroup:
        cp = net.copy(hpk.at[zc * 2 + cc], hb.at[mine], p.at(z=zc, c=cc))
        net.start(cp)
        h_cps.append(cp)
    own_h = pltpu.make_async_copy(hpk.at[mine], hb.at[mine], loc.at[11])
    own_h.start()

    def project(f):
        wv = jnp.concatenate([wbuf[f, c4 + n] for n in range(4)], axis=1)
        lhs = jnp.concatenate([hs[0, f], hs[1, f]], axis=0)
        return jnp.dot(lhs, wv, preferred_element_type=F32)

    hs_c.wait_recv()
    acc[...] = project(p.f)
    zp1.wait_recv()
    acc[...] += project(home + p.zs(3))
    zm0.wait_recv()
    acc[...] += project(home + p.zs(1))
    far_c.wait_recv()
    acc[...] += project(away + z)
    zpf.wait_recv()
    zmf.wait_recv()
    acc[...] += project(home + p.zs(2))
    for n, d in enumerate((1, 3, 2)):
        for e in range(3):
            xs_c[n * 3 + e].wait_recv()
        acc[...] += project(away + p.zs(4 - d))

    home_rows = pl.ds(4 * UNIT, UNIT)

    @pl.when(c == 0)
    def _():
        for g in range(KVH):
            raw = acc[:, g * HD:(g + 1) * HD]
            kraw[g] = raw
            r = lax.rsqrt(jnp.mean(raw * raw, axis=1, keepdims=True) + EPS)
            kv[0, g, home_rows, :] = (raw * r * kg[...]).astype(BF)

    @pl.when(c == 1)
    def _():
        for g in range(KVH):
            kv[1, g, home_rows, :] = acc[:, g * HD:(g + 1) * HD].astype(BF)

    def unit(m):
        return pl.ds((4 - m) * UNIT, UNIT)

    y_c, x_c, b_c = [], [], []
    for g in range(KVH):
        cp = net.copy(kv.at[c, g, unit(0)], kv.at[c, g, unit(4)], near)
        net.start(cp, p.yl == 0)
        y_c.append(cp)
        row = [None]
        for m in (1, 2, 3):
            src = kv.at[c, g, pl.ds(pl.multiple_of(jnp.where(x + m <= 3, 4 * UNIT, 0), UNIT), UNIT)]
            cp = net.copy(src, kv.at[c, g, unit(m)], xd[m])
            net.start(cp, x + m <= 3)
            row.append(cp)
        x_c.append(row)

    def spread(g):
        when(row1, y_c[g].wait_recv)
        for m in (1, 2, 3):
            net.start(x_c[g][m], row1 & (x + m > 3))

    def share(g):
        for m in (1, 2, 3):
            when(k >= m, x_c[g][m].wait_recv)
        cp = net.copy(kv.at[c, g], kv.at[c, g], sib)
        net.start(cp)
        b_c.append(cp)

    span = pl.ds(pl.multiple_of(c * TOK, TOK), WROWS)

    def open_head(g):
        b_c[g].wait_recv()
        ka = kv[0, g, span, :]
        va = kv[1, g, span, :]
        return ka, va, ka.astype(F32).T.astype(BF), va.astype(F32).T.astype(BF)

    gain2 = jnp.concatenate([gain, gain], axis=1)

    def attend(g, pair, head):
        ka, va, kT, vT = head
        lo = pair * 256
        cols = slice(lo, lo + 256)
        full = slice(g * 1024 + lo, g * 1024 + lo + 256)
        scores = jnp.dot(ka, qn[g, :, cols], preferred_element_type=F32)
        m = mask[...]
        e = jnp.exp2(scores * (SCALE * LOG2E)) * jnp.concatenate([m, m], axis=1)
        total = jnp.sum(e, axis=0, keepdims=True)
        wt = e.astype(BF)
        w_s[:, cols] = wt
        inv = 1.0 / total
        d_out = doT[:, full]
        attT = (jnp.dot(vT, wt, preferred_element_type=F32) * inv).astype(BF).astype(F32)
        delta = jnp.sum(d_out * attT, axis=0, keepdims=True) * inv
        dsc = (d_out * inv).astype(BF)
        dos[:, cols] = dsc
        dp = jnp.dot(va, dsc, preferred_element_type=F32)
        ds = (e * (dp - delta)).astype(BF)
        ds_s[:, cols] = ds
        dy = jnp.dot(kT, ds, preferred_element_type=F32) * SCALE
        xhat = xh[:, full]
        r = rq[0:1, full]
        gacc[...] += dy * xhat
        dxh = dy * gain2
        dx = r * (dxh - xhat * jnp.mean(xhat * dxh, axis=0, keepdims=True))
        for n in range(2):
            at = slice(g * 1024 + lo + n * HD, g * 1024 + lo + (n + 1) * HD)
            attv[:, at] = attT[:, n * HD:(n + 1) * HD].T.astype(BF)
            dqv[:, at] = dx[:, n * HD:(n + 1) * HD].T.astype(BF)

    outs = []

    def close_head(g):
        dvv = lax.dot_general(w_s[...], dos[...], NT, preferred_element_type=F32)
        part[1, g, span, :] = dvv.astype(BF)
        dkk = lax.dot_general(ds_s[...], qn[g], NT, preferred_element_type=F32) * SCALE
        part[0, g, span, :] = dkk.astype(BF)
        cols = pl.ds(g * 1024, 1024)
        for n, (a, b) in enumerate(((attv, att), (dqv, dq))):
            cp = pltpu.make_async_copy(a.at[:, cols], b.at[:, cols], loc.at[12 + g * 2 + n])
            cp.start()
            outs.append(cp)

    s_c, u_c, v_c, z_c, w_c = {}, {}, {}, {}, {}

    def c1(g):
        s_c[g] = net.copy(part.at[1 - c, g], sb.at[g], sib)
        net.start(s_c[g])

    def c2(g):
        s_c[g].wait_recv()
        part[c, g] = (part[c, g].astype(F32) + sb[g].astype(F32)).astype(BF)
        u_c[g] = [None]
        for m in (1, 2, 3):
            cp = net.copy(part.at[c, g, unit(m)], xr.at[g, m - 1], xd[4 - m])
            net.start(cp, k >= m)
            u_c[g].append(cp)

    def c3(g):
        t0[...] = part[c, g, unit(0), :].astype(F32)
        for m in (1, 2, 3):
            @pl.when(x + m <= 3)
            def _():
                u_c[g][m].wait_recv()
                t0[...] += xr[g, m - 1].astype(F32)

            @pl.when((x + m > 3) & row1)
            def _():
                u_c[g][m].wait_recv()
                part[c, g, unit(4), :] = (
                    part[c, g, unit(4), :].astype(F32) + xr[g, m - 1].astype(F32)
                ).astype(BF)

        v_c[g] = net.copy(part.at[c, g, unit(4)], yr.at[g], near)
        net.start(v_c[g], row1)
        part[c, g, unit(0), :] = t0[...].astype(BF)

    def c4(g):
        t0[...] = part[c, g, unit(0), :].astype(F32)

        @pl.when(p.yl == 0)
        def _():
            v_c[g].wait_recv()
            t0[...] += yr[g].astype(F32)

        @pl.when(c == 0)
        def _():
            raw = kraw[g]
            r = lax.rsqrt(jnp.mean(raw * raw, axis=1, keepdims=True) + EPS)
            xhat = raw * r
            dy = t0[...]
            kacc[...] += jnp.sum(dy * xhat, axis=0, keepdims=True)
            dxh = dy * kg[...]
            dx = r * (dxh - xhat * jnp.mean(xhat * dxh, axis=1, keepdims=True))
            gb[0, g, z] = dx.astype(BF)

        @pl.when(c == 1)
        def _():
            gb[1, g, z] = t0[...].astype(BF)

        z_c[g] = []
        for d in (1, 3, 2):
            cp = net.copy(gb.at[c, g, z], gb.at[c, g, z], zd[d])
            net.start(cp)
            z_c[g].append(cp)

    def d1(g):
        for cp in z_c[g]:
            cp.wait_recv()
        w_c[g] = net.copy(gb.at[c, g], gb.at[c, g], sib)
        net.start(w_c[g])

    def weight_terms(g):
        w_c[g].wait_recv()
        lhs = jnp.concatenate([hb[i] for i in range(8)], axis=1)
        rhs = jnp.concatenate([gb[0, g].reshape(8 * TOK, HD), gb[1, g].reshape(8 * TOK, HD)], axis=1)
        gf[...] = jnp.dot(lhs, rhs, preferred_element_type=F32)
        for i in range(16):
            for t in range(2):
                st[i, pl.ds(((g % 2) * 2 + t) * 20, 20), :] = gf[pl.ds(i * 20, 20), t * HD:(t + 1) * HD]

    r_c = []

    def scatter(n):
        for i in range(16):
            rbs[n, i] = st[i].astype(BF)
        row = []
        for o, dev in peers:
            cp = net.copy(rbs.at[n, o], rbr.at[n, me16], dev)
            net.start(cp)
            row.append(cp)
        r_c.append(row)
        rbr[n, me16] = rbs[n, me16]

    def collect(n):
        for cp in r_c[n]:
            cp.wait_recv()
        total = rbr[n, 0].astype(F32)
        for i in range(1, 16):
            total = total + rbr[n, i].astype(F32)
        stf[...] = total
        for b in range(2):
            for t in range(2):
                at = (t * 4 + n * 2 + b) * HD
                gw[:, at:at + HD] = stf[pl.ds((b * 2 + t) * 20, 20), :].astype(BF)

    spread(0)
    spread(1)
    share(0)

    w_sib = []

    def weight_share():
        for f in (home + p.zs(1), home + p.zs(2), home + p.zs(3), away, away + 1, away + 2, away + 3):
            w_sib.append(wcopy(f, own, sib))

    todo = {
        0: [lambda: spread(2), lambda: share(1)],
        1: [lambda: spread(3), weight_share],
        2: [lambda: share(2)],
        3: [lambda: c1(0), lambda: share(3)],
        5: [lambda: c2(0)],
        7: [lambda: c1(1)],
        8: [lambda: c3(0)],
        9: [lambda: c2(1)],
        10: [lambda: c4(0)],
        11: [lambda: c1(2)],
        12: [lambda: c3(1), lambda: d1(0)],
        13: [lambda: c2(2)],
        14: [lambda: c4(1)],
        15: [lambda: c1(3)],
    }
    for g in range(KVH):
        head = open_head(g)
        for pair in range(4):
            attend(g, pair, head)
            if pair == 3:
                close_head(g)
            for fn in todo.get(g * 4 + pair, ()):
                fn()

    c3(2)
    d1(1)
    c2(3)
    for cp in h_cps:
        cp.wait_recv()
    own_h.wait()
    c4(2)
    weight_terms(0)
    c3(3)
    weight_terms(1)
    scatter(0)
    d1(2)
    c4(3)
    a = gacc[:, :HD] + gacc[:, HD:]
    gs1[...] = jnp.concatenate(
        [jnp.sum(a.T, axis=0, keepdims=True), kacc[...], jnp.zeros((6, HD), F32)], axis=0
    )
    g1 = []
    for zc, cc in zgroup:
        cp = net.copy(gs1, gr1.at[mine], p.at(z=zc, c=cc))
        net.start(cp)
        g1.append(cp)
    gr1[mine] = gs1[...]
    weight_terms(2)
    d1(3)
    for cp in g1:
        cp.wait_recv()
    gs2[...] = jnp.sum(gr1[...], axis=0)
    g2 = []
    for o, dev in peers:
        cp = net.copy(gs2, gr2.at[me16], dev)
        net.start(cp)
        g2.append(cp)
    gr2[me16] = gs2[...]
    weight_terms(3)
    scatter(1)

    for l in loads[4:8]:
        l.wait()
    for cp in w_sib:
        cp.wait_recv()
    tokens = pl.ds(pl.multiple_of(c * TOK, TOK), TOK)
    gkv = jnp.concatenate([gb[t, g, z, tokens, :] for t in range(2) for g in range(KVH)], axis=1)
    for f in range(8):
        wv = jnp.concatenate([wbuf[f, j] for j in range(8)], axis=1)
        gh[:, f * ROWS:(f + 1) * ROWS] = lax.dot_general(
            gkv, wv, NT, preferred_element_type=F32
        ).astype(BF)
    collect(0)
    for cp in g2:
        cp.wait_recv()
    gsum = jnp.sum(gr2[...], axis=0)
    qgo[...] = gsum[0:1]
    kgo[...] = gsum[1:2]
    for cp in outs:
        cp.wait()
    collect(1)
    net.drain()
    assert net.n <= NSEM


def shards(hidden, queries, doc_ids, kv_weight, q_gain, k_gain, grad_out):
    vm = pl.BlockSpec(memory_space=pltpu.VMEM)
    hbm = pl.BlockSpec(memory_space=pl.ANY)
    sds = jax.ShapeDtypeStruct
    vmem = pltpu.VMEM
    wide = QW = 32 * HD
    att, dq, gh, gw, qgo, kgo = pl.pallas_call(
        mega_kernel,
        out_shape=(
            sds((TOK, QW), BF),
            sds((TOK, QW), BF),
            sds((TOK, D), BF),
            sds((20, 1024), BF),
            sds((1, HD), F32),
            sds((1, HD), F32),
        ),
        in_specs=[hbm, hbm, hbm, hbm, vm, vm, vm],
        out_specs=(hbm, hbm, vm, vm, vm, vm),
        scratch_shapes=[
            vmem((8, 8, ROWS, 128), BF),
            vmem((TOK, D), BF),
            vmem((2, 8, TOK, ROWS), BF),
            vmem((D, TOK), F32),
            vmem((8, ROWS, TOK), BF),
            vmem((8, ROWS, TOK), BF),
            vmem((UNIT, 512), F32),
            vmem((2, KVH, 5 * UNIT, HD), BF),
            vmem((KVH, UNIT, HD), F32),
            vmem((TOK, wide), BF),
            vmem((TOK, wide), BF),
            vmem((HD, wide), F32),
            vmem((8, wide), F32),
            vmem((HD, wide), F32),
            vmem((KVH, HD, GROUP * TOK), BF),
            vmem((HD, GROUP * TOK), BF),
            vmem((WROWS, GROUP * TOK), BF),
            vmem((WROWS, GROUP * TOK), BF),
            vmem((WROWS, TOK), F32),
            vmem((TOK, wide), BF),
            vmem((TOK, wide), BF),
            vmem((2, KVH, 5 * UNIT, HD), BF),
            vmem((KVH, 5 * UNIT, HD), BF),
            vmem((KVH, 3, UNIT, HD), BF),
            vmem((KVH, UNIT, HD), BF),
            vmem((UNIT, HD), F32),
            vmem((2, KVH, 4, UNIT, HD), BF),
            vmem((ROWS, 2 * HD), F32),
            vmem((16, 80, HD), F32),
            vmem((2, 16, 80, HD), BF),
            vmem((2, 16, 80, HD), BF),
            vmem((80, HD), F32),
            vmem((HD, 256), F32),
            vmem((1, HD), F32),
            vmem((8, HD), F32),
            vmem((8, 8, HD), F32),
            vmem((8, HD), F32),
            vmem((16, 8, HD), F32),
            pltpu.SemaphoreType.DMA((NSEM,)),
            pltpu.SemaphoreType.DMA((NSEM,)),
            pltpu.SemaphoreType.DMA((20,)),
        ],
        compiler_params=pltpu.CompilerParams(
            collective_id=0, has_side_effects=True, vmem_limit_bytes=60 * 1024 * 1024
        ),
        name="mega",
    )(
        kv_weight, hidden[0], queries[0], grad_out[0], doc_ids[0].reshape(16, TOK),
        q_gain.reshape(1, HD), k_gain.reshape(1, HD),
    )
    return (att[None], dq[None], gh[None], gw, qgo.reshape(HD), kgo.reshape(HD))


def solution(mesh):
    return jax.shard_map(
        shards,
        mesh=mesh,
        in_specs=(
            P("fsdp", "seq", None),
            P("fsdp", "seq", None),
            P("fsdp", None),
            P("fsdp", None),
            P(),
            P(),
            P("fsdp", "seq", None),
        ),
        out_specs=(
            P("fsdp", "seq", None),
            P("fsdp", "seq", None),
            P("fsdp", "seq", None),
            P(("seq", "fsdp"), None),
            P(),
            P(),
        ),
        check_vma=False,
    )
```

```python
import math

import jax
import jax.numpy as jnp
from jax import lax
from jax.experimental import pallas as pl
from jax.experimental.pallas import tpu as pltpu
from jax.sharding import PartitionSpec as P

MESH = pl.DeviceIdType.MESH
BF = jnp.bfloat16
F32 = jnp.float32
EPS = 1e-06
TOK = 128
HD = 128
KVH = 4
GROUP = 8
D = 2560
ROWS = 320
WIN = 9
SCALE = 1.0 / math.sqrt(HD)
LOG2E = 1.4426950408889634
NT = (((1,), (1,)), ((), ()))


class Place:
    def __init__(self):
        s = lax.axis_index("seq")
        f = lax.axis_index("fsdp")
        self.s, self.f = s, f
        self.c = lax.rem(s, 2)
        self.x = lax.rem(lax.div(s, 2), 4)
        self.yl = lax.div(s, 8)
        self.yh = lax.div(f, 4)
        self.z = lax.rem(f, 4)
        self.k = lax.div(s, 2)

    def at(self, x=None, yl=None, yh=None, z=None, c=None):
        x = self.x if x is None else x
        yl = self.yl if yl is None else yl
        yh = self.yh if yh is None else yh
        z = self.z if z is None else z
        c = self.c if c is None else c
        return ((yl * 4 + x) * 2 + c, yh * 4 + z)

    def xs(self, d):
        return lax.rem(self.x + d, 4)

    def zs(self, d):
        return lax.rem(self.z + d, 4)


class Net:
    def __init__(self, send, recv):
        self.send, self.recv, self.n = send, recv, 0
        self.sent = []

    def copy(self, src, dst, dev):
        i = self.n
        self.n += 1
        return pltpu.make_async_remote_copy(
            src_ref=src,
            dst_ref=dst,
            send_sem=self.send.at[i],
            recv_sem=self.recv.at[i],
            device_id=dev,
            device_id_type=MESH,
        )

    def start(self, copy, cond=None):
        self.sent.append((copy, cond))
        when(cond, copy.start)

    def drain(self):
        for copy, cond in self.sent:
            when(cond, copy.wait_send)


def when(cond, fn):
    if cond is None:
        fn()
    else:
        pl.when(cond)(fn)


def greet(partners):
    barrier = pltpu.get_barrier_semaphore()
    for dev in partners:
        pl.semaphore_signal(barrier, inc=1, device_id=dev, device_id_type=MESH)
    pl.semaphore_wait(barrier, len(partners))


def piece_start(i, c, z):
    return ((i // 8) * 8 + ((i // 2) % 4) * 2 + c) * 160 + ((i % 2) * 4 + z) * 20


NSEM = 208
WROWS = WIN * TOK
UNIT = 2 * TOK
CUTS = (pl.ds(0, 128), pl.ds(128, 48))
HEADS = ((0, 1, 2), (3,))


def mega_kernel(
    w, hid, q, do, docs, qg, kg,
    att, dq, gh, gw, qgo, kgo,
    wbuf, hidv, hT, hpk, hb, kv, kraw, qv, dov, xh, rq, doT, qn, dos, w_s, ds_s, mask,
    attv, dqv, ghv, part, sb, xr, yr, t0, gb, gf, st, rbs, rbr, stf, gacc, kacc, gs1, gr1, gs2, gr2,
    send, recv, loc,
):
    p = Place()
    net = Net(send, recv)
    c, x, z, k = p.c, p.x, p.z, p.k
    row1 = p.yl == 1
    sib = p.at(c=1 - c)
    near = p.at(yl=1 - p.yl)
    far = p.at(yh=1 - p.yh, yl=1 - p.yl)
    xd = [None] + [p.at(x=p.xs(d)) for d in (1, 2, 3)]
    zd = [None] + [p.at(z=p.zs(d)) for d in (1, 2, 3)]
    fard = [None] + [p.at(yh=1 - p.yh, yl=1 - p.yl, z=p.zs(d)) for d in (1, 2, 3)]
    zgroup = [(p.zs(d), lax.rem(c + e, 2)) for d in range(4) for e in range(2)][1:]
    me16 = (p.yl * 4 + x) * 2 + p.yh
    peers = []
    for i in range(1, 16):
        o = lax.rem(me16 + i, 16)
        peers.append((o, p.at(x=lax.rem(lax.div(o, 2), 4), yl=lax.div(o, 8), yh=lax.rem(o, 2))))
    cj = c * 4
    home, away = p.yh * 4, (1 - p.yh) * 4

    own = pl.ds(cj, 4)
    loads = []
    for n in range(8):
        j = lax.rem(cj + n, 8)
        cols = pl.ds(pl.multiple_of(j * 128, 128), 128)
        loads.append(pltpu.make_async_copy(w.at[:, cols], wbuf.at[p.f, j], loc.at[n]))
    loads.append(pltpu.make_async_copy(hid, hidv.at[c], loc.at[8]))
    loads.append(pltpu.make_async_copy(q, qv, loc.at[9]))
    loads.append(pltpu.make_async_copy(do, dov, loc.at[10]))
    for l in loads:
        l.start()
    for m in range(1, 5):
        @pl.when(k < m)
        def _():
            kv[c, :, pl.ds((4 - m) * UNIT, UNIT), :] = jnp.zeros((KVH, UNIT, HD), BF)
    greet([p.at(z=zz, c=cc) for zz, cc in zgroup] + [d for _, d in peers] + fard[1:])
    for l in loads[:4]:
        l.wait()

    def wcopy(f, j, lo, n, dev):
        ref = wbuf.at[f, j, pl.ds(lo, n)]
        cp = net.copy(ref, ref, dev)
        net.start(cp)
        return cp

    half, fourth = ROWS // 2, ROWS // 4
    mine4 = pl.multiple_of(x * fourth, 16)
    quarter, zp0, zp1, zm0, zm1, far_c, zpf, zmf, xs_c = ([None] * KVH for _ in range(9))

    def push(g):
        j = cj + g
        quarter[g] = [None] + [wcopy(p.f, j, mine4, fourth, fard[d]) for d in (1, 2, 3)]
        zp0[g] = wcopy(p.f, j, 0, half, zd[1])
        zm1[g] = wcopy(p.f, j, half, half, zd[3])
        far_c[g] = wcopy(p.f, j, 0, ROWS, far)
        zp1[g] = wcopy(p.f, j, half, half, zd[1])
        zm0[g] = wcopy(p.f, j, 0, half, zd[3])

    def relay(g):
        j = cj + g
        zp0[g].wait_recv()
        zpf[g] = wcopy(home + p.zs(3), j, 0, half, zd[1])
        zm1[g].wait_recv()
        zmf[g] = wcopy(home + p.zs(1), j, half, half, zd[3])
        xs_c[g] = []
        for d in (1, 3, 2):
            quarter[g][d].wait_recv()
            for e in (1, 3, 2):
                xs_c[g].append(wcopy(away + p.zs(4 - d), j, mine4, fourth, xd[e]))

    push(0)
    loads[8].wait()
    hs_c = net.copy(hidv.at[c], hidv.at[c], sib)
    net.start(hs_c)
    push(1)

    gain = jnp.broadcast_to(qg[...], (HD, HD)).T

    def prep(g):
        for h in range(g * GROUP, (g + 1) * GROUP):
            cols = slice(h * HD, (h + 1) * HD)
            t = qv[:, cols].astype(F32).T
            r = lax.rsqrt(jnp.mean(t * t, axis=0, keepdims=True) + EPS)
            xhat = t * r
            xh[:, cols] = xhat
            rq[:, cols] = jnp.broadcast_to(r, (8, HD))
            qn[g, :, (h % GROUP) * HD:(h % GROUP + 1) * HD] = (xhat * gain).astype(BF)
            doT[:, cols] = dov[:, cols].astype(F32).T

    loads[9].wait()
    loads[10].wait()
    prep(0)
    relay(0)
    push(2)
    prep(1)
    relay(1)
    push(3)
    prep(2)

    def window_mask():
        qd = docs[pl.ds(p.s, 1), :].astype(F32)
        tri = (
            lax.broadcasted_iota(jnp.int32, (TOK, TOK), 0)
            <= lax.broadcasted_iota(jnp.int32, (TOK, TOK), 1)
        )
        for d in range(WIN):
            kd = docs[pl.ds(jnp.maximum(p.s - d, 0), 1), :].astype(F32)
            kd = jnp.broadcast_to(kd, (TOK, TOK)).T
            live = jnp.where((kd == qd) & (p.s >= d), 1.0, 0.0)
            if d == 0:
                live = jnp.where(tri, live, 0.0)
            mask[pl.ds((WIN - 1 - d) * TOK, TOK), :] = live

    def clear():
        gacc[...] = jnp.zeros_like(gacc)
        kacc[...] = jnp.zeros_like(kacc)
        st[...] = jnp.zeros_like(st)
        for g in range(KVH):
            for t in range(2):
                part[t, g, pl.ds(pl.multiple_of((1 - c) * WROWS, TOK), TOK), :] = jnp.zeros((TOK, HD), BF)

    mine = z * 2 + c
    h_cps = []
    own_h = pltpu.make_async_copy(hpk.at[mine], hb.at[mine], loc.at[11])

    def exchange_hidden():
        for b in range(D // 128):
            hT[pl.ds(b * 128, 128), :] = hidv[c, :, b * 128:(b + 1) * 128].astype(F32).T
        for zc in range(4):
            for cc in range(2):
                for i in range(16):
                    hpk[zc * 2 + cc, pl.ds(i * 20, 20), :] = hT[pl.ds(piece_start(i, cc, zc), 20), :].astype(BF)
        for zc, cc in zgroup:
            cp = net.copy(hpk.at[zc * 2 + cc], hb.at[mine], p.at(z=zc, c=cc))
            net.start(cp)
            h_cps.append(cp)
        own_h.start()

    home_rows = pl.ds(4 * UNIT, UNIT)

    def unit(m):
        return pl.ds((4 - m) * UNIT, UNIT)

    y_c, x_c, b_c = [], [], []

    def project(g):
        if g == 0:
            hs_c.wait_recv()
        for cp in (zp1[g], zm0[g], far_c[g], zpf[g], zmf[g], *xs_c[g]):
            cp.wait_recv()
        lhs = jnp.concatenate([hidv[0], hidv[1]], axis=0)
        raw = jnp.dot(lhs, wbuf[:, cj + g].reshape(D, 128), preferred_element_type=F32)

        @pl.when(c == 0)
        def _():
            kraw[g] = raw
            r = lax.rsqrt(jnp.mean(raw * raw, axis=1, keepdims=True) + EPS)
            kv[0, g, home_rows, :] = (raw * r * kg[...]).astype(BF)

        @pl.when(c == 1)
        def _():
            kv[1, g, home_rows, :] = raw.astype(BF)

        cp = net.copy(kv.at[c, g, unit(0)], kv.at[c, g, unit(4)], near)
        net.start(cp, p.yl == 0)
        y_c.append(cp)
        row = [None]
        for m in (1, 2, 3):
            src = kv.at[c, g, pl.ds(pl.multiple_of(jnp.where(x + m <= 3, 4 * UNIT, 0), UNIT), UNIT)]
            cp = net.copy(src, kv.at[c, g, unit(m)], xd[m])
            net.start(cp, x + m <= 3)
            row.append(cp)
        x_c.append(row)

    def spread(g):
        when(row1, y_c[g].wait_recv)
        for m in (1, 2, 3):
            net.start(x_c[g][m], row1 & (x + m > 3))

    def share(g):
        for m in (1, 2, 3):
            when(k >= m, x_c[g][m].wait_recv)
        cp = net.copy(kv.at[c, g], kv.at[c, g], sib)
        net.start(cp)
        b_c.append(cp)

    span = pl.ds(pl.multiple_of(c * TOK, TOK), WROWS)

    def open_head(g):
        b_c[g].wait_recv()
        ka = kv[0, g, span, :]
        va = kv[1, g, span, :]
        return ka, va, ka.astype(F32).T.astype(BF), va.astype(F32).T.astype(BF)

    gain2 = jnp.concatenate([gain, gain], axis=1)

    def attend(g, pair, head):
        ka, va, kT, vT = head
        lo = pair * 256
        cols = slice(lo, lo + 256)
        full = slice(g * 1024 + lo, g * 1024 + lo + 256)
        scores = jnp.dot(ka, qn[g, :, cols], preferred_element_type=F32)
        m = mask[...]
        e = jnp.exp2(scores * (SCALE * LOG2E)) * jnp.concatenate([m, m], axis=1)
        total = jnp.sum(e, axis=0, keepdims=True)
        wt = e.astype(BF)
        w_s[:, cols] = wt
        inv = 1.0 / total
        d_out = doT[:, full]
        attT = (jnp.dot(vT, wt, preferred_element_type=F32) * inv).astype(BF).astype(F32)
        delta = jnp.sum(d_out * attT, axis=0, keepdims=True) * inv
        dsc = (d_out * inv).astype(BF)
        dos[:, cols] = dsc
        dp = jnp.dot(va, dsc, preferred_element_type=F32)
        ds = (e * (dp - delta)).astype(BF)
        ds_s[:, cols] = ds
        dy = jnp.dot(kT, ds, preferred_element_type=F32) * SCALE
        xhat = xh[:, full]
        r = rq[0:1, full]
        gacc[...] += dy * xhat
        dxh = dy * gain2
        dx = r * (dxh - xhat * jnp.mean(xhat * dxh, axis=0, keepdims=True))
        for n in range(2):
            at = slice(g * 1024 + lo + n * HD, g * 1024 + lo + (n + 1) * HD)
            attv[:, at] = attT[:, n * HD:(n + 1) * HD].T.astype(BF)
            dqv[:, at] = dx[:, n * HD:(n + 1) * HD].T.astype(BF)

    outs = []

    def close_head(g):
        dvv = lax.dot_general(w_s[...], dos[...], NT, preferred_element_type=F32)
        part[1, g, span, :] = dvv.astype(BF)
        dkk = lax.dot_general(ds_s[...], qn[g], NT, preferred_element_type=F32) * SCALE
        part[0, g, span, :] = dkk.astype(BF)
        cols = pl.ds(g * 1024, 1024)
        for n, (a, b) in enumerate(((attv, att), (dqv, dq))):
            cp = pltpu.make_async_copy(a.at[:, cols], b.at[:, cols], loc.at[12 + g * 2 + n])
            cp.start()
            outs.append(cp)

    s_c, u_c, v_c, z_c, w_c = {}, {}, {}, {}, {}

    def c1(g):
        s_c[g] = net.copy(part.at[1 - c, g], sb.at[g], sib)
        net.start(s_c[g])

    def c2(g):
        s_c[g].wait_recv()
        part[c, g] = (part[c, g].astype(F32) + sb[g].astype(F32)).astype(BF)
        u_c[g] = [None]
        for m in (1, 2, 3):
            cp = net.copy(part.at[c, g, unit(m)], xr.at[g, m - 1], xd[4 - m])
            net.start(cp, k >= m)
            u_c[g].append(cp)

    def c3(g):
        t0[...] = part[c, g, unit(0), :].astype(F32)
        for m in (1, 2, 3):
            @pl.when(x + m <= 3)
            def _():
                u_c[g][m].wait_recv()
                t0[...] += xr[g, m - 1].astype(F32)

            @pl.when((x + m > 3) & row1)
            def _():
                u_c[g][m].wait_recv()
                part[c, g, unit(4), :] = (
                    part[c, g, unit(4), :].astype(F32) + xr[g, m - 1].astype(F32)
                ).astype(BF)

        v_c[g] = net.copy(part.at[c, g, unit(4)], yr.at[g], near)
        net.start(v_c[g], row1)
        part[c, g, unit(0), :] = t0[...].astype(BF)

    def c4(g):
        t0[...] = part[c, g, unit(0), :].astype(F32)

        @pl.when(p.yl == 0)
        def _():
            v_c[g].wait_recv()
            t0[...] += yr[g].astype(F32)

        @pl.when(c == 0)
        def _():
            raw = kraw[g]
            r = lax.rsqrt(jnp.mean(raw * raw, axis=1, keepdims=True) + EPS)
            xhat = raw * r
            dy = t0[...]
            kacc[...] += jnp.sum(dy * xhat, axis=0, keepdims=True)
            dxh = dy * kg[...]
            dx = r * (dxh - xhat * jnp.mean(xhat * dxh, axis=1, keepdims=True))
            gb[0, g, z] = dx.astype(BF)

        @pl.when(c == 1)
        def _():
            gb[1, g, z] = t0[...].astype(BF)

        z_c[g] = []
        for d in (1, 3, 2):
            cp = net.copy(gb.at[c, g, z], gb.at[c, g, z], zd[d])
            net.start(cp)
            z_c[g].append(cp)

    def d1(g):
        for cp in z_c[g]:
            cp.wait_recv()
        w_c[g] = net.copy(gb.at[c, g], gb.at[c, g], sib)
        net.start(w_c[g])

    def offset(g, t):
        return (g * 2 + t) * 20 + (8 if g == 3 else 0)

    def weight_terms(g):
        w_c[g].wait_recv()
        lhs = jnp.concatenate([hb[i] for i in range(8)], axis=1)
        rhs = jnp.concatenate([gb[0, g].reshape(8 * TOK, HD), gb[1, g].reshape(8 * TOK, HD)], axis=1)
        gf[...] = jnp.dot(lhs, rhs, preferred_element_type=F32)
        for i in range(16):
            for t in range(2):
                st[i, pl.ds(offset(g, t), 20), :] = gf[pl.ds(i * 20, 20), t * HD:(t + 1) * HD]

    r_c = []

    def scatter(n):
        rows = CUTS[n]
        for i in range(16):
            rbs[i, rows] = st[i, rows].astype(BF)
        row = []
        for o, dev in peers:
            cp = net.copy(rbs.at[o, rows], rbr.at[me16, rows], dev)
            net.start(cp)
            row.append(cp)
        r_c.append(row)
        rbr[me16, rows] = rbs[me16, rows]

    def collect(n):
        rows = CUTS[n]
        for cp in r_c[n]:
            cp.wait_recv()
        total = rbr[0, rows].astype(F32)
        for i in range(1, 16):
            total = total + rbr[i, rows].astype(F32)
        stf[rows] = total
        for g in HEADS[n]:
            for t in range(2):
                at = (t * 4 + g) * HD
                gw[:, at:at + HD] = stf[pl.ds(offset(g, t), 20), :].astype(BF)

    w_sib = []

    def weight_share():
        for f in (home + p.zs(1), home + p.zs(2), home + p.zs(3), away, away + 1, away + 2, away + 3):
            ref = wbuf.at[f, own]
            cp = net.copy(ref, ref, sib)
            net.start(cp)
            w_sib.append(cp)

    project(0)
    relay(2)
    project(1)
    prep(3)
    relay(3)
    spread(0)
    window_mask()
    clear()
    project(2)
    spread(1)
    exchange_hidden()
    share(0)
    project(3)
    spread(2)

    todo = {
        0: [lambda: share(1)],
        1: [lambda: spread(3)],
        2: [lambda: share(2), weight_share],
        3: [lambda: c1(0)],
        5: [lambda: share(3)],
        6: [lambda: c2(0)],
        7: [lambda: c1(1)],
        10: [lambda: c2(1)],
        11: [lambda: c3(0), lambda: c1(2)],
        14: [lambda: c2(2)],
        15: [lambda: c1(3), lambda: c4(0)],
    }
    for g in range(KVH):
        head = open_head(g)
        for pair in range(4):
            attend(g, pair, head)
            if pair == 3:
                close_head(g)
            for fn in todo.get(g * 4 + pair, ()):
                fn()

    c3(1)
    c2(3)
    for cp in h_cps:
        cp.wait_recv()
    own_h.wait()
    d1(0)
    c3(2)
    c4(1)
    weight_terms(0)
    c3(3)
    d1(1)
    c4(2)
    weight_terms(1)
    c4(3)
    a = gacc[:, :HD] + gacc[:, HD:]
    gs1[...] = jnp.concatenate(
        [jnp.sum(a.T, axis=0, keepdims=True), kacc[...], jnp.zeros((6, HD), F32)], axis=0
    )
    g1 = []
    for zc, cc in zgroup:
        cp = net.copy(gs1, gr1.at[mine], p.at(z=zc, c=cc))
        net.start(cp)
        g1.append(cp)
    gr1[mine] = gs1[...]
    d1(2)
    weight_terms(2)
    scatter(0)
    d1(3)
    for cp in g1:
        cp.wait_recv()
    gs2[...] = jnp.sum(gr1[...], axis=0)
    g2 = []
    for o, dev in peers:
        cp = net.copy(gs2, gr2.at[me16], dev)
        net.start(cp)
        g2.append(cp)
    gr2[me16] = gs2[...]
    weight_terms(3)
    scatter(1)

    for l in loads[4:8]:
        l.wait()
    for cp in w_sib:
        cp.wait_recv()
    tokens = pl.ds(pl.multiple_of(c * TOK, TOK), TOK)
    gkv = jnp.concatenate([gb[t, g, z, tokens, :] for t in range(2) for g in range(KVH)], axis=1)
    for f in range(8):
        wv = jnp.concatenate([wbuf[f, j] for j in range(8)], axis=1)
        ghv[:, f * ROWS:(f + 1) * ROWS] = lax.dot_general(
            gkv, wv, NT, preferred_element_type=F32
        ).astype(BF)
    cp = pltpu.make_async_copy(ghv, gh, loc.at[4])
    cp.start()
    outs.append(cp)
    collect(0)
    for cp in g2:
        cp.wait_recv()
    gsum = jnp.sum(gr2[...], axis=0)
    qgo[...] = gsum[0:1]
    kgo[...] = gsum[1:2]
    for cp in outs:
        cp.wait()
    collect(1)
    net.drain()
    assert net.n <= NSEM


def finish_kernel(*refs):
    n = len(refs) // 2
    for a, b in zip(refs[:n], refs[n:]):
        b[...] = a[...]


def shards(hidden, queries, doc_ids, kv_weight, q_gain, k_gain, grad_out):
    vm = pl.BlockSpec(memory_space=pltpu.VMEM)
    hbm = pl.BlockSpec(memory_space=pl.ANY)
    sds = jax.ShapeDtypeStruct
    vmem = pltpu.VMEM
    wide = 32 * HD
    att, dq, gh, gw, qgo, kgo = pl.pallas_call(
        mega_kernel,
        out_shape=(
            sds((TOK, wide), BF),
            sds((TOK, wide), BF),
            sds((TOK, D), BF),
            sds((20, 1024), BF),
            sds((1, HD), F32),
            sds((1, HD), F32),
        ),
        in_specs=[hbm, hbm, hbm, hbm, vm, vm, vm],
        out_specs=(hbm, hbm, hbm, vm, vm, vm),
        scratch_shapes=[
            vmem((8, 8, ROWS, 128), BF),
            vmem((2, TOK, D), BF),
            vmem((D, TOK), F32),
            vmem((8, ROWS, TOK), BF),
            vmem((8, ROWS, TOK), BF),
            vmem((2, KVH, 5 * UNIT, HD), BF),
            vmem((KVH, UNIT, HD), F32),
            vmem((TOK, wide), BF),
            vmem((TOK, wide), BF),
            vmem((HD, wide), F32),
            vmem((8, wide), F32),
            vmem((HD, wide), F32),
            vmem((KVH, HD, GROUP * TOK), BF),
            vmem((HD, GROUP * TOK), BF),
            vmem((WROWS, GROUP * TOK), BF),
            vmem((WROWS, GROUP * TOK), BF),
            vmem((WROWS, TOK), F32),
            vmem((TOK, wide), BF),
            vmem((TOK, wide), BF),
            vmem((TOK, D), BF),
            vmem((2, KVH, 5 * UNIT, HD), BF),
            vmem((KVH, 5 * UNIT, HD), BF),
            vmem((KVH, 3, UNIT, HD), BF),
            vmem((KVH, UNIT, HD), BF),
            vmem((UNIT, HD), F32),
            vmem((2, KVH, 4, UNIT, HD), BF),
            vmem((ROWS, 2 * HD), F32),
            vmem((16, 176, HD), F32),
            vmem((16, 176, HD), BF),
            vmem((16, 176, HD), BF),
            vmem((176, HD), F32),
            vmem((HD, 256), F32),
            vmem((1, HD), F32),
            vmem((8, HD), F32),
            vmem((8, 8, HD), F32),
            vmem((8, HD), F32),
            vmem((16, 8, HD), F32),
            pltpu.SemaphoreType.DMA((NSEM,)),
            pltpu.SemaphoreType.DMA((NSEM,)),
            pltpu.SemaphoreType.DMA((20,)),
        ],
        compiler_params=pltpu.CompilerParams(
            collective_id=0, has_side_effects=True, vmem_limit_bytes=60 * 1024 * 1024
        ),
        name="mega",
    )(
        kv_weight, hidden[0], queries[0], grad_out[0], doc_ids[0].reshape(16, TOK),
        q_gain.reshape(1, HD), k_gain.reshape(1, HD),
    )
    def cut(width):
        return pl.BlockSpec((TOK, width), lambda i: (0, i))

    def whole(shape):
        return pl.BlockSpec(shape, lambda i: (0, 0))

    specs = [cut(1024), cut(1024), cut(D // 4), whole((20, 1024)), whole((1, HD)), whole((1, HD))]
    results = (att, dq, gh, gw, qgo, kgo)
    att, dq, gh, gw, qgo, kgo = pl.pallas_call(
        finish_kernel,
        grid=(4,),
        out_shape=tuple(sds(r.shape, r.dtype) for r in results),
        in_specs=specs,
        out_specs=tuple(specs),
        name="finish",
    )(*results)
    return (att[None], dq[None], gh[None], gw, qgo.reshape(HD), kgo.reshape(HD))


def solution(mesh):
    return jax.shard_map(
        shards,
        mesh=mesh,
        in_specs=(
            P("fsdp", "seq", None),
            P("fsdp", "seq", None),
            P("fsdp", None),
            P("fsdp", None),
            P(),
            P(),
            P("fsdp", "seq", None),
        ),
        out_specs=(
            P("fsdp", "seq", None),
            P("fsdp", "seq", None),
            P("fsdp", "seq", None),
            P(("seq", "fsdp"), None),
            P(),
            P(),
        ),
        check_vma=False,
    )
```

```python
import math

import jax
import jax.numpy as jnp
from jax import lax
from jax.experimental import pallas as pl
from jax.experimental.pallas import tpu as pltpu
from jax.sharding import PartitionSpec as P

MESH = pl.DeviceIdType.MESH
BF = jnp.bfloat16
F32 = jnp.float32
EPS = 1e-06
TOK = 128
HD = 128
KVH = 4
GROUP = 8
D = 2560
ROWS = 320
WIN = 9
SCALE = 1.0 / math.sqrt(HD)
LOG2E = 1.4426950408889634
NT = (((1,), (1,)), ((), ()))


class Place:
    def __init__(self):
        s = lax.axis_index("seq")
        f = lax.axis_index("fsdp")
        self.s, self.f = s, f
        self.c = lax.rem(s, 2)
        self.x = lax.rem(lax.div(s, 2), 4)
        self.yl = lax.div(s, 8)
        self.yh = lax.div(f, 4)
        self.z = lax.rem(f, 4)
        self.k = lax.div(s, 2)

    def at(self, x=None, yl=None, yh=None, z=None, c=None):
        x = self.x if x is None else x
        yl = self.yl if yl is None else yl
        yh = self.yh if yh is None else yh
        z = self.z if z is None else z
        c = self.c if c is None else c
        return ((yl * 4 + x) * 2 + c, yh * 4 + z)

    def xs(self, d):
        return lax.rem(self.x + d, 4)

    def zs(self, d):
        return lax.rem(self.z + d, 4)


class Net:
    def __init__(self, send, recv, dev):
        self.send, self.recv, self.dev = send, recv, dev
        self.sends, self.recvs, self.drains = 0, 0, []

    def outgoing(self, whole, cond=None):
        sem = self.send.at[self.sends]
        self.sends += 1
        self.drains.append((sem, whole, cond))
        return sem

    def incoming(self):
        self.recvs += 1
        return self.recv.at[self.recvs - 1]

    def copy(self, src, dst, dev, out, into):
        return pltpu.make_async_remote_copy(
            src_ref=src,
            dst_ref=dst,
            send_sem=out,
            recv_sem=into,
            device_id=dev,
            device_id_type=MESH,
        )

    def go(self, src, dst, dev, out, into, cond=None):
        when(cond, self.copy(src, dst, dev, out, into).start)

    def arrived(self, whole, into, cond=None):
        when(cond, self.copy(whole, whole, self.dev, self.send.at[0], into).wait_recv)

    def drain(self):
        for sem, whole, cond in self.drains:
            when(cond, self.copy(whole, whole, self.dev, sem, self.recv.at[0]).wait_send)


def when(cond, fn):
    if cond is None:
        fn()
    else:
        pl.when(cond)(fn)


def greet(partners):
    barrier = pltpu.get_barrier_semaphore()
    for dev in partners:
        pl.semaphore_signal(barrier, inc=1, device_id=dev, device_id_type=MESH)
    pl.semaphore_wait(barrier, len(partners))


def piece_start(i, c, z):
    return ((i // 8) * 8 + ((i // 2) % 4) * 2 + c) * 160 + ((i % 2) * 4 + z) * 20


NSEND = 24
NRECV = 80
WROWS = WIN * TOK
UNIT = 2 * TOK
CUTS = (pl.ds(0, 128), pl.ds(128, 48))
HEADS = ((0, 1, 2), (3,))


def mega_kernel(
    w, hid, q, do, docs_in, qg_in, kg_in,
    att, dq, gh, gw_out, qgo, kgo,
    docs, qg, kg, gw, gsum,
    wbuf, hidv, hT, hpk, hb, kv, kraw, qv, dov, xh, rq, doT, qn, dos, w_s, ds_s, mask,
    attv, dqv, ghv, part, sb, xr, yr, t0, gb, gf, st, rbs, rbr, stf, gacc, kacc, gs1, gr1, gs2, gr2,
    send, recv, loc,
):
    p = Place()
    net = Net(send, recv, p.at(c=1 - p.c))
    c, x, z, k = p.c, p.x, p.z, p.k
    row1 = p.yl == 1
    sib = p.at(c=1 - c)
    near = p.at(yl=1 - p.yl)
    far = p.at(yh=1 - p.yh, yl=1 - p.yl)
    xd = [None] + [p.at(x=p.xs(d)) for d in (1, 2, 3)]
    zd = [None] + [p.at(z=p.zs(d)) for d in (1, 2, 3)]
    fard = [None] + [p.at(yh=1 - p.yh, yl=1 - p.yl, z=p.zs(d)) for d in (1, 2, 3)]
    zgroup = [(p.zs(d), lax.rem(c + e, 2)) for d in range(4) for e in range(2)][1:]
    me16 = (p.yl * 4 + x) * 2 + p.yh
    peers = []
    for i in range(1, 16):
        o = lax.rem(me16 + i, 16)
        peers.append((o, p.at(x=lax.rem(lax.div(o, 2), 4), yl=lax.div(o, 8), yh=lax.rem(o, 2))))
    cj = c * 4
    home, away = p.yh * 4, (1 - p.yh) * 4

    own = pl.ds(cj, 4)
    loads = []
    for n in range(8):
        j = lax.rem(cj + n, 8)
        cols = pl.ds(pl.multiple_of(j * 128, 128), 128)
        loads.append(pltpu.make_async_copy(w.at[:, cols], wbuf.at[p.f, j], loc.at[n]))
    loads.append(pltpu.make_async_copy(hid, hidv.at[c], loc.at[8]))
    loads.append(pltpu.make_async_copy(q, qv, loc.at[9]))
    loads.append(pltpu.make_async_copy(do, dov, loc.at[10]))
    for n, (a, b) in enumerate(((docs_in, docs), (qg_in, qg), (kg_in, kg))):
        loads.append(pltpu.make_async_copy(a, b, loc.at[12 + n]))
    for l in loads:
        l.start()
    for m in range(1, 5):
        @pl.when(k < m)
        def _():
            kv[c, :, pl.ds((4 - m) * UNIT, UNIT), :] = jnp.zeros((KVH, UNIT, HD), BF)
    greet([p.at(z=zz, c=cc) for zz, cc in zgroup] + [d for _, d in peers] + fard[1:])
    for l in loads[:4]:
        l.wait()

    half, fourth = ROWS // 2, ROWS // 4
    mine4 = pl.multiple_of(x * fourth, 16)
    w_out = net.outgoing(wbuf.at[pl.ds(0, 7), pl.ds(0, 4)])
    in_zp, in_zm, in_quarter, in_direct, in_relayed = (
        [net.incoming() for _ in range(KVH)] for _ in range(5)
    )

    def wcopy(f, j, lo, n, dev, into):
        ref = wbuf.at[f, j, pl.ds(lo, n)]
        net.go(ref, ref, dev, w_out, into)

    def push(g):
        j = cj + g
        for d in (1, 2, 3):
            wcopy(p.f, j, mine4, fourth, fard[d], in_quarter[g])
        wcopy(p.f, j, 0, half, zd[1], in_zp[g])
        wcopy(p.f, j, half, half, zd[3], in_zm[g])
        wcopy(p.f, j, 0, ROWS, far, in_direct[g])
        wcopy(p.f, j, half, half, zd[1], in_direct[g])
        wcopy(p.f, j, 0, half, zd[3], in_direct[g])

    def count(rows):
        return part.at[0, 0, pl.ds(0, rows)]

    def relay(g):
        j = cj + g
        net.arrived(count(half), in_zp[g])
        wcopy(home + p.zs(3), j, 0, half, zd[1], in_relayed[g])
        net.arrived(count(half), in_zm[g])
        wcopy(home + p.zs(1), j, half, half, zd[3], in_relayed[g])
        net.arrived(count(3 * fourth), in_quarter[g])
        for d in (1, 3, 2):
            for e in (1, 3, 2):
                wcopy(away + p.zs(4 - d), j, mine4, fourth, xd[e], in_relayed[g])

    push(0)
    loads[8].wait()
    hs_in = net.incoming()
    net.go(hidv.at[c], hidv.at[c], sib, net.outgoing(hidv.at[c]), hs_in)
    push(1)
    for l in loads[4:8] + loads[11:]:
        l.wait()

    gain = jnp.broadcast_to(qg[...], (HD, HD)).T

    def prep(g):
        for h in range(g * GROUP, (g + 1) * GROUP):
            cols = slice(h * HD, (h + 1) * HD)
            t = qv[:, cols].astype(F32).T
            r = lax.rsqrt(jnp.mean(t * t, axis=0, keepdims=True) + EPS)
            xhat = t * r
            xh[:, cols] = xhat
            rq[:, cols] = jnp.broadcast_to(r, (8, HD))
            qn[g, :, (h % GROUP) * HD:(h % GROUP + 1) * HD] = (xhat * gain).astype(BF)
            doT[:, cols] = dov[:, cols].astype(F32).T

    loads[9].wait()
    loads[10].wait()
    prep(0)
    relay(0)
    push(2)
    prep(1)
    relay(1)
    push(3)
    prep(2)

    def window_mask():
        qd = docs[pl.ds(p.s, 1), :].astype(F32)
        tri = (
            lax.broadcasted_iota(jnp.int32, (TOK, TOK), 0)
            <= lax.broadcasted_iota(jnp.int32, (TOK, TOK), 1)
        )
        for d in range(WIN):
            kd = docs[pl.ds(jnp.maximum(p.s - d, 0), 1), :].astype(F32)
            kd = jnp.broadcast_to(kd, (TOK, TOK)).T
            live = jnp.where((kd == qd) & (p.s >= d), 1.0, 0.0)
            if d == 0:
                live = jnp.where(tri, live, 0.0)
            mask[pl.ds((WIN - 1 - d) * TOK, TOK), :] = live

    def clear():
        gacc[...] = jnp.zeros_like(gacc)
        kacc[...] = jnp.zeros_like(kacc)
        st[...] = jnp.zeros_like(st)
        for g in range(KVH):
            for t in range(2):
                part[t, g, pl.ds(pl.multiple_of((1 - c) * WROWS, TOK), TOK), :] = jnp.zeros((TOK, HD), BF)

    mine = z * 2 + c
    h_in = net.incoming()
    own_h = pltpu.make_async_copy(hpk.at[mine], hb.at[mine], loc.at[11])

    def exchange_hidden():
        for b in range(D // 128):
            hT[pl.ds(b * 128, 128), :] = hidv[c, :, b * 128:(b + 1) * 128].astype(F32).T
        for zc in range(4):
            for cc in range(2):
                for i in range(16):
                    hpk[zc * 2 + cc, pl.ds(i * 20, 20), :] = hT[pl.ds(piece_start(i, cc, zc), 20), :].astype(BF)
        out = net.outgoing(hpk.at[pl.ds(0, 7)])
        for zc, cc in zgroup:
            net.go(hpk.at[zc * 2 + cc], hb.at[mine], p.at(z=zc, c=cc), out, h_in)
        own_h.start()

    home_rows = pl.ds(4 * UNIT, UNIT)

    def unit(m):
        return pl.ds((4 - m) * UNIT, UNIT)

    four = kv.at[c, :, pl.ds(0, UNIT)]
    one = kv.at[c, 0, pl.ds(0, UNIT)]
    y_out = net.outgoing(four, p.yl == 0)
    x_out = [None] + [net.outgoing(four, row1 | (x + m <= 3)) for m in (1, 2, 3)]
    b_out = net.outgoing(kv.at[c])
    y_in = [net.incoming() for _ in range(KVH)]
    x_in = [[None] + [net.incoming() for _ in range(3)] for _ in range(KVH)]
    b_in = [net.incoming() for _ in range(KVH)]

    def along_x(g, m, src, cond):
        net.go(kv.at[c, g, src], kv.at[c, g, unit(m)], xd[m], x_out[m], x_in[g][m], cond)


    def project(g):
        if g == 0:
            net.arrived(hidv.at[c], hs_in)
        net.arrived(count(2 * ROWS), in_direct[g])
        net.arrived(count(ROWS + 9 * fourth), in_relayed[g])
        lhs = jnp.concatenate([hidv[0], hidv[1]], axis=0)
        raw = jnp.dot(lhs, wbuf[:, cj + g].reshape(D, 128), preferred_element_type=F32)

        @pl.when(c == 0)
        def _():
            kraw[g] = raw
            r = lax.rsqrt(jnp.mean(raw * raw, axis=1, keepdims=True) + EPS)
            kv[0, g, home_rows, :] = (raw * r * kg[...]).astype(BF)

        @pl.when(c == 1)
        def _():
            kv[1, g, home_rows, :] = raw.astype(BF)

        net.go(kv.at[c, g, unit(0)], kv.at[c, g, unit(4)], near, y_out, y_in[g], p.yl == 0)
        for m in (1, 2, 3):
            along_x(g, m, unit(0), x + m <= 3)

    def spread(g):
        net.arrived(one, y_in[g], row1)
        for m in (1, 2, 3):
            along_x(g, m, unit(4), row1 & (x + m > 3))

    def share(g):
        for m in (1, 2, 3):
            net.arrived(one, x_in[g][m], k >= m)
        net.go(kv.at[c, g], kv.at[c, g], sib, b_out, b_in[g])

    span = pl.ds(pl.multiple_of(c * TOK, TOK), WROWS)

    def open_head(g):
        net.arrived(kv.at[c, g], b_in[g])
        ka = kv[0, g, span, :]
        va = kv[1, g, span, :]
        return ka, va, ka.astype(F32).T.astype(BF), va.astype(F32).T.astype(BF)

    gain2 = jnp.concatenate([gain, gain], axis=1)

    def attend(g, pair, head):
        ka, va, kT, vT = head
        lo = pair * 256
        cols = slice(lo, lo + 256)
        full = slice(g * 1024 + lo, g * 1024 + lo + 256)
        scores = jnp.dot(ka, qn[g, :, cols], preferred_element_type=F32)
        m = mask[...]
        e = jnp.exp2(scores * (SCALE * LOG2E)) * jnp.concatenate([m, m], axis=1)
        total = jnp.sum(e, axis=0, keepdims=True)
        wt = e.astype(BF)
        w_s[:, cols] = wt
        inv = 1.0 / total
        d_out = doT[:, full]
        attT = (jnp.dot(vT, wt, preferred_element_type=F32) * inv).astype(BF).astype(F32)
        delta = jnp.sum(d_out * attT, axis=0, keepdims=True) * inv
        dsc = (d_out * inv).astype(BF)
        dos[:, cols] = dsc
        dp = jnp.dot(va, dsc, preferred_element_type=F32)
        ds = (e * (dp - delta)).astype(BF)
        ds_s[:, cols] = ds
        dy = jnp.dot(kT, ds, preferred_element_type=F32) * SCALE
        xhat = xh[:, full]
        r = rq[0:1, full]
        gacc[...] += dy * xhat
        dxh = dy * gain2
        dx = r * (dxh - xhat * jnp.mean(xhat * dxh, axis=0, keepdims=True))
        for n in range(2):
            at = slice(g * 1024 + lo + n * HD, g * 1024 + lo + (n + 1) * HD)
            attv[:, at] = attT[:, n * HD:(n + 1) * HD].T.astype(BF)
            dqv[:, at] = dx[:, n * HD:(n + 1) * HD].T.astype(BF)

    outs = []

    def close_head(g):
        dvv = lax.dot_general(w_s[...], dos[...], NT, preferred_element_type=F32)
        part[1, g, span, :] = dvv.astype(BF)
        dkk = lax.dot_general(ds_s[...], qn[g], NT, preferred_element_type=F32) * SCALE
        part[0, g, span, :] = dkk.astype(BF)
        cols = pl.ds(g * 1024, 1024)
        for n, (a, b) in enumerate(((attv, att), (dqv, dq))):
            cp = pltpu.make_async_copy(a.at[:, cols], b.at[:, cols], loc.at[g * 2 + n])
            cp.start()
            outs.append(cp)

    s_out, w_out2 = net.outgoing(part.at[1 - c]), net.outgoing(gb.at[c])
    u_out = [None] + [net.outgoing(four, k >= m) for m in (1, 2, 3)]
    v_out = net.outgoing(four, row1)
    z_out = net.outgoing(gb.at[c, :, pl.ds(0, 3)])
    s_in, v_in, z_in, w_in = ([net.incoming() for _ in range(KVH)] for _ in range(4))
    u_in = [[None] + [net.incoming() for _ in range(3)] for _ in range(KVH)]

    def c1(g):
        net.go(part.at[1 - c, g], sb.at[g], sib, s_out, s_in[g])

    def c2(g):
        net.arrived(sb.at[g], s_in[g])
        part[c, g] = (part[c, g].astype(F32) + sb[g].astype(F32)).astype(BF)
        for m in (1, 2, 3):
            net.go(part.at[c, g, unit(m)], xr.at[g, m - 1], xd[4 - m], u_out[m], u_in[g][m], k >= m)

    def c3(g):
        t0[...] = part[c, g, unit(0), :].astype(F32)
        for m in (1, 2, 3):
            @pl.when(x + m <= 3)
            def _():
                net.arrived(xr.at[g, m - 1], u_in[g][m])
                t0[...] += xr[g, m - 1].astype(F32)

            @pl.when((x + m > 3) & row1)
            def _():
                net.arrived(xr.at[g, m - 1], u_in[g][m])
                part[c, g, unit(4), :] = (
                    part[c, g, unit(4), :].astype(F32) + xr[g, m - 1].astype(F32)
                ).astype(BF)

        net.go(part.at[c, g, unit(4)], yr.at[g], near, v_out, v_in[g], row1)
        part[c, g, unit(0), :] = t0[...].astype(BF)

    def c4(g):
        t0[...] = part[c, g, unit(0), :].astype(F32)

        @pl.when(p.yl == 0)
        def _():
            net.arrived(yr.at[g], v_in[g])
            t0[...] += yr[g].astype(F32)

        @pl.when(c == 0)
        def _():
            raw = kraw[g]
            r = lax.rsqrt(jnp.mean(raw * raw, axis=1, keepdims=True) + EPS)
            xhat = raw * r
            dy = t0[...]
            kacc[...] += jnp.sum(dy * xhat, axis=0, keepdims=True)
            dxh = dy * kg[...]
            dx = r * (dxh - xhat * jnp.mean(xhat * dxh, axis=1, keepdims=True))
            gb[0, g, z] = dx.astype(BF)

        @pl.when(c == 1)
        def _():
            gb[1, g, z] = t0[...].astype(BF)

        for d in (1, 3, 2):
            net.go(gb.at[c, g, z], gb.at[c, g, z], zd[d], z_out, z_in[g])

    def d1(g):
        net.arrived(gb.at[c, g, pl.ds(0, 3)], z_in[g])
        net.go(gb.at[c, g], gb.at[c, g], sib, w_out2, w_in[g])

    def offset(g, t):
        return (g * 2 + t) * 20 + (8 if g == 3 else 0)

    def weight_terms(g):
        net.arrived(gb.at[c, g], w_in[g])
        lhs = jnp.concatenate([hb[i] for i in range(8)], axis=1)
        rhs = jnp.concatenate([gb[0, g].reshape(8 * TOK, HD), gb[1, g].reshape(8 * TOK, HD)], axis=1)
        gf[...] = jnp.dot(lhs, rhs, preferred_element_type=F32)
        for i in range(16):
            for t in range(2):
                st[i, pl.ds(offset(g, t), 20), :] = gf[pl.ds(i * 20, 20), t * HD:(t + 1) * HD]

    r_in = [net.incoming() for _ in CUTS]

    def scatter(n):
        rows = CUTS[n]
        for i in range(16):
            rbs[i, rows] = st[i, rows].astype(BF)
        out = net.outgoing(rbs.at[pl.ds(0, 15), rows])
        for o, dev in peers:
            net.go(rbs.at[o, rows], rbr.at[me16, rows], dev, out, r_in[n])
        rbr[me16, rows] = rbs[me16, rows]

    def collect(n):
        rows = CUTS[n]
        net.arrived(rbr.at[pl.ds(0, 15), rows], r_in[n])
        total = rbr[0, rows].astype(F32)
        for i in range(1, 16):
            total = total + rbr[i, rows].astype(F32)
        stf[rows] = total
        for g in HEADS[n]:
            for t in range(2):
                at = (t * 4 + g) * HD
                gw[:, at:at + HD] = stf[pl.ds(offset(g, t), 20), :].astype(BF)

    w_in_sib = net.incoming()

    def weight_share():
        out = net.outgoing(wbuf.at[pl.ds(0, 7), pl.ds(0, 4)])
        for f in (home + p.zs(1), home + p.zs(2), home + p.zs(3), away, away + 1, away + 2, away + 3):
            ref = wbuf.at[f, own]
            net.go(ref, ref, sib, out, w_in_sib)

    project(0)
    relay(2)
    project(1)
    prep(3)
    relay(3)
    spread(0)
    window_mask()
    clear()
    project(2)
    spread(1)
    exchange_hidden()
    share(0)
    project(3)
    spread(2)

    todo = {
        0: [lambda: share(1)],
        1: [lambda: spread(3)],
        2: [lambda: share(2), weight_share],
        3: [lambda: c1(0)],
        5: [lambda: share(3)],
        6: [lambda: c2(0)],
        7: [lambda: c1(1)],
        10: [lambda: c2(1)],
        11: [lambda: c1(2)],
        12: [lambda: c3(0)],
        14: [lambda: c2(2)],
        15: [lambda: c1(3)],
    }
    for g in range(KVH):
        head = open_head(g)
        for pair in range(4):
            attend(g, pair, head)
            if pair == 3:
                close_head(g)
            for fn in todo.get(g * 4 + pair, ()):
                fn()

    c4(0)
    c3(1)
    net.arrived(hpk.at[pl.ds(0, 7)], h_in)
    own_h.wait()
    c2(3)
    c3(2)
    c4(1)
    d1(0)
    c3(3)
    c4(2)
    weight_terms(0)
    d1(1)
    c4(3)
    a = gacc[:, :HD] + gacc[:, HD:]
    gs1[...] = jnp.concatenate(
        [jnp.sum(a.T, axis=0, keepdims=True), kacc[...], jnp.zeros((6, HD), F32)], axis=0
    )
    g1_in, g2_in = net.incoming(), net.incoming()
    out = net.outgoing(gr1.at[pl.ds(0, 7)])
    for zc, cc in zgroup:
        net.go(gs1, gr1.at[mine], p.at(z=zc, c=cc), out, g1_in)
    gr1[mine] = gs1[...]
    weight_terms(1)
    d1(2)
    d1(3)
    weight_terms(2)
    scatter(0)
    net.arrived(gr1.at[pl.ds(0, 7)], g1_in)
    gs2[...] = jnp.sum(gr1[...], axis=0)
    out = net.outgoing(gr2.at[pl.ds(0, 15)])
    for o, dev in peers:
        net.go(gs2, gr2.at[me16], dev, out, g2_in)
    gr2[me16] = gs2[...]
    weight_terms(3)
    scatter(1)

    net.arrived(wbuf.at[pl.ds(0, 7), pl.ds(0, 4)], w_in_sib)
    tokens = pl.ds(pl.multiple_of(c * TOK, TOK), TOK)
    gkv = jnp.concatenate([gb[t, g, z, tokens, :] for t in range(2) for g in range(KVH)], axis=1)
    for f in range(8):
        wv = jnp.concatenate([wbuf[f, j] for j in range(8)], axis=1)
        ghv[:, f * ROWS:(f + 1) * ROWS] = lax.dot_general(
            gkv, wv, NT, preferred_element_type=F32
        ).astype(BF)
    cp = pltpu.make_async_copy(ghv, gh, loc.at[8])
    cp.start()
    outs.append(cp)
    collect(0)
    net.arrived(gr2.at[pl.ds(0, 15)], g2_in)
    gsum[...] = jnp.sum(gr2[...], axis=0)
    collect(1)
    for n, (a, b) in enumerate(((gw, gw_out), (gsum.at[pl.ds(0, 1)], qgo), (gsum.at[pl.ds(1, 1)], kgo))):
        cp = pltpu.make_async_copy(a, b, loc.at[9 + n])
        cp.start()
        outs.append(cp)
    net.drain()
    for cp in outs:
        cp.wait()
    assert net.sends <= NSEND and net.recvs <= NRECV


def finish_kernel(*refs):
    n = (len(refs) - 2) // 3
    ins, outs, held = refs[:n], refs[n:2 * n], refs[2 * n:3 * n]
    sem_in, sem_out = refs[3 * n:]
    jobs = []
    for a, b, h in zip(ins, outs, held):
        parts = 4 if a.shape[0] == TOK else 1
        width = a.shape[1] // parts
        for i in range(parts):
            at = (slice(None), pl.ds(i * width, width))
            j = len(jobs)
            jobs.append((
                pltpu.make_async_copy(a.at[at], h.at[at], sem_in.at[j]),
                pltpu.make_async_copy(h.at[at], b.at[at], sem_out.at[j]),
            ))
    for load, _ in jobs:
        load.start()
    for load, store in jobs:
        load.wait()
        store.start()
    for _, store in jobs:
        store.wait()


def shards(hidden, queries, doc_ids, kv_weight, q_gain, k_gain, grad_out):
    hbm = pl.BlockSpec(memory_space=pl.ANY)
    sds = jax.ShapeDtypeStruct
    vmem = pltpu.VMEM
    wide = 32 * HD
    att, dq, gh, gw, qgo, kgo = pl.pallas_call(
        mega_kernel,
        out_shape=(
            sds((TOK, wide), BF),
            sds((TOK, wide), BF),
            sds((TOK, D), BF),
            sds((20, 1024), BF),
            sds((1, HD), F32),
            sds((1, HD), F32),
        ),
        in_specs=[hbm] * 7,
        out_specs=(hbm,) * 6,
        scratch_shapes=[
            vmem((16, TOK), jnp.int32),
            vmem((1, HD), F32),
            vmem((1, HD), F32),
            vmem((20, 1024), BF),
            vmem((8, HD), F32),
            vmem((8, 8, ROWS, 128), BF),
            vmem((2, TOK, D), BF),
            vmem((D, TOK), F32),
            vmem((8, ROWS, TOK), BF),
            vmem((8, ROWS, TOK), BF),
            vmem((2, KVH, 5 * UNIT, HD), BF),
            vmem((KVH, UNIT, HD), F32),
            vmem((TOK, wide), BF),
            vmem((TOK, wide), BF),
            vmem((HD, wide), F32),
            vmem((8, wide), F32),
            vmem((HD, wide), F32),
            vmem((KVH, HD, GROUP * TOK), BF),
            vmem((HD, GROUP * TOK), BF),
            vmem((WROWS, GROUP * TOK), BF),
            vmem((WROWS, GROUP * TOK), BF),
            vmem((WROWS, TOK), F32),
            vmem((TOK, wide), BF),
            vmem((TOK, wide), BF),
            vmem((TOK, D), BF),
            vmem((2, KVH, 5 * UNIT, HD), BF),
            vmem((KVH, 5 * UNIT, HD), BF),
            vmem((KVH, 3, UNIT, HD), BF),
            vmem((KVH, UNIT, HD), BF),
            vmem((UNIT, HD), F32),
            vmem((2, KVH, 4, UNIT, HD), BF),
            vmem((ROWS, 2 * HD), F32),
            vmem((16, 176, HD), F32),
            vmem((16, 176, HD), BF),
            vmem((16, 176, HD), BF),
            vmem((176, HD), F32),
            vmem((HD, 256), F32),
            vmem((1, HD), F32),
            vmem((8, HD), F32),
            vmem((8, 8, HD), F32),
            vmem((8, HD), F32),
            vmem((16, 8, HD), F32),
            pltpu.SemaphoreType.DMA((NSEND,)),
            pltpu.SemaphoreType.DMA((NRECV,)),
            pltpu.SemaphoreType.DMA((15,)),
        ],
        compiler_params=pltpu.CompilerParams(
            collective_id=0, has_side_effects=True, vmem_limit_bytes=60 * 1024 * 1024
        ),
        name="mega",
    )(
        kv_weight, hidden[0], queries[0], grad_out[0], doc_ids[0].reshape(16, TOK),
        q_gain.reshape(1, HD), k_gain.reshape(1, HD),
    )
    results = (att, dq, gh, gw, qgo, kgo)
    att, dq, gh, gw, qgo, kgo = pl.pallas_call(
        finish_kernel,
        out_shape=tuple(sds(r.shape, r.dtype) for r in results),
        in_specs=[hbm] * 6,
        out_specs=(hbm,) * 6,
        scratch_shapes=[vmem(r.shape, r.dtype) for r in results]
        + [pltpu.SemaphoreType.DMA((15,))] * 2,
        compiler_params=pltpu.CompilerParams(vmem_limit_bytes=16 * 1024 * 1024),
        name="finish",
    )(*results)
    return (att[None], dq[None], gh[None], gw, qgo.reshape(HD), kgo.reshape(HD))


def solution(mesh):
    return jax.shard_map(
        shards,
        mesh=mesh,
        in_specs=(
            P("fsdp", "seq", None),
            P("fsdp", "seq", None),
            P("fsdp", None),
            P("fsdp", None),
            P(),
            P(),
            P("fsdp", "seq", None),
        ),
        out_specs=(
            P("fsdp", "seq", None),
            P("fsdp", "seq", None),
            P("fsdp", "seq", None),
            P(("seq", "fsdp"), None),
            P(),
            P(),
        ),
        check_vma=False,
    )
```

```python
import math

import jax
import jax.numpy as jnp
from jax import lax
from jax.experimental import pallas as pl
from jax.experimental.pallas import tpu as pltpu
from jax.sharding import PartitionSpec as P

MESH = pl.DeviceIdType.MESH
BF = jnp.bfloat16
F32 = jnp.float32
EPS = 1e-06
TOK = 128
HD = 128
KVH = 4
GROUP = 8
D = 2560
ROWS = 320
WIN = 9
SCALE = 1.0 / math.sqrt(HD)
LOG2E = 1.4426950408889634
NT = (((1,), (1,)), ((), ()))


class Place:
    def __init__(self):
        s = lax.axis_index("seq")
        f = lax.axis_index("fsdp")
        self.s, self.f = s, f
        self.c = lax.rem(s, 2)
        self.x = lax.rem(lax.div(s, 2), 4)
        self.yl = lax.div(s, 8)
        self.yh = lax.div(f, 4)
        self.z = lax.rem(f, 4)
        self.k = lax.div(s, 2)

    def at(self, x=None, yl=None, yh=None, z=None, c=None):
        x = self.x if x is None else x
        yl = self.yl if yl is None else yl
        yh = self.yh if yh is None else yh
        z = self.z if z is None else z
        c = self.c if c is None else c
        return ((yl * 4 + x) * 2 + c, yh * 4 + z)

    def xs(self, d):
        return lax.rem(self.x + d, 4)

    def zs(self, d):
        return lax.rem(self.z + d, 4)


class Net:
    def __init__(self, send, recv, dev):
        self.send, self.recv, self.dev = send, recv, dev
        self.sends, self.recvs, self.drains = 0, 0, []

    def outgoing(self, whole, cond=None):
        sem = self.send.at[self.sends]
        self.sends += 1
        self.drains.append((sem, whole, cond))
        return sem

    def incoming(self):
        self.recvs += 1
        return self.recv.at[self.recvs - 1]

    def copy(self, src, dst, dev, out, into):
        return pltpu.make_async_remote_copy(
            src_ref=src,
            dst_ref=dst,
            send_sem=out,
            recv_sem=into,
            device_id=dev,
            device_id_type=MESH,
        )

    def go(self, src, dst, dev, out, into, cond=None):
        when(cond, self.copy(src, dst, dev, out, into).start)

    def arrived(self, whole, into, cond=None):
        when(cond, self.copy(whole, whole, self.dev, self.send.at[0], into).wait_recv)

    def drain(self):
        for sem, whole, cond in self.drains:
            when(cond, self.copy(whole, whole, self.dev, sem, self.recv.at[0]).wait_send)


def when(cond, fn):
    if cond is None:
        fn()
    else:
        pl.when(cond)(fn)


def greet(partners):
    barrier = pltpu.get_barrier_semaphore()
    for dev in partners:
        pl.semaphore_signal(barrier, inc=1, device_id=dev, device_id_type=MESH)
    pl.semaphore_wait(barrier, len(partners))


def piece_start(i, c, z):
    return ((i // 8) * 8 + ((i // 2) % 4) * 2 + c) * 160 + ((i % 2) * 4 + z) * 20


NSEND = 24
NRECV = 88
WROWS = WIN * TOK
UNIT = 2 * TOK
CUTS = (pl.ds(0, 128), pl.ds(128, 48))
HEADS = ((0, 1, 2), (3,))


def mega_kernel(
    w, hid, q, do, docs_in, qg_in, kg_in,
    att, dq, gh, gw_out, qgo, kgo,
    docs, qg, kg, gw, gsum,
    wbuf, hidv, hT, hpk, hb, kv, kraw, qv, dov, xh, rq, doT, qn, dos, w_s, ds_s, mask,
    attv, dqv, ghv, part, sb, xr, yr, t0, gb, gf, st, rbs, rbr, stf, gacc, kacc, gs1, gr1, gs2, gr2,
    send, recv, loc,
):
    p = Place()
    net = Net(send, recv, p.at(c=1 - p.c))
    c, x, z, k = p.c, p.x, p.z, p.k
    row1 = p.yl == 1
    sib = p.at(c=1 - c)
    near = p.at(yl=1 - p.yl)
    far = p.at(yh=1 - p.yh, yl=1 - p.yl)
    xd = [None] + [p.at(x=p.xs(d)) for d in (1, 2, 3)]
    zd = [None] + [p.at(z=p.zs(d)) for d in (1, 2, 3)]
    fard = [None] + [p.at(yh=1 - p.yh, yl=1 - p.yl, z=p.zs(d)) for d in (1, 2, 3)]
    zgroup = [(p.zs(d), lax.rem(c + e, 2)) for d in range(4) for e in range(2)][1:]
    me16 = (p.yl * 4 + x) * 2 + p.yh
    peers = []
    for i in range(1, 16):
        o = lax.rem(me16 + i, 16)
        peers.append((o, p.at(x=lax.rem(lax.div(o, 2), 4), yl=lax.div(o, 8), yh=lax.rem(o, 2))))
    cj = c * 4
    home, away = p.yh * 4, (1 - p.yh) * 4

    own = pl.ds(cj, 4)
    loads = []
    for n in range(8):
        j = lax.rem(cj + n, 8)
        cols = pl.ds(pl.multiple_of(j * 128, 128), 128)
        loads.append(pltpu.make_async_copy(w.at[:, cols], wbuf.at[p.f, j], loc.at[n]))
    loads.append(pltpu.make_async_copy(hid, hidv.at[c], loc.at[8]))
    loads.append(pltpu.make_async_copy(q, qv, loc.at[9]))
    loads.append(pltpu.make_async_copy(do, dov, loc.at[10]))
    for n, (a, b) in enumerate(((docs_in, docs), (qg_in, qg), (kg_in, kg))):
        loads.append(pltpu.make_async_copy(a, b, loc.at[12 + n]))
    for l in loads:
        l.start()
    for m in range(1, 5):
        @pl.when(k < m)
        def _():
            kv[c, :, pl.ds((4 - m) * UNIT, UNIT), :] = jnp.zeros((KVH, UNIT, HD), BF)
    greet([p.at(z=zz, c=cc) for zz, cc in zgroup] + [d for _, d in peers] + fard[1:])
    for l in loads[:4]:
        l.wait()

    half, fourth = ROWS // 2, ROWS // 4
    mine4 = pl.multiple_of(x * fourth, 16)
    w_out = net.outgoing(wbuf.at[pl.ds(0, 7), pl.ds(0, 4)])
    in_zp, in_zm, in_quarter, in_direct, in_relayed = (
        [net.incoming() for _ in range(KVH)] for _ in range(5)
    )

    def wcopy(f, j, lo, n, dev, into):
        ref = wbuf.at[f, j, pl.ds(lo, n)]
        net.go(ref, ref, dev, w_out, into)

    def push(g):
        j = cj + g
        for d in (1, 2, 3):
            wcopy(p.f, j, mine4, fourth, fard[d], in_quarter[g])
        wcopy(p.f, j, 0, half, zd[1], in_zp[g])
        wcopy(p.f, j, half, half, zd[3], in_zm[g])
        wcopy(p.f, j, 0, ROWS, far, in_direct[g])
        wcopy(p.f, j, half, half, zd[1], in_direct[g])
        wcopy(p.f, j, 0, half, zd[3], in_direct[g])

    def count(rows):
        return part.at[0, 0, pl.ds(0, rows)]

    def relay(g):
        j = cj + g
        net.arrived(count(half), in_zp[g])
        wcopy(home + p.zs(3), j, 0, half, zd[1], in_relayed[g])
        net.arrived(count(half), in_zm[g])
        wcopy(home + p.zs(1), j, half, half, zd[3], in_relayed[g])
        net.arrived(count(3 * fourth), in_quarter[g])
        for d in (1, 3, 2):
            for e in (1, 3, 2):
                wcopy(away + p.zs(4 - d), j, mine4, fourth, xd[e], in_relayed[g])

    push(0)
    loads[8].wait()
    hs_in = net.incoming()
    net.go(hidv.at[c], hidv.at[c], sib, net.outgoing(hidv.at[c]), hs_in)
    push(1)
    for l in loads[4:8] + loads[11:]:
        l.wait()

    gain = jnp.broadcast_to(qg[...], (HD, HD)).T

    def prep(g):
        for h in range(g * GROUP, (g + 1) * GROUP):
            cols = slice(h * HD, (h + 1) * HD)
            t = qv[:, cols].astype(F32).T
            r = lax.rsqrt(jnp.mean(t * t, axis=0, keepdims=True) + EPS)
            xhat = t * r
            xh[:, cols] = xhat
            rq[:, cols] = jnp.broadcast_to(r, (8, HD))
            qn[g, :, (h % GROUP) * HD:(h % GROUP + 1) * HD] = (xhat * gain).astype(BF)
            doT[:, cols] = dov[:, cols].astype(F32).T

    loads[9].wait()
    loads[10].wait()
    prep(0)
    relay(0)
    push(2)
    prep(1)
    relay(1)
    push(3)
    prep(2)

    def window_mask():
        qd = docs[pl.ds(p.s, 1), :].astype(F32)
        tri = (
            lax.broadcasted_iota(jnp.int32, (TOK, TOK), 0)
            <= lax.broadcasted_iota(jnp.int32, (TOK, TOK), 1)
        )
        for d in range(WIN):
            kd = docs[pl.ds(jnp.maximum(p.s - d, 0), 1), :].astype(F32)
            kd = jnp.broadcast_to(kd, (TOK, TOK)).T
            live = jnp.where((kd == qd) & (p.s >= d), 1.0, 0.0)
            if d == 0:
                live = jnp.where(tri, live, 0.0)
            mask[pl.ds((WIN - 1 - d) * TOK, TOK), :] = live

    def clear():
        gacc[...] = jnp.zeros_like(gacc)
        kacc[...] = jnp.zeros_like(kacc)
        st[...] = jnp.zeros_like(st)
        for g in range(KVH):
            for t in range(2):
                part[t, g, pl.ds(pl.multiple_of((1 - c) * WROWS, TOK), TOK), :] = jnp.zeros((TOK, HD), BF)

    mine = z * 2 + c
    h_in = net.incoming()
    own_h = pltpu.make_async_copy(hpk.at[mine], hb.at[mine], loc.at[11])

    def exchange_hidden():
        for b in range(D // 128):
            hT[pl.ds(b * 128, 128), :] = hidv[c, :, b * 128:(b + 1) * 128].astype(F32).T
        for zc in range(4):
            for cc in range(2):
                for i in range(16):
                    hpk[zc * 2 + cc, pl.ds(i * 20, 20), :] = hT[pl.ds(piece_start(i, cc, zc), 20), :].astype(BF)
        out = net.outgoing(hpk.at[pl.ds(0, 7)])
        for zc, cc in zgroup:
            net.go(hpk.at[zc * 2 + cc], hb.at[mine], p.at(z=zc, c=cc), out, h_in)
        own_h.start()

    home_rows = pl.ds(4 * UNIT, UNIT)

    def unit(m):
        return pl.ds((4 - m) * UNIT, UNIT)

    four = kv.at[c, :, pl.ds(0, UNIT)]
    one = kv.at[c, 0, pl.ds(0, UNIT)]
    y_out = net.outgoing(four, p.yl == 0)
    x_out = [None] + [net.outgoing(four, row1 | (x + m <= 3)) for m in (1, 2, 3)]
    b_out = net.outgoing(kv.at[c])
    y_in = [net.incoming() for _ in range(KVH)]
    x_in = [[None] + [net.incoming() for _ in range(3)] for _ in range(KVH)]
    b_in = [net.incoming() for _ in range(KVH)]

    def along_x(g, m, src, cond):
        net.go(kv.at[c, g, src], kv.at[c, g, unit(m)], xd[m], x_out[m], x_in[g][m], cond)


    def project(g):
        if g == 0:
            net.arrived(hidv.at[c], hs_in)
        net.arrived(count(2 * ROWS), in_direct[g])
        net.arrived(count(ROWS + 9 * fourth), in_relayed[g])
        lhs = jnp.concatenate([hidv[0], hidv[1]], axis=0)
        raw = jnp.dot(lhs, wbuf[:, cj + g].reshape(D, 128), preferred_element_type=F32)

        @pl.when(c == 0)
        def _():
            kraw[g] = raw
            r = lax.rsqrt(jnp.mean(raw * raw, axis=1, keepdims=True) + EPS)
            kv[0, g, home_rows, :] = (raw * r * kg[...]).astype(BF)

        @pl.when(c == 1)
        def _():
            kv[1, g, home_rows, :] = raw.astype(BF)

        net.go(kv.at[c, g, unit(0)], kv.at[c, g, unit(4)], near, y_out, y_in[g], p.yl == 0)
        for m in (1, 2, 3):
            along_x(g, m, unit(0), x + m <= 3)

    def spread(g):
        net.arrived(one, y_in[g], row1)
        for m in (1, 2, 3):
            along_x(g, m, unit(4), row1 & (x + m > 3))

    def share(g):
        for m in (1, 2, 3):
            net.arrived(one, x_in[g][m], k >= m)
        net.go(kv.at[c, g], kv.at[c, g], sib, b_out, b_in[g])

    span = pl.ds(pl.multiple_of(c * TOK, TOK), WROWS)

    def open_head(g):
        net.arrived(kv.at[c, g], b_in[g])
        ka = kv[0, g, span, :]
        va = kv[1, g, span, :]
        return ka, va, ka.astype(F32).T.astype(BF), va.astype(F32).T.astype(BF)

    gain2 = jnp.concatenate([gain, gain], axis=1)

    def attend(g, pair, head):
        ka, va, kT, vT = head
        lo = pair * 256
        cols = slice(lo, lo + 256)
        full = slice(g * 1024 + lo, g * 1024 + lo + 256)
        scores = jnp.dot(ka, qn[g, :, cols], preferred_element_type=F32)
        m = mask[...]
        e = jnp.exp2(scores * (SCALE * LOG2E)) * jnp.concatenate([m, m], axis=1)
        total = jnp.sum(e, axis=0, keepdims=True)
        wt = e.astype(BF)
        w_s[:, cols] = wt
        inv = 1.0 / total
        d_out = doT[:, full]
        attT = (jnp.dot(vT, wt, preferred_element_type=F32) * inv).astype(BF).astype(F32)
        delta = jnp.sum(d_out * attT, axis=0, keepdims=True) * inv
        dsc = (d_out * inv).astype(BF)
        dos[:, cols] = dsc
        dp = jnp.dot(va, dsc, preferred_element_type=F32)
        ds = (e * (dp - delta)).astype(BF)
        ds_s[:, cols] = ds
        dy = jnp.dot(kT, ds, preferred_element_type=F32) * SCALE
        xhat = xh[:, full]
        r = rq[0:1, full]
        gacc[...] += dy * xhat
        dxh = dy * gain2
        dx = r * (dxh - xhat * jnp.mean(xhat * dxh, axis=0, keepdims=True))
        for n in range(2):
            at = slice(g * 1024 + lo + n * HD, g * 1024 + lo + (n + 1) * HD)
            attv[:, at] = attT[:, n * HD:(n + 1) * HD].T.astype(BF)
            dqv[:, at] = dx[:, n * HD:(n + 1) * HD].T.astype(BF)

    outs = []

    def close_head(g):
        dvv = lax.dot_general(w_s[...], dos[...], NT, preferred_element_type=F32)
        part[1, g, span, :] = dvv.astype(BF)
        dkk = lax.dot_general(ds_s[...], qn[g], NT, preferred_element_type=F32) * SCALE
        part[0, g, span, :] = dkk.astype(BF)
        cols = pl.ds(g * 1024, 1024)
        for n, (a, b) in enumerate(((attv, att), (dqv, dq))):
            cp = pltpu.make_async_copy(a.at[:, cols], b.at[:, cols], loc.at[g * 2 + n])
            cp.start()
            outs.append(cp)

    s_out, w_out2 = net.outgoing(part.at[1 - c]), net.outgoing(gb.at[c])
    u_out = [None] + [net.outgoing(four, k >= m) for m in (1, 2, 3)]
    v_out = net.outgoing(four, row1)
    z_out = net.outgoing(gb.at[c, :, pl.ds(0, 3)])
    s_in = [net.incoming() for _ in range(KVH)]
    pieces = [(g, h) for g in range(KVH) for h in ((None,) if g < KVH - 1 else (0, 1))]
    v_in, z_in, w_in = ({key: net.incoming() for key in pieces} for _ in range(3))
    u_in = {(g, h, m): net.incoming() for g, h in pieces for m in (1, 2, 3)}

    def part_of(h, start=0):
        return pl.ds(start, UNIT) if h is None else pl.ds(start + h * TOK, TOK)

    def unit_of(m, h):
        return part_of(h, (4 - m) * UNIT)

    def c1(g):
        net.go(part.at[1 - c, g], sb.at[g], sib, s_out, s_in[g])

    def c2(g):
        net.arrived(sb.at[g], s_in[g])
        part[c, g] = (part[c, g].astype(F32) + sb[g].astype(F32)).astype(BF)
        for h in [h for gg, h in pieces if gg == g]:
            for m in (1, 2, 3):
                net.go(
                    part.at[c, g, unit_of(m, h)], xr.at[g, m - 1, part_of(h)], xd[4 - m],
                    u_out[m], u_in[g, h, m], k >= m,
                )

    def c3(g, h=None):
        rows = part_of(h)
        t0[rows] = part[c, g, unit_of(0, h), :].astype(F32)
        for m in (1, 2, 3):
            @pl.when(x + m <= 3)
            def _():
                net.arrived(xr.at[g, m - 1, rows], u_in[g, h, m])
                t0[rows] += xr[g, m - 1, rows].astype(F32)

            @pl.when((x + m > 3) & row1)
            def _():
                net.arrived(xr.at[g, m - 1, rows], u_in[g, h, m])
                part[c, g, unit_of(4, h), :] = (
                    part[c, g, unit_of(4, h), :].astype(F32) + xr[g, m - 1, rows].astype(F32)
                ).astype(BF)

        net.go(part.at[c, g, unit_of(4, h)], yr.at[g, rows], near, v_out, v_in[g, h], row1)
        part[c, g, unit_of(0, h), :] = t0[rows].astype(BF)

    def c4(g, h=None):
        rows = part_of(h)
        t0[rows] = part[c, g, unit_of(0, h), :].astype(F32)

        @pl.when(p.yl == 0)
        def _():
            net.arrived(yr.at[g, rows], v_in[g, h])
            t0[rows] += yr[g, rows].astype(F32)

        @pl.when(c == 0)
        def _():
            raw = kraw[g, rows]
            r = lax.rsqrt(jnp.mean(raw * raw, axis=1, keepdims=True) + EPS)
            xhat = raw * r
            dy = t0[rows]
            kacc[...] += jnp.sum(dy * xhat, axis=0, keepdims=True)
            dxh = dy * kg[...]
            dx = r * (dxh - xhat * jnp.mean(xhat * dxh, axis=1, keepdims=True))
            gb[0, g, z, rows] = dx.astype(BF)

        @pl.when(c == 1)
        def _():
            gb[1, g, z, rows] = t0[rows].astype(BF)

        ref = gb.at[c, g, z, rows]
        for d in (1, 3, 2):
            net.go(ref, ref, zd[d], z_out, z_in[g, h])

    def d1(g, h=None):
        rows = part_of(h)
        net.arrived(gb.at[c, g, pl.ds(0, 3), rows], z_in[g, h])
        ref = gb.at[c, g, :, rows]
        net.go(ref, ref, sib, w_out2, w_in[g, h])

    def offset(g, t):
        return (g * 2 + t) * 20 + (8 if g == 3 else 0)

    def weight_terms(g):
        for gg, h in pieces:
            if gg == g:
                net.arrived(gb.at[c, g, :, part_of(h)], w_in[g, h])
        lhs = jnp.concatenate([hb[i] for i in range(8)], axis=1)
        rhs = jnp.concatenate([gb[0, g].reshape(8 * TOK, HD), gb[1, g].reshape(8 * TOK, HD)], axis=1)
        gf[...] = jnp.dot(lhs, rhs, preferred_element_type=F32)
        for i in range(16):
            for t in range(2):
                st[i, pl.ds(offset(g, t), 20), :] = gf[pl.ds(i * 20, 20), t * HD:(t + 1) * HD]

    r_in = [net.incoming() for _ in CUTS]

    def scatter(n):
        rows = CUTS[n]
        for i in range(16):
            rbs[i, rows] = st[i, rows].astype(BF)
        out = net.outgoing(rbs.at[pl.ds(0, 15), rows])
        for o, dev in peers:
            net.go(rbs.at[o, rows], rbr.at[me16, rows], dev, out, r_in[n])
        rbr[me16, rows] = rbs[me16, rows]

    def collect(n):
        rows = CUTS[n]
        net.arrived(rbr.at[pl.ds(0, 15), rows], r_in[n])
        total = rbr[0, rows].astype(F32)
        for i in range(1, 16):
            total = total + rbr[i, rows].astype(F32)
        stf[rows] = total
        for g in HEADS[n]:
            for t in range(2):
                at = (t * 4 + g) * HD
                gw[:, at:at + HD] = stf[pl.ds(offset(g, t), 20), :].astype(BF)

    w_in_sib = net.incoming()

    share_out = net.outgoing(wbuf.at[pl.ds(0, 7), pl.ds(0, 4)])

    def weight_share(n):
        for f in (home + p.zs(1), home + p.zs(2), home + p.zs(3), away, away + 1, away + 2, away + 3):
            ref = wbuf.at[f, cj + n]
            net.go(ref, ref, sib, share_out, w_in_sib)

    project(0)
    relay(2)
    prep(3)
    project(1)
    spread(0)
    relay(3)
    window_mask()
    clear()
    project(2)
    spread(1)
    share(0)
    exchange_hidden()
    project(3)
    spread(2)

    todo = {
        0: [lambda: share(1), lambda: spread(3)],
        3: [lambda: c1(0)],
        4: [lambda: share(2)],
        5: [lambda: weight_share(0)],
        6: [lambda: c2(0)],
        7: [lambda: c1(1), lambda: share(3)],
        8: [lambda: weight_share(1)],
        9: [lambda: weight_share(2)],
        10: [lambda: c2(1)],
        11: [lambda: c1(2)],
        12: [lambda: c3(0), lambda: weight_share(3)],
        14: [lambda: c2(2)],
        15: [lambda: c1(3)],
    }
    for g in range(KVH):
        head = open_head(g)
        for pair in range(4):
            attend(g, pair, head)
            if pair == 3:
                close_head(g)
            for fn in todo.get(g * 4 + pair, ()):
                fn()

    c4(0)
    c3(1)
    net.arrived(hpk.at[pl.ds(0, 7)], h_in)
    own_h.wait()
    c2(3)
    c3(2)
    c4(1)
    d1(0)
    c3(3, 0)
    c3(3, 1)
    c4(2)
    weight_terms(0)
    d1(1)
    c4(3, 0)
    c4(3, 1)
    a = gacc[:, :HD] + gacc[:, HD:]
    gs1[...] = jnp.concatenate(
        [jnp.sum(a.T, axis=0, keepdims=True), kacc[...], jnp.zeros((6, HD), F32)], axis=0
    )
    g1_in, g2_in = net.incoming(), net.incoming()
    out = net.outgoing(gr1.at[pl.ds(0, 7)])
    for zc, cc in zgroup:
        net.go(gs1, gr1.at[mine], p.at(z=zc, c=cc), out, g1_in)
    gr1[mine] = gs1[...]
    weight_terms(1)
    d1(2)
    d1(3, 0)
    d1(3, 1)
    weight_terms(2)
    scatter(0)
    net.arrived(gr1.at[pl.ds(0, 7)], g1_in)
    gs2[...] = jnp.sum(gr1[...], axis=0)
    out = net.outgoing(gr2.at[pl.ds(0, 15)])
    for o, dev in peers:
        net.go(gs2, gr2.at[me16], dev, out, g2_in)
    gr2[me16] = gs2[...]
    weight_terms(3)
    scatter(1)

    net.arrived(wbuf.at[pl.ds(0, 7), pl.ds(0, 4)], w_in_sib)
    tokens = pl.ds(pl.multiple_of(c * TOK, TOK), TOK)
    gkv = jnp.concatenate([gb[t, g, z, tokens, :] for t in range(2) for g in range(KVH)], axis=1)
    for f in range(8):
        wv = jnp.concatenate([wbuf[f, j] for j in range(8)], axis=1)
        ghv[:, f * ROWS:(f + 1) * ROWS] = lax.dot_general(
            gkv, wv, NT, preferred_element_type=F32
        ).astype(BF)
    cp = pltpu.make_async_copy(ghv, gh, loc.at[8])
    cp.start()
    outs.append(cp)
    collect(0)
    net.arrived(gr2.at[pl.ds(0, 15)], g2_in)
    gsum[...] = jnp.sum(gr2[...], axis=0)
    collect(1)
    for n, (a, b) in enumerate(((gw, gw_out), (gsum.at[pl.ds(0, 1)], qgo), (gsum.at[pl.ds(1, 1)], kgo))):
        cp = pltpu.make_async_copy(a, b, loc.at[9 + n])
        cp.start()
        outs.append(cp)
    net.drain()
    for cp in outs:
        cp.wait()
    assert net.sends <= NSEND and net.recvs <= NRECV


def finish_kernel(*refs):
    n = (len(refs) - 2) // 3
    ins, outs, held = refs[:n], refs[n:2 * n], refs[2 * n:3 * n]
    sem_in, sem_out = refs[3 * n:]
    jobs = []
    for a, b, h in zip(ins, outs, held):
        parts = 4 if a.shape[0] == TOK else 1
        width = a.shape[1] // parts
        for i in range(parts):
            at = (slice(None), pl.ds(i * width, width))
            j = len(jobs)
            jobs.append((
                pltpu.make_async_copy(a.at[at], h.at[at], sem_in.at[j]),
                pltpu.make_async_copy(h.at[at], b.at[at], sem_out.at[j]),
            ))
    for load, _ in jobs:
        load.start()
    for load, store in jobs:
        load.wait()
        store.start()
    for _, store in jobs:
        store.wait()


def shards(hidden, queries, doc_ids, kv_weight, q_gain, k_gain, grad_out):
    hbm = pl.BlockSpec(memory_space=pl.ANY)
    sds = jax.ShapeDtypeStruct
    vmem = pltpu.VMEM
    wide = 32 * HD
    att, dq, gh, gw, qgo, kgo = pl.pallas_call(
        mega_kernel,
        out_shape=(
            sds((TOK, wide), BF),
            sds((TOK, wide), BF),
            sds((TOK, D), BF),
            sds((20, 1024), BF),
            sds((1, HD), F32),
            sds((1, HD), F32),
        ),
        in_specs=[hbm] * 7,
        out_specs=(hbm,) * 6,
        scratch_shapes=[
            vmem((16, TOK), jnp.int32),
            vmem((1, HD), F32),
            vmem((1, HD), F32),
            vmem((20, 1024), BF),
            vmem((8, HD), F32),
            vmem((8, 8, ROWS, 128), BF),
            vmem((2, TOK, D), BF),
            vmem((D, TOK), F32),
            vmem((8, ROWS, TOK), BF),
            vmem((8, ROWS, TOK), BF),
            vmem((2, KVH, 5 * UNIT, HD), BF),
            vmem((KVH, UNIT, HD), F32),
            vmem((TOK, wide), BF),
            vmem((TOK, wide), BF),
            vmem((HD, wide), F32),
            vmem((8, wide), F32),
            vmem((HD, wide), F32),
            vmem((KVH, HD, GROUP * TOK), BF),
            vmem((HD, GROUP * TOK), BF),
            vmem((WROWS, GROUP * TOK), BF),
            vmem((WROWS, GROUP * TOK), BF),
            vmem((WROWS, TOK), F32),
            vmem((TOK, wide), BF),
            vmem((TOK, wide), BF),
            vmem((TOK, D), BF),
            vmem((2, KVH, 5 * UNIT, HD), BF),
            vmem((KVH, 5 * UNIT, HD), BF),
            vmem((KVH, 3, UNIT, HD), BF),
            vmem((KVH, UNIT, HD), BF),
            vmem((UNIT, HD), F32),
            vmem((2, KVH, 4, UNIT, HD), BF),
            vmem((ROWS, 2 * HD), F32),
            vmem((16, 176, HD), F32),
            vmem((16, 176, HD), BF),
            vmem((16, 176, HD), BF),
            vmem((176, HD), F32),
            vmem((HD, 256), F32),
            vmem((1, HD), F32),
            vmem((8, HD), F32),
            vmem((8, 8, HD), F32),
            vmem((8, HD), F32),
            vmem((16, 8, HD), F32),
            pltpu.SemaphoreType.DMA((NSEND,)),
            pltpu.SemaphoreType.DMA((NRECV,)),
            pltpu.SemaphoreType.DMA((15,)),
        ],
        compiler_params=pltpu.CompilerParams(
            collective_id=0, has_side_effects=True, vmem_limit_bytes=60 * 1024 * 1024
        ),
        name="mega",
    )(
        kv_weight, hidden[0], queries[0], grad_out[0], doc_ids[0].reshape(16, TOK),
        q_gain.reshape(1, HD), k_gain.reshape(1, HD),
    )
    results = (att, dq, gh, gw, qgo, kgo)
    att, dq, gh, gw, qgo, kgo = pl.pallas_call(
        finish_kernel,
        out_shape=tuple(sds(r.shape, r.dtype) for r in results),
        in_specs=[hbm] * 6,
        out_specs=(hbm,) * 6,
        scratch_shapes=[vmem(r.shape, r.dtype) for r in results]
        + [pltpu.SemaphoreType.DMA((15,))] * 2,
        compiler_params=pltpu.CompilerParams(vmem_limit_bytes=60 * 1024 * 1024),
        name="finish",
    )(*results)
    return (att[None], dq[None], gh[None], gw, qgo.reshape(HD), kgo.reshape(HD))


def solution(mesh):
    return jax.shard_map(
        shards,
        mesh=mesh,
        in_specs=(
            P("fsdp", "seq", None),
            P("fsdp", "seq", None),
            P("fsdp", None),
            P("fsdp", None),
            P(),
            P(),
            P("fsdp", "seq", None),
        ),
        out_specs=(
            P("fsdp", "seq", None),
            P("fsdp", "seq", None),
            P("fsdp", "seq", None),
            P(("seq", "fsdp"), None),
            P(),
            P(),
        ),
        check_vma=False,
    )
```

```python
import math

import jax
import jax.numpy as jnp
from jax import lax
from jax.experimental import pallas as pl
from jax.experimental.pallas import tpu as pltpu
from jax.sharding import PartitionSpec as P

MESH = pl.DeviceIdType.MESH
BF = jnp.bfloat16
F32 = jnp.float32
EPS = 1e-06
TOK = 128
HD = 128
KVH = 4
GROUP = 8
D = 2560
ROWS = 320
WIN = 9
SCALE = 1.0 / math.sqrt(HD)
LOG2E = 1.4426950408889634
NT = (((1,), (1,)), ((), ()))


class Place:
    def __init__(self):
        s = lax.axis_index("seq")
        f = lax.axis_index("fsdp")
        self.s, self.f = s, f
        self.c = lax.rem(s, 2)
        self.x = lax.rem(lax.div(s, 2), 4)
        self.yl = lax.div(s, 8)
        self.yh = lax.div(f, 4)
        self.z = lax.rem(f, 4)
        self.k = lax.div(s, 2)

    def at(self, x=None, yl=None, yh=None, z=None, c=None):
        x = self.x if x is None else x
        yl = self.yl if yl is None else yl
        yh = self.yh if yh is None else yh
        z = self.z if z is None else z
        c = self.c if c is None else c
        return ((yl * 4 + x) * 2 + c, yh * 4 + z)

    def xs(self, d):
        return lax.rem(self.x + d, 4)

    def zs(self, d):
        return lax.rem(self.z + d, 4)


class Net:
    def __init__(self, send, recv, dev):
        self.send, self.recv, self.dev = send, recv, dev
        self.sends, self.recvs, self.drains = 0, 0, []

    def outgoing(self, whole, cond=None):
        sem = self.send.at[self.sends]
        self.sends += 1
        self.drains.append((sem, whole, cond))
        return sem

    def incoming(self):
        self.recvs += 1
        return self.recv.at[self.recvs - 1]

    def copy(self, src, dst, dev, out, into):
        return pltpu.make_async_remote_copy(
            src_ref=src,
            dst_ref=dst,
            send_sem=out,
            recv_sem=into,
            device_id=dev,
            device_id_type=MESH,
        )

    def go(self, src, dst, dev, out, into, cond=None):
        when(cond, self.copy(src, dst, dev, out, into).start)

    def arrived(self, whole, into, cond=None):
        when(cond, self.copy(whole, whole, self.dev, self.send.at[0], into).wait_recv)

    def drain(self):
        for sem, whole, cond in self.drains:
            when(cond, self.copy(whole, whole, self.dev, sem, self.recv.at[0]).wait_send)


def when(cond, fn):
    if cond is None:
        fn()
    else:
        pl.when(cond)(fn)


def greet(partners):
    barrier = pltpu.get_barrier_semaphore()
    for dev in partners:
        pl.semaphore_signal(barrier, inc=1, device_id=dev, device_id_type=MESH)
    pl.semaphore_wait(barrier, len(partners))


def piece_start(i, c, z):
    return ((i // 8) * 8 + ((i // 2) % 4) * 2 + c) * 160 + ((i % 2) * 4 + z) * 20


NSEND = 24
NRECV = 88
WROWS = WIN * TOK
UNIT = 2 * TOK
CUTS = tuple(pl.ds(g * 48, 48) for g in range(KVH))


def mega_kernel(
    w, hid, q, do, docs_in, qg_in, kg_in,
    att, dq, gh, gw_out, qgo, kgo,
    docs, qg, kg, gw, gsum,
    wbuf, hidv, hT, hpk, hb, kv, kraw, qv, dov, xh, rq, doT, qn, dos, w_s, ds_s, mask,
    attv, dqv, ghv, part, sb, xr, yr, t0, gb, gf, st, rbs, rbr, stf, gacc, kacc, gs1, gr1, gs2, gr2,
    send, recv, loc,
):
    p = Place()
    net = Net(send, recv, p.at(c=1 - p.c))
    c, x, z, k = p.c, p.x, p.z, p.k
    row1 = p.yl == 1
    sib = p.at(c=1 - c)
    near = p.at(yl=1 - p.yl)
    far = p.at(yh=1 - p.yh, yl=1 - p.yl)
    xd = [None] + [p.at(x=p.xs(d)) for d in (1, 2, 3)]
    zd = [None] + [p.at(z=p.zs(d)) for d in (1, 2, 3)]
    fard = [None] + [p.at(yh=1 - p.yh, yl=1 - p.yl, z=p.zs(d)) for d in (1, 2, 3)]
    zgroup = [(p.zs(d), lax.rem(c + e, 2)) for d in range(4) for e in range(2)][1:]
    me16 = (p.yl * 4 + x) * 2 + p.yh
    peers = []
    for i in range(1, 16):
        o = lax.rem(me16 + i, 16)
        peers.append((o, p.at(x=lax.rem(lax.div(o, 2), 4), yl=lax.div(o, 8), yh=lax.rem(o, 2))))
    cj = c * 4
    home, away = p.yh * 4, (1 - p.yh) * 4

    own = pl.ds(cj, 4)
    loads = []
    for n in range(8):
        j = lax.rem(cj + n, 8)
        cols = pl.ds(pl.multiple_of(j * 128, 128), 128)
        loads.append(pltpu.make_async_copy(w.at[:, cols], wbuf.at[p.f, j], loc.at[n]))
    loads.append(pltpu.make_async_copy(hid, hidv.at[c], loc.at[8]))
    loads.append(pltpu.make_async_copy(q, qv, loc.at[9]))
    loads.append(pltpu.make_async_copy(do, dov, loc.at[10]))
    for n, (a, b) in enumerate(((docs_in, docs), (qg_in, qg), (kg_in, kg))):
        loads.append(pltpu.make_async_copy(a, b, loc.at[12 + n]))
    for l in loads:
        l.start()
    for m in range(1, 5):
        @pl.when(k < m)
        def _():
            kv[c, :, pl.ds((4 - m) * UNIT, UNIT), :] = jnp.zeros((KVH, UNIT, HD), BF)
    greet([p.at(z=zz, c=cc) for zz, cc in zgroup] + [d for _, d in peers] + fard[1:])
    for l in loads[:4]:
        l.wait()

    half, fourth = ROWS // 2, ROWS // 4
    mine4 = pl.multiple_of(x * fourth, 16)
    w_out = net.outgoing(wbuf.at[pl.ds(0, 7), pl.ds(0, 4)])
    in_zp, in_zm, in_quarter, in_direct, in_relayed = (
        [net.incoming() for _ in range(KVH)] for _ in range(5)
    )

    def wcopy(f, j, lo, n, dev, into):
        ref = wbuf.at[f, j, pl.ds(lo, n)]
        net.go(ref, ref, dev, w_out, into)

    def push(g):
        j = cj + g
        for d in (1, 2, 3):
            wcopy(p.f, j, mine4, fourth, fard[d], in_quarter[g])
        wcopy(p.f, j, 0, half, zd[1], in_zp[g])
        wcopy(p.f, j, half, half, zd[3], in_zm[g])
        wcopy(p.f, j, 0, ROWS, far, in_direct[g])
        wcopy(p.f, j, half, half, zd[1], in_direct[g])
        wcopy(p.f, j, 0, half, zd[3], in_direct[g])

    def count(rows):
        return part.at[0, 0, pl.ds(0, rows)]

    def relay(g):
        j = cj + g
        net.arrived(count(half), in_zp[g])
        wcopy(home + p.zs(3), j, 0, half, zd[1], in_relayed[g])
        net.arrived(count(half), in_zm[g])
        wcopy(home + p.zs(1), j, half, half, zd[3], in_relayed[g])
        net.arrived(count(3 * fourth), in_quarter[g])
        for d in (1, 3, 2):
            for e in (1, 3, 2):
                wcopy(away + p.zs(4 - d), j, mine4, fourth, xd[e], in_relayed[g])

    push(0)
    loads[8].wait()
    hs_in = net.incoming()
    net.go(hidv.at[c], hidv.at[c], sib, net.outgoing(hidv.at[c]), hs_in)
    push(1)
    for l in loads[4:8] + loads[11:]:
        l.wait()

    gain = jnp.broadcast_to(qg[...], (HD, HD)).T

    def prep(g):
        for h in range(g * GROUP, (g + 1) * GROUP):
            cols = slice(h * HD, (h + 1) * HD)
            t = qv[:, cols].astype(F32).T
            r = lax.rsqrt(jnp.mean(t * t, axis=0, keepdims=True) + EPS)
            xhat = t * r
            xh[:, cols] = xhat
            rq[:, cols] = jnp.broadcast_to(r, (8, HD))
            qn[g, :, (h % GROUP) * HD:(h % GROUP + 1) * HD] = (xhat * gain).astype(BF)
            doT[:, cols] = dov[:, cols].astype(F32).T

    loads[9].wait()
    loads[10].wait()
    prep(0)
    relay(0)
    push(2)
    prep(1)
    relay(1)
    push(3)
    prep(2)

    def window_mask():
        qd = docs[pl.ds(p.s, 1), :].astype(F32)
        tri = (
            lax.broadcasted_iota(jnp.int32, (TOK, TOK), 0)
            <= lax.broadcasted_iota(jnp.int32, (TOK, TOK), 1)
        )
        for d in range(WIN):
            kd = docs[pl.ds(jnp.maximum(p.s - d, 0), 1), :].astype(F32)
            kd = jnp.broadcast_to(kd, (TOK, TOK)).T
            live = jnp.where((kd == qd) & (p.s >= d), 1.0, 0.0)
            if d == 0:
                live = jnp.where(tri, live, 0.0)
            mask[pl.ds((WIN - 1 - d) * TOK, TOK), :] = live

    def clear():
        gacc[...] = jnp.zeros_like(gacc)
        kacc[...] = jnp.zeros_like(kacc)
        st[...] = jnp.zeros_like(st)
        for g in range(KVH):
            for t in range(2):
                part[t, g, pl.ds(pl.multiple_of((1 - c) * WROWS, TOK), TOK), :] = jnp.zeros((TOK, HD), BF)

    mine = z * 2 + c
    h_in = net.incoming()
    own_h = pltpu.make_async_copy(hpk.at[mine], hb.at[mine], loc.at[11])

    def exchange_hidden():
        for b in range(D // 128):
            hT[pl.ds(b * 128, 128), :] = hidv[c, :, b * 128:(b + 1) * 128].astype(F32).T
        for zc in range(4):
            for cc in range(2):
                for i in range(16):
                    hpk[zc * 2 + cc, pl.ds(i * 20, 20), :] = hT[pl.ds(piece_start(i, cc, zc), 20), :].astype(BF)
        out = net.outgoing(hpk.at[pl.ds(0, 7)])
        for zc, cc in zgroup:
            net.go(hpk.at[zc * 2 + cc], hb.at[mine], p.at(z=zc, c=cc), out, h_in)
        own_h.start()

    home_rows = pl.ds(4 * UNIT, UNIT)

    def unit(m):
        return pl.ds((4 - m) * UNIT, UNIT)

    four = kv.at[c, :, pl.ds(0, UNIT)]
    one = kv.at[c, 0, pl.ds(0, UNIT)]
    y_out = net.outgoing(four, p.yl == 0)
    x_out = [None] + [net.outgoing(four, row1 | (x + m <= 3)) for m in (1, 2, 3)]
    b_out = net.outgoing(kv.at[c])
    y_in = [net.incoming() for _ in range(KVH)]
    x_in = [[None] + [net.incoming() for _ in range(3)] for _ in range(KVH)]
    b_in = [net.incoming() for _ in range(KVH)]

    def along_x(g, m, src, cond):
        net.go(kv.at[c, g, src], kv.at[c, g, unit(m)], xd[m], x_out[m], x_in[g][m], cond)


    def project(g):
        if g == 0:
            net.arrived(hidv.at[c], hs_in)
        net.arrived(count(2 * ROWS), in_direct[g])
        net.arrived(count(ROWS + 9 * fourth), in_relayed[g])
        lhs = jnp.concatenate([hidv[0], hidv[1]], axis=0)
        raw = jnp.dot(lhs, wbuf[:, cj + g].reshape(D, 128), preferred_element_type=F32)

        @pl.when(c == 0)
        def _():
            kraw[g] = raw
            r = lax.rsqrt(jnp.mean(raw * raw, axis=1, keepdims=True) + EPS)
            kv[0, g, home_rows, :] = (raw * r * kg[...]).astype(BF)

        @pl.when(c == 1)
        def _():
            kv[1, g, home_rows, :] = raw.astype(BF)

        net.go(kv.at[c, g, unit(0)], kv.at[c, g, unit(4)], near, y_out, y_in[g], p.yl == 0)
        for m in (1, 2, 3):
            along_x(g, m, unit(0), x + m <= 3)

    def spread(g):
        net.arrived(one, y_in[g], row1)
        for m in (1, 2, 3):
            along_x(g, m, unit(4), row1 & (x + m > 3))

    def share(g):
        for m in (1, 2, 3):
            net.arrived(one, x_in[g][m], k >= m)
        net.go(kv.at[c, g], kv.at[c, g], sib, b_out, b_in[g])

    span = pl.ds(pl.multiple_of(c * TOK, TOK), WROWS)

    def open_head(g):
        net.arrived(kv.at[c, g], b_in[g])
        ka = kv[0, g, span, :]
        va = kv[1, g, span, :]
        return ka, va, ka.astype(F32).T.astype(BF), va.astype(F32).T.astype(BF)

    gain2 = jnp.concatenate([gain, gain], axis=1)

    def attend(g, pair, head):
        ka, va, kT, vT = head
        lo = pair * 256
        cols = slice(lo, lo + 256)
        full = slice(g * 1024 + lo, g * 1024 + lo + 256)
        scores = jnp.dot(ka, qn[g, :, cols], preferred_element_type=F32)
        m = mask[...]
        e = jnp.exp2(scores * (SCALE * LOG2E)) * jnp.concatenate([m, m], axis=1)
        total = jnp.sum(e, axis=0, keepdims=True)
        wt = e.astype(BF)
        w_s[:, cols] = wt
        inv = 1.0 / total
        d_out = doT[:, full]
        attT = (jnp.dot(vT, wt, preferred_element_type=F32) * inv).astype(BF).astype(F32)
        delta = jnp.sum(d_out * attT, axis=0, keepdims=True) * inv
        dsc = (d_out * inv).astype(BF)
        dos[:, cols] = dsc
        dp = jnp.dot(va, dsc, preferred_element_type=F32)
        ds = (e * (dp - delta)).astype(BF)
        ds_s[:, cols] = ds
        dy = jnp.dot(kT, ds, preferred_element_type=F32) * SCALE
        xhat = xh[:, full]
        r = rq[0:1, full]
        gacc[...] += dy * xhat
        dxh = dy * gain2
        dx = r * (dxh - xhat * jnp.mean(xhat * dxh, axis=0, keepdims=True))
        for n in range(2):
            at = slice(g * 1024 + lo + n * HD, g * 1024 + lo + (n + 1) * HD)
            attv[:, at] = attT[:, n * HD:(n + 1) * HD].T.astype(BF)
            dqv[:, at] = dx[:, n * HD:(n + 1) * HD].T.astype(BF)

    outs = []

    def close_head(g):
        dvv = lax.dot_general(w_s[...], dos[...], NT, preferred_element_type=F32)
        part[1, g, span, :] = dvv.astype(BF)
        dkk = lax.dot_general(ds_s[...], qn[g], NT, preferred_element_type=F32) * SCALE
        part[0, g, span, :] = dkk.astype(BF)
        cols = pl.ds(g * 1024, 1024)
        for n, (a, b) in enumerate(((attv, att), (dqv, dq))):
            cp = pltpu.make_async_copy(a.at[:, cols], b.at[:, cols], loc.at[g * 2 + n])
            cp.start()
            outs.append(cp)

    s_out, w_out2 = net.outgoing(part.at[1 - c]), net.outgoing(gb.at[c])
    u_out = [None] + [net.outgoing(four, k >= m) for m in (1, 2, 3)]
    v_out = net.outgoing(four, row1)
    z_out = net.outgoing(gb.at[c, :, pl.ds(0, 3)])
    s_in = [net.incoming() for _ in range(KVH)]
    pieces = [(g, h) for g in range(KVH) for h in ((None,) if g < KVH - 1 else (0, 1))]
    v_in, z_in, w_in = ({key: net.incoming() for key in pieces} for _ in range(3))
    u_in = {(g, h, m): net.incoming() for g, h in pieces for m in (1, 2, 3)}

    def part_of(h, start=0):
        return pl.ds(start, UNIT) if h is None else pl.ds(start + h * TOK, TOK)

    def unit_of(m, h):
        return part_of(h, (4 - m) * UNIT)

    def c1(g):
        net.go(part.at[1 - c, g], sb.at[g], sib, s_out, s_in[g])

    def c2(g):
        net.arrived(sb.at[g], s_in[g])
        part[c, g] = (part[c, g].astype(F32) + sb[g].astype(F32)).astype(BF)
        for h in [h for gg, h in pieces if gg == g]:
            for m in (1, 2, 3):
                net.go(
                    part.at[c, g, unit_of(m, h)], xr.at[g, m - 1, part_of(h)], xd[4 - m],
                    u_out[m], u_in[g, h, m], k >= m,
                )

    def c3(g, h=None):
        rows = part_of(h)
        t0[rows] = part[c, g, unit_of(0, h), :].astype(F32)
        for m in (1, 2, 3):
            @pl.when(x + m <= 3)
            def _():
                net.arrived(xr.at[g, m - 1, rows], u_in[g, h, m])
                t0[rows] += xr[g, m - 1, rows].astype(F32)

            @pl.when((x + m > 3) & row1)
            def _():
                net.arrived(xr.at[g, m - 1, rows], u_in[g, h, m])
                part[c, g, unit_of(4, h), :] = (
                    part[c, g, unit_of(4, h), :].astype(F32) + xr[g, m - 1, rows].astype(F32)
                ).astype(BF)

        net.go(part.at[c, g, unit_of(4, h)], yr.at[g, rows], near, v_out, v_in[g, h], row1)
        part[c, g, unit_of(0, h), :] = t0[rows].astype(BF)

    def c4(g, h=None):
        rows = part_of(h)
        t0[rows] = part[c, g, unit_of(0, h), :].astype(F32)

        @pl.when(p.yl == 0)
        def _():
            net.arrived(yr.at[g, rows], v_in[g, h])
            t0[rows] += yr[g, rows].astype(F32)

        @pl.when(c == 0)
        def _():
            raw = kraw[g, rows]
            r = lax.rsqrt(jnp.mean(raw * raw, axis=1, keepdims=True) + EPS)
            xhat = raw * r
            dy = t0[rows]
            kacc[...] += jnp.sum(dy * xhat, axis=0, keepdims=True)
            dxh = dy * kg[...]
            dx = r * (dxh - xhat * jnp.mean(xhat * dxh, axis=1, keepdims=True))
            gb[0, g, z, rows] = dx.astype(BF)

        @pl.when(c == 1)
        def _():
            gb[1, g, z, rows] = t0[rows].astype(BF)

        ref = gb.at[c, g, z, rows]
        for d in (1, 3, 2):
            net.go(ref, ref, zd[d], z_out, z_in[g, h])

    def d1(g, h=None):
        rows = part_of(h)
        net.arrived(gb.at[c, g, pl.ds(0, 3), rows], z_in[g, h])
        ref = gb.at[c, g, :, rows]
        net.go(ref, ref, sib, w_out2, w_in[g, h])

    def offset(g, t):
        return g * 48 + t * 20

    def weight_terms(g):
        for gg, h in pieces:
            if gg == g:
                net.arrived(gb.at[c, g, :, part_of(h)], w_in[g, h])
        lhs = jnp.concatenate([hb[i] for i in range(8)], axis=1)
        rhs = jnp.concatenate([gb[0, g].reshape(8 * TOK, HD), gb[1, g].reshape(8 * TOK, HD)], axis=1)
        gf[...] = jnp.dot(lhs, rhs, preferred_element_type=F32)
        for i in range(16):
            for t in range(2):
                st[i, pl.ds(offset(g, t), 20), :] = gf[pl.ds(i * 20, 20), t * HD:(t + 1) * HD]

    r_in = [net.incoming() for _ in CUTS]

    def scatter(n):
        rows = CUTS[n]
        for i in range(16):
            rbs[i, rows] = st[i, rows].astype(BF)
        out = net.outgoing(rbs.at[pl.ds(0, 15), rows])
        for o, dev in peers:
            net.go(rbs.at[o, rows], rbr.at[me16, rows], dev, out, r_in[n])
        rbr[me16, rows] = rbs[me16, rows]

    def collect(n):
        rows = CUTS[n]
        net.arrived(rbr.at[pl.ds(0, 15), rows], r_in[n])
        total = rbr[0, rows].astype(F32)
        for i in range(1, 16):
            total = total + rbr[i, rows].astype(F32)
        stf[rows] = total
        for t in range(2):
            at = (t * 4 + n) * HD
            gw[:, at:at + HD] = stf[pl.ds(offset(n, t), 20), :].astype(BF)

    w_in_sib = net.incoming()

    share_out = net.outgoing(wbuf.at[pl.ds(0, 7), pl.ds(0, 4)])

    def weight_share(n):
        for f in (home + p.zs(1), home + p.zs(2), home + p.zs(3), away, away + 1, away + 2, away + 3):
            ref = wbuf.at[f, cj + n]
            net.go(ref, ref, sib, share_out, w_in_sib)

    project(0)
    relay(2)
    prep(3)
    project(1)
    spread(0)
    relay(3)
    window_mask()
    clear()
    project(2)
    spread(1)
    share(0)
    exchange_hidden()
    project(3)
    spread(2)

    todo = {
        0: [lambda: share(1), lambda: spread(3)],
        3: [lambda: c1(0), lambda: share(2)],
        7: [lambda: c2(0), lambda: share(3), lambda: c1(1), lambda: weight_share(0)],
        10: [lambda: c2(1), lambda: weight_share(1)],
        11: [lambda: c1(2), lambda: weight_share(2)],
        14: [lambda: c3(0), lambda: c2(2), lambda: weight_share(3)],
        15: [lambda: c1(3)],
    }
    for g in range(KVH):
        head = open_head(g)
        for pair in range(4):
            attend(g, pair, head)
            if pair == 3:
                close_head(g)
            for fn in todo.get(g * 4 + pair, ()):
                fn()

    c4(0)
    c3(1)
    net.arrived(hpk.at[pl.ds(0, 7)], h_in)
    own_h.wait()
    c2(3)
    c3(2)
    c4(1)
    d1(0)
    c3(3, 0)
    c3(3, 1)
    c4(2)
    weight_terms(0)
    scatter(0)
    d1(1)
    c4(3, 0)
    c4(3, 1)
    a = gacc[:, :HD] + gacc[:, HD:]
    gs1[...] = jnp.concatenate(
        [jnp.sum(a.T, axis=0, keepdims=True), kacc[...], jnp.zeros((6, HD), F32)], axis=0
    )
    g1_in, g2_in = net.incoming(), net.incoming()
    out = net.outgoing(gr1.at[pl.ds(0, 7)])
    for zc, cc in zgroup:
        net.go(gs1, gr1.at[mine], p.at(z=zc, c=cc), out, g1_in)
    gr1[mine] = gs1[...]
    weight_terms(1)
    scatter(1)
    d1(2)
    d1(3, 0)
    d1(3, 1)
    weight_terms(2)
    scatter(2)
    net.arrived(gr1.at[pl.ds(0, 7)], g1_in)
    gs2[...] = jnp.sum(gr1[...], axis=0)
    out = net.outgoing(gr2.at[pl.ds(0, 15)])
    for o, dev in peers:
        net.go(gs2, gr2.at[me16], dev, out, g2_in)
    gr2[me16] = gs2[...]
    weight_terms(3)
    scatter(3)

    net.arrived(wbuf.at[pl.ds(0, 7), pl.ds(0, 4)], w_in_sib)
    tokens = pl.ds(pl.multiple_of(c * TOK, TOK), TOK)
    gkv = jnp.concatenate([gb[t, g, z, tokens, :] for t in range(2) for g in range(KVH)], axis=1)
    for f in range(8):
        wv = jnp.concatenate([wbuf[f, j] for j in range(8)], axis=1)
        ghv[:, f * ROWS:(f + 1) * ROWS] = lax.dot_general(
            gkv, wv, NT, preferred_element_type=F32
        ).astype(BF)
    cp = pltpu.make_async_copy(ghv, gh, loc.at[8])
    cp.start()
    outs.append(cp)
    collect(0)
    collect(1)
    collect(2)
    net.arrived(gr2.at[pl.ds(0, 15)], g2_in)
    gsum[...] = jnp.sum(gr2[...], axis=0)
    collect(3)
    for n, (a, b) in enumerate(((gw, gw_out), (gsum.at[pl.ds(0, 1)], qgo), (gsum.at[pl.ds(1, 1)], kgo))):
        cp = pltpu.make_async_copy(a, b, loc.at[9 + n])
        cp.start()
        outs.append(cp)
    net.drain()
    for cp in outs:
        cp.wait()
    assert net.sends <= NSEND and net.recvs <= NRECV


def finish_kernel(*refs):
    n = (len(refs) - 2) // 3
    ins, outs, held = refs[:n], refs[n:2 * n], refs[2 * n:3 * n]
    sem_in, sem_out = refs[3 * n:]
    jobs = []
    for a, b, h in zip(ins, outs, held):
        parts = 4 if a.shape[0] == TOK else 1
        width = a.shape[1] // parts
        for i in range(parts):
            at = (slice(None), pl.ds(i * width, width))
            j = len(jobs)
            jobs.append((
                pltpu.make_async_copy(a.at[at], h.at[at], sem_in.at[j]),
                pltpu.make_async_copy(h.at[at], b.at[at], sem_out.at[j]),
            ))
    for load, _ in jobs:
        load.start()
    for load, store in jobs:
        load.wait()
        store.start()
    for _, store in jobs:
        store.wait()


def shards(hidden, queries, doc_ids, kv_weight, q_gain, k_gain, grad_out):
    hbm = pl.BlockSpec(memory_space=pl.ANY)
    sds = jax.ShapeDtypeStruct
    vmem = pltpu.VMEM
    wide = 32 * HD
    att, dq, gh, gw, qgo, kgo = pl.pallas_call(
        mega_kernel,
        out_shape=(
            sds((TOK, wide), BF),
            sds((TOK, wide), BF),
            sds((TOK, D), BF),
            sds((20, 1024), BF),
            sds((1, HD), F32),
            sds((1, HD), F32),
        ),
        in_specs=[hbm] * 7,
        out_specs=(hbm,) * 6,
        scratch_shapes=[
            vmem((16, TOK), jnp.int32),
            vmem((1, HD), F32),
            vmem((1, HD), F32),
            vmem((20, 1024), BF),
            vmem((8, HD), F32),
            vmem((8, 8, ROWS, 128), BF),
            vmem((2, TOK, D), BF),
            vmem((D, TOK), F32),
            vmem((8, ROWS, TOK), BF),
            vmem((8, ROWS, TOK), BF),
            vmem((2, KVH, 5 * UNIT, HD), BF),
            vmem((KVH, UNIT, HD), F32),
            vmem((TOK, wide), BF),
            vmem((TOK, wide), BF),
            vmem((HD, wide), F32),
            vmem((8, wide), F32),
            vmem((HD, wide), F32),
            vmem((KVH, HD, GROUP * TOK), BF),
            vmem((HD, GROUP * TOK), BF),
            vmem((WROWS, GROUP * TOK), BF),
            vmem((WROWS, GROUP * TOK), BF),
            vmem((WROWS, TOK), F32),
            vmem((TOK, wide), BF),
            vmem((TOK, wide), BF),
            vmem((TOK, D), BF),
            vmem((2, KVH, 5 * UNIT, HD), BF),
            vmem((KVH, 5 * UNIT, HD), BF),
            vmem((KVH, 3, UNIT, HD), BF),
            vmem((KVH, UNIT, HD), BF),
            vmem((UNIT, HD), F32),
            vmem((2, KVH, 4, UNIT, HD), BF),
            vmem((ROWS, 2 * HD), F32),
            vmem((16, 192, HD), F32),
            vmem((16, 192, HD), BF),
            vmem((16, 192, HD), BF),
            vmem((192, HD), F32),
            vmem((HD, 256), F32),
            vmem((1, HD), F32),
            vmem((8, HD), F32),
            vmem((8, 8, HD), F32),
            vmem((8, HD), F32),
            vmem((16, 8, HD), F32),
            pltpu.SemaphoreType.DMA((NSEND,)),
            pltpu.SemaphoreType.DMA((NRECV,)),
            pltpu.SemaphoreType.DMA((15,)),
        ],
        compiler_params=pltpu.CompilerParams(
            collective_id=0, has_side_effects=True, vmem_limit_bytes=60 * 1024 * 1024
        ),
        name="mega",
    )(
        kv_weight, hidden[0], queries[0], grad_out[0], doc_ids[0].reshape(16, TOK),
        q_gain.reshape(1, HD), k_gain.reshape(1, HD),
    )
    results = (att, dq, gh, gw, qgo, kgo)
    att, dq, gh, gw, qgo, kgo = pl.pallas_call(
        finish_kernel,
        out_shape=tuple(sds(r.shape, r.dtype) for r in results),
        in_specs=[hbm] * 6,
        out_specs=(hbm,) * 6,
        scratch_shapes=[vmem(r.shape, r.dtype) for r in results]
        + [pltpu.SemaphoreType.DMA((15,))] * 2,
        compiler_params=pltpu.CompilerParams(vmem_limit_bytes=60 * 1024 * 1024),
        name="finish",
    )(*results)
    return (att[None], dq[None], gh[None], gw, qgo.reshape(HD), kgo.reshape(HD))


def solution(mesh):
    return jax.shard_map(
        shards,
        mesh=mesh,
        in_specs=(
            P("fsdp", "seq", None),
            P("fsdp", "seq", None),
            P("fsdp", None),
            P("fsdp", None),
            P(),
            P(),
            P("fsdp", "seq", None),
        ),
        out_specs=(
            P("fsdp", "seq", None),
            P("fsdp", "seq", None),
            P("fsdp", "seq", None),
            P(("seq", "fsdp"), None),
            P(),
            P(),
        ),
        check_vma=False,
    )
```

```python
import math

import jax
import jax.numpy as jnp
from jax import lax
from jax.experimental import pallas as pl
from jax.experimental.pallas import tpu as pltpu
from jax.sharding import PartitionSpec as P

MESH = pl.DeviceIdType.MESH
BF = jnp.bfloat16
F32 = jnp.float32
EPS = 1e-06
TOK = 128
HD = 128
KVH = 4
GROUP = 8
D = 2560
ROWS = 320
WIN = 9
SCALE = 1.0 / math.sqrt(HD)
LOG2E = 1.4426950408889634
NT = (((1,), (1,)), ((), ()))


class Place:
    def __init__(self):
        s = lax.axis_index("seq")
        f = lax.axis_index("fsdp")
        self.s, self.f = s, f
        self.c = lax.rem(s, 2)
        self.x = lax.rem(lax.div(s, 2), 4)
        self.yl = lax.div(s, 8)
        self.yh = lax.div(f, 4)
        self.z = lax.rem(f, 4)
        self.k = lax.div(s, 2)

    def at(self, x=None, yl=None, yh=None, z=None, c=None):
        x = self.x if x is None else x
        yl = self.yl if yl is None else yl
        yh = self.yh if yh is None else yh
        z = self.z if z is None else z
        c = self.c if c is None else c
        return ((yl * 4 + x) * 2 + c, yh * 4 + z)

    def xs(self, d):
        return lax.rem(self.x + d, 4)

    def zs(self, d):
        return lax.rem(self.z + d, 4)


class Net:
    def __init__(self, send, recv, dev):
        self.send, self.recv, self.dev = send, recv, dev
        self.sends, self.recvs, self.drains = 0, 0, []

    def outgoing(self, whole, cond=None):
        sem = self.send.at[self.sends]
        self.sends += 1
        self.drains.append((sem, whole, cond))
        return sem

    def incoming(self):
        self.recvs += 1
        return self.recv.at[self.recvs - 1]

    def copy(self, src, dst, dev, out, into):
        return pltpu.make_async_remote_copy(
            src_ref=src,
            dst_ref=dst,
            send_sem=out,
            recv_sem=into,
            device_id=dev,
            device_id_type=MESH,
        )

    def go(self, src, dst, dev, out, into, cond=None):
        when(cond, self.copy(src, dst, dev, out, into).start)

    def arrived(self, whole, into, cond=None):
        when(cond, self.copy(whole, whole, self.dev, self.send.at[0], into).wait_recv)

    def drain(self):
        for sem, whole, cond in self.drains:
            when(cond, self.copy(whole, whole, self.dev, sem, self.recv.at[0]).wait_send)


def when(cond, fn):
    if cond is None:
        fn()
    else:
        pl.when(cond)(fn)


def greet(partners):
    barrier = pltpu.get_barrier_semaphore()
    for dev in partners:
        pl.semaphore_signal(barrier, inc=1, device_id=dev, device_id_type=MESH)
    pl.semaphore_wait(barrier, len(partners))


def piece_start(i, c, z):
    return ((i // 8) * 8 + ((i // 2) % 4) * 2 + c) * 160 + ((i % 2) * 4 + z) * 20


NSEND = 24
NRECV = 88
WROWS = WIN * TOK
UNIT = 2 * TOK
CUTS = tuple(pl.ds(g * 48, 48) for g in range(KVH))


def mega_kernel(
    w, hid, q, do, docs_in, qg_in, kg_in,
    att, dq, gh, gw_out, qgo, kgo,
    docs, qg, kg, gw, gsum,
    wbuf, hidv, hT, hpk, hb, kv, kraw, qv, dov, xh, rq, doT, qn, dos, w_s, ds_s, mask,
    attv, dqv, ghv, part, sb, xr, yr, t0, gb, gf, st, rbs, rbr, stf, gacc, kacc, gs1, gr1, gs2, gr2,
    send, recv, loc,
):
    p = Place()
    net = Net(send, recv, p.at(c=1 - p.c))
    c, x, z, k = p.c, p.x, p.z, p.k
    row1 = p.yl == 1
    sib = p.at(c=1 - c)
    near = p.at(yl=1 - p.yl)
    far = p.at(yh=1 - p.yh, yl=1 - p.yl)
    xd = [None] + [p.at(x=p.xs(d)) for d in (1, 2, 3)]
    zd = [None] + [p.at(z=p.zs(d)) for d in (1, 2, 3)]
    fard = [None] + [p.at(yh=1 - p.yh, yl=1 - p.yl, z=p.zs(d)) for d in (1, 2, 3)]
    zgroup = [(p.zs(d), lax.rem(c + e, 2)) for d in range(4) for e in range(2)][1:]
    me16 = (p.yl * 4 + x) * 2 + p.yh
    peers = []
    for i in range(1, 16):
        o = lax.rem(me16 + i, 16)
        peers.append((o, p.at(x=lax.rem(lax.div(o, 2), 4), yl=lax.div(o, 8), yh=lax.rem(o, 2))))
    cj = c * 4
    home, away = p.yh * 4, (1 - p.yh) * 4

    own = pl.ds(cj, 4)
    loads = []
    for n in range(8):
        j = lax.rem(cj + n, 8)
        cols = pl.ds(pl.multiple_of(j * 128, 128), 128)
        loads.append(pltpu.make_async_copy(w.at[:, cols], wbuf.at[p.f, j], loc.at[n]))
    loads.append(pltpu.make_async_copy(hid, hidv.at[c], loc.at[8]))
    loads.append(pltpu.make_async_copy(q, qv, loc.at[9]))
    loads.append(pltpu.make_async_copy(do, dov, loc.at[10]))
    for n, (a, b) in enumerate(((docs_in, docs), (qg_in, qg), (kg_in, kg))):
        loads.append(pltpu.make_async_copy(a, b, loc.at[12 + n]))
    for l in loads:
        l.start()
    for m in range(1, 5):
        @pl.when(k < m)
        def _():
            kv[c, :, pl.ds((4 - m) * UNIT, UNIT), :] = jnp.zeros((KVH, UNIT, HD), BF)
    greet([p.at(z=zz, c=cc) for zz, cc in zgroup] + [d for _, d in peers] + fard[1:])
    for l in loads[:4]:
        l.wait()

    half, fourth = ROWS // 2, ROWS // 4
    mine4 = pl.multiple_of(x * fourth, 16)
    w_out = net.outgoing(wbuf.at[pl.ds(0, 7), pl.ds(0, 4)])
    in_zp, in_zm, in_quarter, in_direct, in_relayed = (
        [net.incoming() for _ in range(KVH)] for _ in range(5)
    )

    def wcopy(f, j, lo, n, dev, into):
        ref = wbuf.at[f, j, pl.ds(lo, n)]
        net.go(ref, ref, dev, w_out, into)

    def push(g):
        j = cj + g
        for d in (1, 2, 3):
            wcopy(p.f, j, mine4, fourth, fard[d], in_quarter[g])
        wcopy(p.f, j, 0, half, zd[1], in_zp[g])
        wcopy(p.f, j, half, half, zd[3], in_zm[g])
        wcopy(p.f, j, 0, ROWS, far, in_direct[g])
        wcopy(p.f, j, half, half, zd[1], in_direct[g])
        wcopy(p.f, j, 0, half, zd[3], in_direct[g])

    def count(rows):
        return part.at[0, 0, pl.ds(0, rows)]

    def relay(g):
        j = cj + g
        net.arrived(count(half), in_zp[g])
        wcopy(home + p.zs(3), j, 0, half, zd[1], in_relayed[g])
        net.arrived(count(half), in_zm[g])
        wcopy(home + p.zs(1), j, half, half, zd[3], in_relayed[g])
        net.arrived(count(3 * fourth), in_quarter[g])
        for d in (1, 3, 2):
            for e in (1, 3, 2):
                wcopy(away + p.zs(4 - d), j, mine4, fourth, xd[e], in_relayed[g])

    push(0)
    loads[8].wait()
    hs_in = net.incoming()
    net.go(hidv.at[c], hidv.at[c], sib, net.outgoing(hidv.at[c]), hs_in)
    push(1)
    for l in loads[4:8] + loads[11:]:
        l.wait()

    gain = jnp.broadcast_to(qg[...], (HD, HD)).T

    def prep(g):
        for h in range(g * GROUP, (g + 1) * GROUP):
            cols = slice(h * HD, (h + 1) * HD)
            t = qv[:, cols].astype(F32).T
            r = lax.rsqrt(jnp.mean(t * t, axis=0, keepdims=True) + EPS)
            xhat = t * r
            xh[:, cols] = xhat
            rq[:, cols] = jnp.broadcast_to(r, (8, HD))
            qn[g, :, (h % GROUP) * HD:(h % GROUP + 1) * HD] = (xhat * gain).astype(BF)
            doT[:, cols] = dov[:, cols].astype(F32).T

    loads[9].wait()
    loads[10].wait()
    prep(0)
    relay(0)
    push(2)
    prep(1)
    relay(1)
    push(3)
    prep(2)

    def window_mask():
        qd = docs[pl.ds(p.s, 1), :].astype(F32)
        tri = (
            lax.broadcasted_iota(jnp.int32, (TOK, TOK), 0)
            <= lax.broadcasted_iota(jnp.int32, (TOK, TOK), 1)
        )
        for d in range(WIN):
            kd = docs[pl.ds(jnp.maximum(p.s - d, 0), 1), :].astype(F32)
            kd = jnp.broadcast_to(kd, (TOK, TOK)).T
            live = jnp.where((kd == qd) & (p.s >= d), 1.0, 0.0)
            if d == 0:
                live = jnp.where(tri, live, 0.0)
            mask[pl.ds((WIN - 1 - d) * TOK, TOK), :] = live

    def clear():
        gacc[...] = jnp.zeros_like(gacc)
        kacc[...] = jnp.zeros_like(kacc)
        st[...] = jnp.zeros_like(st)
        for g in range(KVH):
            for t in range(2):
                part[t, g, pl.ds(pl.multiple_of((1 - c) * WROWS, TOK), TOK), :] = jnp.zeros((TOK, HD), BF)

    mine = z * 2 + c
    h_in = net.incoming()
    own_h = pltpu.make_async_copy(hpk.at[mine], hb.at[mine], loc.at[11])

    def exchange_hidden():
        for b in range(D // 128):
            hT[pl.ds(b * 128, 128), :] = hidv[c, :, b * 128:(b + 1) * 128].astype(F32).T
        for zc in range(4):
            for cc in range(2):
                for i in range(16):
                    hpk[zc * 2 + cc, pl.ds(i * 20, 20), :] = hT[pl.ds(piece_start(i, cc, zc), 20), :].astype(BF)
        out = net.outgoing(hpk.at[pl.ds(0, 7)])
        for zc, cc in zgroup:
            net.go(hpk.at[zc * 2 + cc], hb.at[mine], p.at(z=zc, c=cc), out, h_in)
        own_h.start()

    home_rows = pl.ds(4 * UNIT, UNIT)

    def unit(m):
        return pl.ds((4 - m) * UNIT, UNIT)

    four = kv.at[c, :, pl.ds(0, UNIT)]
    one = kv.at[c, 0, pl.ds(0, UNIT)]
    y_out = net.outgoing(four, p.yl == 0)
    x_out = [None] + [net.outgoing(four, row1 | (x + m <= 3)) for m in (1, 2, 3)]
    b_out = net.outgoing(kv.at[c])
    y_in = [net.incoming() for _ in range(KVH)]
    x_in = [[None] + [net.incoming() for _ in range(3)] for _ in range(KVH)]
    b_in = [net.incoming() for _ in range(KVH)]

    def along_x(g, m, src, cond):
        net.go(kv.at[c, g, src], kv.at[c, g, unit(m)], xd[m], x_out[m], x_in[g][m], cond)


    def project(g):
        if g == 0:
            net.arrived(hidv.at[c], hs_in)
        net.arrived(count(2 * ROWS), in_direct[g])
        net.arrived(count(ROWS + 9 * fourth), in_relayed[g])
        lhs = jnp.concatenate([hidv[0], hidv[1]], axis=0)
        raw = jnp.dot(lhs, wbuf[:, cj + g].reshape(D, 128), preferred_element_type=F32)

        @pl.when(c == 0)
        def _():
            kraw[g] = raw
            r = lax.rsqrt(jnp.mean(raw * raw, axis=1, keepdims=True) + EPS)
            kv[0, g, home_rows, :] = (raw * r * kg[...]).astype(BF)

        @pl.when(c == 1)
        def _():
            kv[1, g, home_rows, :] = raw.astype(BF)

        net.go(kv.at[c, g, unit(0)], kv.at[c, g, unit(4)], near, y_out, y_in[g], p.yl == 0)
        for m in (1, 2, 3):
            along_x(g, m, unit(0), x + m <= 3)

    def spread(g):
        net.arrived(one, y_in[g], row1)
        for m in (1, 2, 3):
            along_x(g, m, unit(4), row1 & (x + m > 3))

    def share(g):
        for m in (1, 2, 3):
            net.arrived(one, x_in[g][m], k >= m)
        net.go(kv.at[c, g], kv.at[c, g], sib, b_out, b_in[g])

    span = pl.ds(pl.multiple_of(c * TOK, TOK), WROWS)

    def open_head(g):
        net.arrived(kv.at[c, g], b_in[g])
        ka = kv[0, g, span, :]
        va = kv[1, g, span, :]
        return ka, va, ka.astype(F32).T.astype(BF), va.astype(F32).T.astype(BF)

    gain2 = jnp.concatenate([gain, gain], axis=1)

    def attend(g, pair, head):
        ka, va, kT, vT = head
        lo = pair * 256
        cols = slice(lo, lo + 256)
        full = slice(g * 1024 + lo, g * 1024 + lo + 256)
        scores = jnp.dot(ka, qn[g, :, cols], preferred_element_type=F32)
        m = mask[...]
        e = jnp.exp2(scores * (SCALE * LOG2E)) * jnp.concatenate([m, m], axis=1)
        total = jnp.sum(e, axis=0, keepdims=True)
        wt = e.astype(BF)
        w_s[:, cols] = wt
        inv = 1.0 / total
        d_out = doT[:, full]
        attT = (jnp.dot(vT, wt, preferred_element_type=F32) * inv).astype(BF).astype(F32)
        delta = jnp.sum(d_out * attT, axis=0, keepdims=True) * inv
        dsc = (d_out * inv).astype(BF)
        dos[:, cols] = dsc
        dp = jnp.dot(va, dsc, preferred_element_type=F32)
        ds = (e * (dp - delta)).astype(BF)
        ds_s[:, cols] = ds
        dy = jnp.dot(kT, ds, preferred_element_type=F32) * SCALE
        xhat = xh[:, full]
        r = rq[0:1, full]
        gacc[...] += dy * xhat
        dxh = dy * gain2
        dx = r * (dxh - xhat * jnp.mean(xhat * dxh, axis=0, keepdims=True))
        for n in range(2):
            at = slice(g * 1024 + lo + n * HD, g * 1024 + lo + (n + 1) * HD)
            attv[:, at] = attT[:, n * HD:(n + 1) * HD].T.astype(BF)
            dqv[:, at] = dx[:, n * HD:(n + 1) * HD].T.astype(BF)

    outs = []

    def close_head(g):
        dvv = lax.dot_general(w_s[...], dos[...], NT, preferred_element_type=F32)
        part[1, g, span, :] = dvv.astype(BF)
        dkk = lax.dot_general(ds_s[...], qn[g], NT, preferred_element_type=F32) * SCALE
        part[0, g, span, :] = dkk.astype(BF)
        cols = pl.ds(g * 1024, 1024)
        for n, (a, b) in enumerate(((attv, att), (dqv, dq))):
            cp = pltpu.make_async_copy(a.at[:, cols], b.at[:, cols], loc.at[g * 2 + n])
            cp.start()
            outs.append(cp)

    s_out, w_out2 = net.outgoing(part.at[1 - c]), net.outgoing(gb.at[c])
    u_out = [None] + [net.outgoing(four, k >= m) for m in (1, 2, 3)]
    v_out = net.outgoing(four, row1)
    z_out = net.outgoing(gb.at[c, :, pl.ds(0, 3)])
    s_in = [net.incoming() for _ in range(KVH)]
    pieces = [(g, h) for g in range(KVH) for h in ((None,) if g < KVH - 1 else (0, 1))]
    v_in, z_in, w_in = ({key: net.incoming() for key in pieces} for _ in range(3))
    u_in = {(g, h, m): net.incoming() for g, h in pieces for m in (1, 2, 3)}

    def part_of(h, start=0):
        return pl.ds(start, UNIT) if h is None else pl.ds(start + h * TOK, TOK)

    def unit_of(m, h):
        return part_of(h, (4 - m) * UNIT)

    def c1(g):
        net.go(part.at[1 - c, g], sb.at[g], sib, s_out, s_in[g])

    def c2(g):
        net.arrived(sb.at[g], s_in[g])
        part[c, g] = (part[c, g].astype(F32) + sb[g].astype(F32)).astype(BF)
        for h in [h for gg, h in pieces if gg == g]:
            for m in (1, 2, 3):
                net.go(
                    part.at[c, g, unit_of(m, h)], xr.at[g, m - 1, part_of(h)], xd[4 - m],
                    u_out[m], u_in[g, h, m], k >= m,
                )

    def c3(g, h=None):
        rows = part_of(h)
        t0[rows] = part[c, g, unit_of(0, h), :].astype(F32)
        for m in (1, 2, 3):
            @pl.when(x + m <= 3)
            def _():
                net.arrived(xr.at[g, m - 1, rows], u_in[g, h, m])
                t0[rows] += xr[g, m - 1, rows].astype(F32)

            @pl.when((x + m > 3) & row1)
            def _():
                net.arrived(xr.at[g, m - 1, rows], u_in[g, h, m])
                part[c, g, unit_of(4, h), :] = (
                    part[c, g, unit_of(4, h), :].astype(F32) + xr[g, m - 1, rows].astype(F32)
                ).astype(BF)

        net.go(part.at[c, g, unit_of(4, h)], yr.at[g, rows], near, v_out, v_in[g, h], row1)
        part[c, g, unit_of(0, h), :] = t0[rows].astype(BF)

    def c4(g, h=None):
        rows = part_of(h)
        t0[rows] = part[c, g, unit_of(0, h), :].astype(F32)

        @pl.when(p.yl == 0)
        def _():
            net.arrived(yr.at[g, rows], v_in[g, h])
            t0[rows] += yr[g, rows].astype(F32)

        @pl.when(c == 0)
        def _():
            raw = kraw[g, rows]
            r = lax.rsqrt(jnp.mean(raw * raw, axis=1, keepdims=True) + EPS)
            xhat = raw * r
            dy = t0[rows]
            kacc[...] += jnp.sum(dy * xhat, axis=0, keepdims=True)
            dxh = dy * kg[...]
            dx = r * (dxh - xhat * jnp.mean(xhat * dxh, axis=1, keepdims=True))
            gb[0, g, z, rows] = dx.astype(BF)

        @pl.when(c == 1)
        def _():
            gb[1, g, z, rows] = t0[rows].astype(BF)

        ref = gb.at[c, g, z, rows]
        for d in (1, 3, 2):
            net.go(ref, ref, zd[d], z_out, z_in[g, h])

    def d1(g, h=None):
        rows = part_of(h)
        net.arrived(gb.at[c, g, pl.ds(0, 3), rows], z_in[g, h])
        ref = gb.at[c, g, :, rows]
        net.go(ref, ref, sib, w_out2, w_in[g, h])

    def offset(g, t):
        return g * 48 + t * 20

    def weight_terms(g):
        for gg, h in pieces:
            if gg == g:
                net.arrived(gb.at[c, g, :, part_of(h)], w_in[g, h])
        lhs = jnp.concatenate([hb[i] for i in range(8)], axis=1)
        rhs = jnp.concatenate([gb[0, g].reshape(8 * TOK, HD), gb[1, g].reshape(8 * TOK, HD)], axis=1)
        gf[...] = jnp.dot(lhs, rhs, preferred_element_type=F32)
        for i in range(16):
            for t in range(2):
                st[i, pl.ds(offset(g, t), 20), :] = gf[pl.ds(i * 20, 20), t * HD:(t + 1) * HD]

    r_in = [net.incoming() for _ in CUTS]

    def scatter(n):
        rows = CUTS[n]
        for i in range(16):
            rbs[i, rows] = st[i, rows].astype(BF)
        out = net.outgoing(rbs.at[pl.ds(0, 15), rows])
        for o, dev in peers:
            net.go(rbs.at[o, rows], rbr.at[me16, rows], dev, out, r_in[n])
        rbr[me16, rows] = rbs[me16, rows]

    def collect(n):
        rows = CUTS[n]
        net.arrived(rbr.at[pl.ds(0, 15), rows], r_in[n])
        total = rbr[0, rows].astype(F32)
        for i in range(1, 16):
            total = total + rbr[i, rows].astype(F32)
        stf[rows] = total
        for t in range(2):
            at = (t * 4 + n) * HD
            gw[:, at:at + HD] = stf[pl.ds(offset(n, t), 20), :].astype(BF)

    w_in_sib = net.incoming()

    share_out = net.outgoing(wbuf.at[pl.ds(0, 7), pl.ds(0, 4)])

    def weight_share(n):
        for f in (home + p.zs(1), home + p.zs(2), home + p.zs(3), away, away + 1, away + 2, away + 3):
            ref = wbuf.at[f, cj + n]
            net.go(ref, ref, sib, share_out, w_in_sib)

    project(0)
    relay(2)
    prep(3)
    project(1)
    spread(0)
    relay(3)
    window_mask()
    clear()
    project(2)
    spread(1)
    share(0)
    exchange_hidden()
    project(3)

    todo = {
        0: [lambda: spread(2), lambda: share(1)],
        1: [lambda: spread(3)],
        3: [lambda: c1(0), lambda: share(2)],
        6: [lambda: c2(0)],
        7: [lambda: share(3), lambda: c1(1), lambda: weight_share(0)],
        10: [lambda: c2(1), lambda: weight_share(1)],
        11: [lambda: c1(2), lambda: c3(0), lambda: weight_share(2)],
        14: [lambda: c2(2), lambda: weight_share(3)],
        15: [lambda: c1(3), lambda: c4(0)],
    }
    for g in range(KVH):
        head = open_head(g)
        for pair in range(4):
            attend(g, pair, head)
            if pair == 3:
                close_head(g)
            for fn in todo.get(g * 4 + pair, ()):
                fn()

    c3(1)
    c2(3)
    c4(1)
    c3(2)
    c3(3, 0)
    c3(3, 1)
    c4(2)
    d1(0)
    c4(3, 0)
    c4(3, 1)
    net.arrived(hpk.at[pl.ds(0, 7)], h_in)
    own_h.wait()
    d1(1)
    weight_terms(0)
    scatter(0)
    a = gacc[:, :HD] + gacc[:, HD:]
    gs1[...] = jnp.concatenate(
        [jnp.sum(a.T, axis=0, keepdims=True), kacc[...], jnp.zeros((6, HD), F32)], axis=0
    )
    g1_in, g2_in = net.incoming(), net.incoming()
    out = net.outgoing(gr1.at[pl.ds(0, 7)])
    for zc, cc in zgroup:
        net.go(gs1, gr1.at[mine], p.at(z=zc, c=cc), out, g1_in)
    gr1[mine] = gs1[...]
    weight_terms(1)
    scatter(1)
    d1(2)
    d1(3, 0)
    d1(3, 1)
    weight_terms(2)
    scatter(2)
    net.arrived(gr1.at[pl.ds(0, 7)], g1_in)
    gs2[...] = jnp.sum(gr1[...], axis=0)
    out = net.outgoing(gr2.at[pl.ds(0, 15)])
    for o, dev in peers:
        net.go(gs2, gr2.at[me16], dev, out, g2_in)
    gr2[me16] = gs2[...]
    weight_terms(3)
    scatter(3)

    net.arrived(wbuf.at[pl.ds(0, 7), pl.ds(0, 4)], w_in_sib)
    tokens = pl.ds(pl.multiple_of(c * TOK, TOK), TOK)
    gkv = jnp.concatenate([gb[t, g, z, tokens, :] for t in range(2) for g in range(KVH)], axis=1)
    for f in range(8):
        wv = jnp.concatenate([wbuf[f, j] for j in range(8)], axis=1)
        ghv[:, f * ROWS:(f + 1) * ROWS] = lax.dot_general(
            gkv, wv, NT, preferred_element_type=F32
        ).astype(BF)
    cp = pltpu.make_async_copy(ghv, gh, loc.at[8])
    cp.start()
    outs.append(cp)
    collect(0)
    collect(1)
    collect(2)
    net.arrived(gr2.at[pl.ds(0, 15)], g2_in)
    gsum[...] = jnp.sum(gr2[...], axis=0)
    collect(3)
    for n, (a, b) in enumerate(((gw, gw_out), (gsum.at[pl.ds(0, 1)], qgo), (gsum.at[pl.ds(1, 1)], kgo))):
        cp = pltpu.make_async_copy(a, b, loc.at[9 + n])
        cp.start()
        outs.append(cp)
    net.drain()
    for cp in outs:
        cp.wait()
    assert net.sends <= NSEND and net.recvs <= NRECV


def finish_kernel(*refs):
    n = (len(refs) - 2) // 3
    ins, outs, held = refs[:n], refs[n:2 * n], refs[2 * n:3 * n]
    sem_in, sem_out = refs[3 * n:]
    jobs = []
    for a, b, h in zip(ins, outs, held):
        parts = 4 if a.shape[0] == TOK else 1
        width = a.shape[1] // parts
        for i in range(parts):
            at = (slice(None), pl.ds(i * width, width))
            j = len(jobs)
            jobs.append((
                pltpu.make_async_copy(a.at[at], h.at[at], sem_in.at[j]),
                pltpu.make_async_copy(h.at[at], b.at[at], sem_out.at[j]),
            ))
    for load, _ in jobs:
        load.start()
    for load, store in jobs:
        load.wait()
        store.start()
    for _, store in jobs:
        store.wait()


def shards(hidden, queries, doc_ids, kv_weight, q_gain, k_gain, grad_out):
    hbm = pl.BlockSpec(memory_space=pl.ANY)
    sds = jax.ShapeDtypeStruct
    vmem = pltpu.VMEM
    wide = 32 * HD
    att, dq, gh, gw, qgo, kgo = pl.pallas_call(
        mega_kernel,
        out_shape=(
            sds((TOK, wide), BF),
            sds((TOK, wide), BF),
            sds((TOK, D), BF),
            sds((20, 1024), BF),
            sds((1, HD), F32),
            sds((1, HD), F32),
        ),
        in_specs=[hbm] * 7,
        out_specs=(hbm,) * 6,
        scratch_shapes=[
            vmem((16, TOK), jnp.int32),
            vmem((1, HD), F32),
            vmem((1, HD), F32),
            vmem((20, 1024), BF),
            vmem((8, HD), F32),
            vmem((8, 8, ROWS, 128), BF),
            vmem((2, TOK, D), BF),
            vmem((D, TOK), F32),
            vmem((8, ROWS, TOK), BF),
            vmem((8, ROWS, TOK), BF),
            vmem((2, KVH, 5 * UNIT, HD), BF),
            vmem((KVH, UNIT, HD), F32),
            vmem((TOK, wide), BF),
            vmem((TOK, wide), BF),
            vmem((HD, wide), F32),
            vmem((8, wide), F32),
            vmem((HD, wide), F32),
            vmem((KVH, HD, GROUP * TOK), BF),
            vmem((HD, GROUP * TOK), BF),
            vmem((WROWS, GROUP * TOK), BF),
            vmem((WROWS, GROUP * TOK), BF),
            vmem((WROWS, TOK), F32),
            vmem((TOK, wide), BF),
            vmem((TOK, wide), BF),
            vmem((TOK, D), BF),
            vmem((2, KVH, 5 * UNIT, HD), BF),
            vmem((KVH, 5 * UNIT, HD), BF),
            vmem((KVH, 3, UNIT, HD), BF),
            vmem((KVH, UNIT, HD), BF),
            vmem((UNIT, HD), F32),
            vmem((2, KVH, 4, UNIT, HD), BF),
            vmem((ROWS, 2 * HD), F32),
            vmem((16, 192, HD), F32),
            vmem((16, 192, HD), BF),
            vmem((16, 192, HD), BF),
            vmem((192, HD), F32),
            vmem((HD, 256), F32),
            vmem((1, HD), F32),
            vmem((8, HD), F32),
            vmem((8, 8, HD), F32),
            vmem((8, HD), F32),
            vmem((16, 8, HD), F32),
            pltpu.SemaphoreType.DMA((NSEND,)),
            pltpu.SemaphoreType.DMA((NRECV,)),
            pltpu.SemaphoreType.DMA((15,)),
        ],
        compiler_params=pltpu.CompilerParams(
            collective_id=0, has_side_effects=True, vmem_limit_bytes=60 * 1024 * 1024
        ),
        name="mega",
    )(
        kv_weight, hidden[0], queries[0], grad_out[0], doc_ids[0].reshape(16, TOK),
        q_gain.reshape(1, HD), k_gain.reshape(1, HD),
    )
    results = (att, dq, gh, gw, qgo, kgo)
    att, dq, gh, gw, qgo, kgo = pl.pallas_call(
        finish_kernel,
        out_shape=tuple(sds(r.shape, r.dtype) for r in results),
        in_specs=[hbm] * 6,
        out_specs=(hbm,) * 6,
        scratch_shapes=[vmem(r.shape, r.dtype) for r in results]
        + [pltpu.SemaphoreType.DMA((15,))] * 2,
        compiler_params=pltpu.CompilerParams(vmem_limit_bytes=60 * 1024 * 1024),
        name="finish",
    )(*results)
    return (att[None], dq[None], gh[None], gw, qgo.reshape(HD), kgo.reshape(HD))


def solution(mesh):
    return jax.shard_map(
        shards,
        mesh=mesh,
        in_specs=(
            P("fsdp", "seq", None),
            P("fsdp", "seq", None),
            P("fsdp", None),
            P("fsdp", None),
            P(),
            P(),
            P("fsdp", "seq", None),
        ),
        out_specs=(
            P("fsdp", "seq", None),
            P("fsdp", "seq", None),
            P("fsdp", "seq", None),
            P(("seq", "fsdp"), None),
            P(),
            P(),
        ),
        check_vma=False,
    )
```

```python
import math

import jax
import jax.numpy as jnp
from jax import lax
from jax.experimental import pallas as pl
from jax.experimental.pallas import tpu as pltpu
from jax.sharding import PartitionSpec as P

MESH = pl.DeviceIdType.MESH
BF = jnp.bfloat16
F32 = jnp.float32
EPS = 1e-06
TOK = 128
HD = 128
KVH = 4
GROUP = 8
D = 2560
ROWS = 320
WIN = 9
SCALE = 1.0 / math.sqrt(HD)
LOG2E = 1.4426950408889634
NT = (((1,), (1,)), ((), ()))


class Place:
    def __init__(self):
        s = lax.axis_index("seq")
        f = lax.axis_index("fsdp")
        self.s, self.f = s, f
        self.c = lax.rem(s, 2)
        self.x = lax.rem(lax.div(s, 2), 4)
        self.yl = lax.div(s, 8)
        self.yh = lax.div(f, 4)
        self.z = lax.rem(f, 4)
        self.k = lax.div(s, 2)

    def at(self, x=None, yl=None, yh=None, z=None, c=None):
        x = self.x if x is None else x
        yl = self.yl if yl is None else yl
        yh = self.yh if yh is None else yh
        z = self.z if z is None else z
        c = self.c if c is None else c
        return ((yl * 4 + x) * 2 + c, yh * 4 + z)

    def xs(self, d):
        return lax.rem(self.x + d, 4)

    def zs(self, d):
        return lax.rem(self.z + d, 4)


class Net:
    def __init__(self, send, recv, dev):
        self.send, self.recv, self.dev = send, recv, dev
        self.sends, self.recvs, self.drains = 0, 0, []

    def outgoing(self, whole, cond=None):
        sem = self.send.at[self.sends]
        self.sends += 1
        self.drains.append((sem, whole, cond))
        return sem

    def incoming(self):
        self.recvs += 1
        return self.recv.at[self.recvs - 1]

    def copy(self, src, dst, dev, out, into):
        return pltpu.make_async_remote_copy(
            src_ref=src,
            dst_ref=dst,
            send_sem=out,
            recv_sem=into,
            device_id=dev,
            device_id_type=MESH,
        )

    def go(self, src, dst, dev, out, into, cond=None):
        when(cond, self.copy(src, dst, dev, out, into).start)

    def arrived(self, whole, into, cond=None):
        when(cond, self.copy(whole, whole, self.dev, self.send.at[0], into).wait_recv)

    def drain(self):
        for sem, whole, cond in self.drains:
            when(cond, self.copy(whole, whole, self.dev, sem, self.recv.at[0]).wait_send)


def when(cond, fn):
    if cond is None:
        fn()
    else:
        pl.when(cond)(fn)


def greet(partners):
    barrier = pltpu.get_barrier_semaphore()
    for dev in partners:
        pl.semaphore_signal(barrier, inc=1, device_id=dev, device_id_type=MESH)
    pl.semaphore_wait(barrier, len(partners))


def piece_start(i, c, z):
    return ((i // 8) * 8 + ((i // 2) % 4) * 2 + c) * 160 + ((i % 2) * 4 + z) * 20


NSEND = 24
NRECV = 88
WROWS = WIN * TOK
STEP = 4
UNIT = 2 * TOK
CUTS = tuple(pl.ds(g * 48, 48) for g in range(KVH))


def mega_kernel(
    w, hid, q, do, docs_in, qg_in, kg_in,
    att, dq, gh, gw_out, qgo, kgo,
    docs, qg, kg, gw, gsum,
    wbuf, hidv, hT, hpk, hb, kv, kraw, qv, dov, xh, rq, doT, qn, dos, w_s, ds_s, mask,
    attv, dqv, ghv, part, sb, xr, yr, t0, gb, gf, st, rbs, rbr, stf, gacc, kacc, gs1, gr1, gs2, gr2,
    send, recv, loc,
):
    p = Place()
    net = Net(send, recv, p.at(c=1 - p.c))
    c, x, z, k = p.c, p.x, p.z, p.k
    row1 = p.yl == 1
    sib = p.at(c=1 - c)
    near = p.at(yl=1 - p.yl)
    far = p.at(yh=1 - p.yh, yl=1 - p.yl)
    xd = [None] + [p.at(x=p.xs(d)) for d in (1, 2, 3)]
    zd = [None] + [p.at(z=p.zs(d)) for d in (1, 2, 3)]
    fard = [None] + [p.at(yh=1 - p.yh, yl=1 - p.yl, z=p.zs(d)) for d in (1, 2, 3)]
    zgroup = [(p.zs(d), lax.rem(c + e, 2)) for d in range(4) for e in range(2)][1:]
    me16 = (p.yl * 4 + x) * 2 + p.yh
    peers = []
    for i in range(1, 16):
        o = lax.rem(me16 + i, 16)
        peers.append((o, p.at(x=lax.rem(lax.div(o, 2), 4), yl=lax.div(o, 8), yh=lax.rem(o, 2))))
    cj = c * 4
    home, away = p.yh * 4, (1 - p.yh) * 4

    own = pl.ds(cj, 4)
    loads = []
    for n in range(8):
        j = lax.rem(cj + n, 8)
        cols = pl.ds(pl.multiple_of(j * 128, 128), 128)
        loads.append(pltpu.make_async_copy(w.at[:, cols], wbuf.at[p.f, j], loc.at[n]))
    loads.append(pltpu.make_async_copy(hid, hidv.at[c], loc.at[8]))
    loads.append(pltpu.make_async_copy(q, qv, loc.at[9]))
    loads.append(pltpu.make_async_copy(do, dov, loc.at[10]))
    for n, (a, b) in enumerate(((docs_in, docs), (qg_in, qg), (kg_in, kg))):
        loads.append(pltpu.make_async_copy(a, b, loc.at[12 + n]))
    for l in loads:
        l.start()
    for m in range(1, 5):
        @pl.when(k < m)
        def _():
            kv[c, :, pl.ds((4 - m) * UNIT, UNIT), :] = jnp.zeros((KVH, UNIT, HD), BF)
    greet([p.at(z=zz, c=cc) for zz, cc in zgroup] + [d for _, d in peers] + fard[1:])
    for l in loads[:4]:
        l.wait()

    half, fourth = ROWS // 2, ROWS // 4
    mine4 = pl.multiple_of(x * fourth, 16)
    w_out = net.outgoing(wbuf.at[pl.ds(0, 7), pl.ds(0, 4)])
    in_zp, in_zm, in_quarter, in_direct, in_relayed = (
        [net.incoming() for _ in range(KVH)] for _ in range(5)
    )

    def wcopy(f, j, lo, n, dev, into):
        ref = wbuf.at[f, j, pl.ds(lo, n)]
        net.go(ref, ref, dev, w_out, into)

    def push(g):
        j = cj + g
        for d in (1, 2, 3):
            wcopy(p.f, j, mine4, fourth, fard[d], in_quarter[g])
        wcopy(p.f, j, 0, half, zd[1], in_zp[g])
        wcopy(p.f, j, half, half, zd[3], in_zm[g])
        wcopy(p.f, j, 0, ROWS, far, in_direct[g])
        wcopy(p.f, j, half, half, zd[1], in_direct[g])
        wcopy(p.f, j, 0, half, zd[3], in_direct[g])

    def count(rows):
        return part.at[0, 0, pl.ds(0, rows)]

    def relay(g):
        j = cj + g
        net.arrived(count(half), in_zp[g])
        wcopy(home + p.zs(3), j, 0, half, zd[1], in_relayed[g])
        net.arrived(count(half), in_zm[g])
        wcopy(home + p.zs(1), j, half, half, zd[3], in_relayed[g])
        net.arrived(count(3 * fourth), in_quarter[g])
        for d in (1, 3, 2):
            for e in (1, 3, 2):
                wcopy(away + p.zs(4 - d), j, mine4, fourth, xd[e], in_relayed[g])

    push(0)
    loads[8].wait()
    hs_in = net.incoming()
    net.go(hidv.at[c], hidv.at[c], sib, net.outgoing(hidv.at[c]), hs_in)
    push(1)
    for l in loads[4:8] + loads[11:]:
        l.wait()

    gain = jnp.broadcast_to(qg[...], (HD, HD)).T

    def prep(g):
        for h in range(g * GROUP, (g + 1) * GROUP):
            cols = slice(h * HD, (h + 1) * HD)
            t = qv[:, cols].astype(F32).T
            r = lax.rsqrt(jnp.mean(t * t, axis=0, keepdims=True) + EPS)
            xhat = t * r
            xh[:, cols] = xhat
            rq[:, cols] = jnp.broadcast_to(r, (8, HD))
            qn[g, :, (h % GROUP) * HD:(h % GROUP + 1) * HD] = (xhat * gain).astype(BF)
            doT[:, cols] = dov[:, cols].astype(F32).T

    loads[9].wait()
    loads[10].wait()
    prep(0)
    relay(0)
    push(2)
    prep(1)
    relay(1)
    push(3)
    prep(2)

    def window_mask():
        qd = docs[pl.ds(p.s, 1), :].astype(F32)
        tri = (
            lax.broadcasted_iota(jnp.int32, (TOK, TOK), 0)
            <= lax.broadcasted_iota(jnp.int32, (TOK, TOK), 1)
        )
        for d in range(WIN):
            kd = docs[pl.ds(jnp.maximum(p.s - d, 0), 1), :].astype(F32)
            kd = jnp.broadcast_to(kd, (TOK, TOK)).T
            live = jnp.where((kd == qd) & (p.s >= d), 1.0, 0.0)
            if d == 0:
                live = jnp.where(tri, live, 0.0)
            mask[pl.ds((WIN - 1 - d) * TOK, TOK), :] = live

    def clear():
        gacc[...] = jnp.zeros_like(gacc)
        kacc[...] = jnp.zeros_like(kacc)
        st[...] = jnp.zeros_like(st)
        for g in range(KVH):
            for t in range(2):
                part[t, g, pl.ds(pl.multiple_of((1 - c) * WROWS, TOK), TOK), :] = jnp.zeros((TOK, HD), BF)

    mine = z * 2 + c
    h_in = net.incoming()
    own_h = pltpu.make_async_copy(hpk.at[mine], hb.at[mine], loc.at[11])

    def exchange_hidden():
        for b in range(D // 128):
            hT[pl.ds(b * 128, 128), :] = hidv[c, :, b * 128:(b + 1) * 128].astype(F32).T
        for zc in range(4):
            for cc in range(2):
                for i in range(16):
                    hpk[zc * 2 + cc, pl.ds(i * 20, 20), :] = hT[pl.ds(piece_start(i, cc, zc), 20), :].astype(BF)
        out = net.outgoing(hpk.at[pl.ds(0, 7)])
        for zc, cc in zgroup:
            net.go(hpk.at[zc * 2 + cc], hb.at[mine], p.at(z=zc, c=cc), out, h_in)
        own_h.start()

    home_rows = pl.ds(4 * UNIT, UNIT)

    def unit(m):
        return pl.ds((4 - m) * UNIT, UNIT)

    four = kv.at[c, :, pl.ds(0, UNIT)]
    one = kv.at[c, 0, pl.ds(0, UNIT)]
    y_out = net.outgoing(four, p.yl == 0)
    x_out = [None] + [net.outgoing(four, row1 | (x + m <= 3)) for m in (1, 2, 3)]
    b_out = net.outgoing(kv.at[c])
    y_in = [net.incoming() for _ in range(KVH)]
    x_in = [[None] + [net.incoming() for _ in range(3)] for _ in range(KVH)]
    b_in = [net.incoming() for _ in range(KVH)]

    def along_x(g, m, src, cond):
        net.go(kv.at[c, g, src], kv.at[c, g, unit(m)], xd[m], x_out[m], x_in[g][m], cond)


    def project(g):
        if g == 0:
            net.arrived(hidv.at[c], hs_in)
        net.arrived(count(2 * ROWS), in_direct[g])
        net.arrived(count(ROWS + 9 * fourth), in_relayed[g])
        lhs = jnp.concatenate([hidv[0], hidv[1]], axis=0)
        raw = jnp.dot(lhs, wbuf[:, cj + g].reshape(D, 128), preferred_element_type=F32)

        @pl.when(c == 0)
        def _():
            kraw[g] = raw
            r = lax.rsqrt(jnp.mean(raw * raw, axis=1, keepdims=True) + EPS)
            kv[0, g, home_rows, :] = (raw * r * kg[...]).astype(BF)

        @pl.when(c == 1)
        def _():
            kv[1, g, home_rows, :] = raw.astype(BF)

        net.go(kv.at[c, g, unit(0)], kv.at[c, g, unit(4)], near, y_out, y_in[g], p.yl == 0)
        for m in (1, 2, 3):
            along_x(g, m, unit(0), x + m <= 3)

    def spread(g):
        net.arrived(one, y_in[g], row1)
        for m in (1, 2, 3):
            along_x(g, m, unit(4), row1 & (x + m > 3))

    def share(g):
        for m in (1, 2, 3):
            net.arrived(one, x_in[g][m], k >= m)
        net.go(kv.at[c, g], kv.at[c, g], sib, b_out, b_in[g])

    span = pl.ds(pl.multiple_of(c * TOK, TOK), WROWS)

    def open_head(g):
        net.arrived(kv.at[c, g], b_in[g])
        ka = kv[0, g, span, :]
        va = kv[1, g, span, :]
        return ka, va, ka.astype(F32).T.astype(BF), va.astype(F32).T.astype(BF)

    wide_gain = jnp.concatenate([gain] * STEP, axis=1)

    def attend(g, pair, head):
        ka, va, kT, vT = head
        lo = pair * STEP * HD
        cols = slice(lo, lo + STEP * HD)
        full = slice(g * 1024 + lo, g * 1024 + lo + STEP * HD)
        scores = jnp.dot(ka, qn[g, :, cols], preferred_element_type=F32)
        m = mask[...]
        e = jnp.exp2(scores * (SCALE * LOG2E)) * jnp.concatenate([m] * STEP, axis=1)
        total = jnp.sum(e, axis=0, keepdims=True)
        wt = e.astype(BF)
        w_s[:, cols] = wt
        inv = 1.0 / total
        d_out = doT[:, full]
        attT = (jnp.dot(vT, wt, preferred_element_type=F32) * inv).astype(BF).astype(F32)
        delta = jnp.sum(d_out * attT, axis=0, keepdims=True) * inv
        dsc = (d_out * inv).astype(BF)
        dos[:, cols] = dsc
        dp = jnp.dot(va, dsc, preferred_element_type=F32)
        ds = (e * (dp - delta)).astype(BF)
        ds_s[:, cols] = ds
        dy = jnp.dot(kT, ds, preferred_element_type=F32) * SCALE
        xhat = xh[:, full]
        r = rq[0:1, full]
        gacc[...] += dy * xhat
        dxh = dy * wide_gain
        dx = r * (dxh - xhat * jnp.mean(xhat * dxh, axis=0, keepdims=True))
        for n in range(STEP):
            at = slice(g * 1024 + lo + n * HD, g * 1024 + lo + (n + 1) * HD)
            attv[:, at] = attT[:, n * HD:(n + 1) * HD].T.astype(BF)
            dqv[:, at] = dx[:, n * HD:(n + 1) * HD].T.astype(BF)

    outs = []

    def close_head(g):
        dvv = lax.dot_general(w_s[...], dos[...], NT, preferred_element_type=F32)
        part[1, g, span, :] = dvv.astype(BF)
        dkk = lax.dot_general(ds_s[...], qn[g], NT, preferred_element_type=F32) * SCALE
        part[0, g, span, :] = dkk.astype(BF)
        cols = pl.ds(g * 1024, 1024)
        for n, (a, b) in enumerate(((attv, att), (dqv, dq))):
            cp = pltpu.make_async_copy(a.at[:, cols], b.at[:, cols], loc.at[g * 2 + n])
            cp.start()
            outs.append(cp)

    s_out, w_out2 = net.outgoing(part.at[1 - c]), net.outgoing(gb.at[c])
    u_out = [None] + [net.outgoing(four, k >= m) for m in (1, 2, 3)]
    v_out = net.outgoing(four, row1)
    z_out = net.outgoing(gb.at[c, :, pl.ds(0, 3)])
    s_in = [net.incoming() for _ in range(KVH)]
    pieces = [(g, h) for g in range(KVH) for h in ((None,) if g < KVH - 1 else (0, 1))]
    v_in, z_in, w_in = ({key: net.incoming() for key in pieces} for _ in range(3))
    u_in = {(g, h, m): net.incoming() for g, h in pieces for m in (1, 2, 3)}

    def part_of(h, start=0):
        return pl.ds(start, UNIT) if h is None else pl.ds(start + h * TOK, TOK)

    def unit_of(m, h):
        return part_of(h, (4 - m) * UNIT)

    def c1(g):
        net.go(part.at[1 - c, g], sb.at[g], sib, s_out, s_in[g])

    def c2(g):
        net.arrived(sb.at[g], s_in[g])
        part[c, g] = (part[c, g].astype(F32) + sb[g].astype(F32)).astype(BF)
        for h in [h for gg, h in pieces if gg == g]:
            for m in (1, 2, 3):
                net.go(
                    part.at[c, g, unit_of(m, h)], xr.at[g, m - 1, part_of(h)], xd[4 - m],
                    u_out[m], u_in[g, h, m], k >= m,
                )

    def c3(g, h=None):
        rows = part_of(h)
        t0[rows] = part[c, g, unit_of(0, h), :].astype(F32)
        for m in (1, 2, 3):
            @pl.when(x + m <= 3)
            def _():
                net.arrived(xr.at[g, m - 1, rows], u_in[g, h, m])
                t0[rows] += xr[g, m - 1, rows].astype(F32)

            @pl.when((x + m > 3) & row1)
            def _():
                net.arrived(xr.at[g, m - 1, rows], u_in[g, h, m])
                part[c, g, unit_of(4, h), :] = (
                    part[c, g, unit_of(4, h), :].astype(F32) + xr[g, m - 1, rows].astype(F32)
                ).astype(BF)

        net.go(part.at[c, g, unit_of(4, h)], yr.at[g, rows], near, v_out, v_in[g, h], row1)
        part[c, g, unit_of(0, h), :] = t0[rows].astype(BF)

    def c4(g, h=None):
        rows = part_of(h)
        t0[rows] = part[c, g, unit_of(0, h), :].astype(F32)

        @pl.when(p.yl == 0)
        def _():
            net.arrived(yr.at[g, rows], v_in[g, h])
            t0[rows] += yr[g, rows].astype(F32)

        @pl.when(c == 0)
        def _():
            raw = kraw[g, rows]
            r = lax.rsqrt(jnp.mean(raw * raw, axis=1, keepdims=True) + EPS)
            xhat = raw * r
            dy = t0[rows]
            kacc[...] += jnp.sum(dy * xhat, axis=0, keepdims=True)
            dxh = dy * kg[...]
            dx = r * (dxh - xhat * jnp.mean(xhat * dxh, axis=1, keepdims=True))
            gb[0, g, z, rows] = dx.astype(BF)

        @pl.when(c == 1)
        def _():
            gb[1, g, z, rows] = t0[rows].astype(BF)

        ref = gb.at[c, g, z, rows]
        for d in (1, 3, 2):
            net.go(ref, ref, zd[d], z_out, z_in[g, h])

    def d1(g, h=None):
        rows = part_of(h)
        net.arrived(gb.at[c, g, pl.ds(0, 3), rows], z_in[g, h])
        ref = gb.at[c, g, :, rows]
        net.go(ref, ref, sib, w_out2, w_in[g, h])

    def offset(g, t):
        return g * 48 + t * 20

    def weight_terms(g):
        for gg, h in pieces:
            if gg == g:
                net.arrived(gb.at[c, g, :, part_of(h)], w_in[g, h])
        lhs = jnp.concatenate([hb[i] for i in range(8)], axis=1)
        rhs = jnp.concatenate([gb[0, g].reshape(8 * TOK, HD), gb[1, g].reshape(8 * TOK, HD)], axis=1)
        gf[...] = jnp.dot(lhs, rhs, preferred_element_type=F32)
        for i in range(16):
            for t in range(2):
                st[i, pl.ds(offset(g, t), 20), :] = gf[pl.ds(i * 20, 20), t * HD:(t + 1) * HD]

    r_in = [net.incoming() for _ in CUTS]

    def scatter(n):
        rows = CUTS[n]
        for i in range(16):
            rbs[i, rows] = st[i, rows].astype(BF)
        out = net.outgoing(rbs.at[pl.ds(0, 15), rows])
        for o, dev in peers:
            net.go(rbs.at[o, rows], rbr.at[me16, rows], dev, out, r_in[n])
        rbr[me16, rows] = rbs[me16, rows]

    def collect(n):
        rows = CUTS[n]
        net.arrived(rbr.at[pl.ds(0, 15), rows], r_in[n])
        total = rbr[0, rows].astype(F32)
        for i in range(1, 16):
            total = total + rbr[i, rows].astype(F32)
        stf[rows] = total
        for t in range(2):
            at = (t * 4 + n) * HD
            gw[:, at:at + HD] = stf[pl.ds(offset(n, t), 20), :].astype(BF)

    w_in_sib = net.incoming()

    share_out = net.outgoing(wbuf.at[pl.ds(0, 7), pl.ds(0, 4)])

    def weight_share(n):
        for f in (home + p.zs(1), home + p.zs(2), home + p.zs(3), away, away + 1, away + 2, away + 3):
            ref = wbuf.at[f, cj + n]
            net.go(ref, ref, sib, share_out, w_in_sib)

    project(0)
    relay(2)
    prep(3)
    project(1)
    spread(0)
    relay(3)
    window_mask()
    clear()
    project(2)
    spread(1)
    share(0)
    exchange_hidden()
    project(3)

    todo = {
        0: [lambda: spread(2), lambda: share(1), lambda: spread(3)],
        1: [lambda: c1(0), lambda: share(2)],
        3: [lambda: c2(0), lambda: share(3), lambda: c1(1), lambda: weight_share(0)],
        5: [lambda: c2(1), lambda: c1(2), lambda: weight_share(1), lambda: weight_share(2)],
        6: [lambda: c3(0), lambda: weight_share(3)],
        7: [lambda: c1(3), lambda: c2(2)],
    }
    for g in range(KVH):
        head = open_head(g)
        for pair in range(GROUP // STEP):
            attend(g, pair, head)
            if pair == GROUP // STEP - 1:
                close_head(g)
            for fn in todo.get(g * (GROUP // STEP) + pair, ()):
                fn()

    c3(1)
    c2(3)
    c4(0)
    c4(1)
    c3(2)
    c3(3, 0)
    c3(3, 1)
    c4(2)
    d1(0)
    c4(3, 0)
    c4(3, 1)
    net.arrived(hpk.at[pl.ds(0, 7)], h_in)
    own_h.wait()
    d1(1)
    weight_terms(0)
    scatter(0)
    a = sum(gacc[:, n * HD:(n + 1) * HD] for n in range(STEP))
    gs1[...] = jnp.concatenate(
        [jnp.sum(a.T, axis=0, keepdims=True), kacc[...], jnp.zeros((6, HD), F32)], axis=0
    )
    g1_in, g2_in = net.incoming(), net.incoming()
    out = net.outgoing(gr1.at[pl.ds(0, 7)])
    for zc, cc in zgroup:
        net.go(gs1, gr1.at[mine], p.at(z=zc, c=cc), out, g1_in)
    gr1[mine] = gs1[...]
    weight_terms(1)
    scatter(1)
    d1(2)
    d1(3, 0)
    d1(3, 1)
    weight_terms(2)
    scatter(2)
    net.arrived(gr1.at[pl.ds(0, 7)], g1_in)
    gs2[...] = jnp.sum(gr1[...], axis=0)
    out = net.outgoing(gr2.at[pl.ds(0, 15)])
    for o, dev in peers:
        net.go(gs2, gr2.at[me16], dev, out, g2_in)
    gr2[me16] = gs2[...]
    weight_terms(3)
    scatter(3)

    net.arrived(wbuf.at[pl.ds(0, 7), pl.ds(0, 4)], w_in_sib)
    tokens = pl.ds(pl.multiple_of(c * TOK, TOK), TOK)
    gkv = jnp.concatenate([gb[t, g, z, tokens, :] for t in range(2) for g in range(KVH)], axis=1)
    for f in range(8):
        wv = jnp.concatenate([wbuf[f, j] for j in range(8)], axis=1)
        ghv[:, f * ROWS:(f + 1) * ROWS] = lax.dot_general(
            gkv, wv, NT, preferred_element_type=F32
        ).astype(BF)
    cp = pltpu.make_async_copy(ghv, gh, loc.at[8])
    cp.start()
    outs.append(cp)
    collect(0)
    collect(1)
    collect(2)
    net.arrived(gr2.at[pl.ds(0, 15)], g2_in)
    gsum[...] = jnp.sum(gr2[...], axis=0)
    collect(3)
    for n, (a, b) in enumerate(((gw, gw_out), (gsum.at[pl.ds(0, 1)], qgo), (gsum.at[pl.ds(1, 1)], kgo))):
        cp = pltpu.make_async_copy(a, b, loc.at[9 + n])
        cp.start()
        outs.append(cp)
    net.drain()
    for cp in outs:
        cp.wait()
    assert net.sends <= NSEND and net.recvs <= NRECV


def finish_kernel(*refs):
    n = (len(refs) - 2) // 3
    ins, outs, held = refs[:n], refs[n:2 * n], refs[2 * n:3 * n]
    sem_in, sem_out = refs[3 * n:]
    jobs = []
    for a, b, h in zip(ins, outs, held):
        parts = 4 if a.shape[0] == TOK else 1
        width = a.shape[1] // parts
        for i in range(parts):
            at = (slice(None), pl.ds(i * width, width))
            j = len(jobs)
            jobs.append((
                pltpu.make_async_copy(a.at[at], h.at[at], sem_in.at[j]),
                pltpu.make_async_copy(h.at[at], b.at[at], sem_out.at[j]),
            ))
    for load, _ in jobs:
        load.start()
    for load, store in jobs:
        load.wait()
        store.start()
    for _, store in jobs:
        store.wait()


def shards(hidden, queries, doc_ids, kv_weight, q_gain, k_gain, grad_out):
    hbm = pl.BlockSpec(memory_space=pl.ANY)
    sds = jax.ShapeDtypeStruct
    vmem = pltpu.VMEM
    wide = 32 * HD
    att, dq, gh, gw, qgo, kgo = pl.pallas_call(
        mega_kernel,
        out_shape=(
            sds((TOK, wide), BF),
            sds((TOK, wide), BF),
            sds((TOK, D), BF),
            sds((20, 1024), BF),
            sds((1, HD), F32),
            sds((1, HD), F32),
        ),
        in_specs=[hbm] * 7,
        out_specs=(hbm,) * 6,
        scratch_shapes=[
            vmem((16, TOK), jnp.int32),
            vmem((1, HD), F32),
            vmem((1, HD), F32),
            vmem((20, 1024), BF),
            vmem((8, HD), F32),
            vmem((8, 8, ROWS, 128), BF),
            vmem((2, TOK, D), BF),
            vmem((D, TOK), F32),
            vmem((8, ROWS, TOK), BF),
            vmem((8, ROWS, TOK), BF),
            vmem((2, KVH, 5 * UNIT, HD), BF),
            vmem((KVH, UNIT, HD), F32),
            vmem((TOK, wide), BF),
            vmem((TOK, wide), BF),
            vmem((HD, wide), F32),
            vmem((8, wide), F32),
            vmem((HD, wide), F32),
            vmem((KVH, HD, GROUP * TOK), BF),
            vmem((HD, GROUP * TOK), BF),
            vmem((WROWS, GROUP * TOK), BF),
            vmem((WROWS, GROUP * TOK), BF),
            vmem((WROWS, TOK), F32),
            vmem((TOK, wide), BF),
            vmem((TOK, wide), BF),
            vmem((TOK, D), BF),
            vmem((2, KVH, 5 * UNIT, HD), BF),
            vmem((KVH, 5 * UNIT, HD), BF),
            vmem((KVH, 3, UNIT, HD), BF),
            vmem((KVH, UNIT, HD), BF),
            vmem((UNIT, HD), F32),
            vmem((2, KVH, 4, UNIT, HD), BF),
            vmem((ROWS, 2 * HD), F32),
            vmem((16, 192, HD), F32),
            vmem((16, 192, HD), BF),
            vmem((16, 192, HD), BF),
            vmem((192, HD), F32),
            vmem((HD, STEP * HD), F32),
            vmem((1, HD), F32),
            vmem((8, HD), F32),
            vmem((8, 8, HD), F32),
            vmem((8, HD), F32),
            vmem((16, 8, HD), F32),
            pltpu.SemaphoreType.DMA((NSEND,)),
            pltpu.SemaphoreType.DMA((NRECV,)),
            pltpu.SemaphoreType.DMA((15,)),
        ],
        compiler_params=pltpu.CompilerParams(
            collective_id=0, has_side_effects=True, vmem_limit_bytes=60 * 1024 * 1024
        ),
        name="mega",
    )(
        kv_weight, hidden[0], queries[0], grad_out[0], doc_ids[0].reshape(16, TOK),
        q_gain.reshape(1, HD), k_gain.reshape(1, HD),
    )
    results = (att, dq, gh, gw, qgo, kgo)
    att, dq, gh, gw, qgo, kgo = pl.pallas_call(
        finish_kernel,
        out_shape=tuple(sds(r.shape, r.dtype) for r in results),
        in_specs=[hbm] * 6,
        out_specs=(hbm,) * 6,
        scratch_shapes=[vmem(r.shape, r.dtype) for r in results]
        + [pltpu.SemaphoreType.DMA((15,))] * 2,
        compiler_params=pltpu.CompilerParams(vmem_limit_bytes=60 * 1024 * 1024),
        name="finish",
    )(*results)
    return (att[None], dq[None], gh[None], gw, qgo.reshape(HD), kgo.reshape(HD))


def solution(mesh):
    return jax.shard_map(
        shards,
        mesh=mesh,
        in_specs=(
            P("fsdp", "seq", None),
            P("fsdp", "seq", None),
            P("fsdp", None),
            P("fsdp", None),
            P(),
            P(),
            P("fsdp", "seq", None),
        ),
        out_specs=(
            P("fsdp", "seq", None),
            P("fsdp", "seq", None),
            P("fsdp", "seq", None),
            P(("seq", "fsdp"), None),
            P(),
            P(),
        ),
        check_vma=False,
    )
```

```python
import math

import jax
import jax.numpy as jnp
from jax import lax
from jax.experimental import pallas as pl
from jax.experimental.pallas import tpu as pltpu
from jax.sharding import PartitionSpec as P

MESH = pl.DeviceIdType.MESH
BF = jnp.bfloat16
F32 = jnp.float32
EPS = 1e-06
TOK = 128
HD = 128
KVH = 4
GROUP = 8
D = 2560
ROWS = 320
WIN = 9
SCALE = 1.0 / math.sqrt(HD)
LOG2E = 1.4426950408889634
NT = (((1,), (1,)), ((), ()))


class Place:
    def __init__(self):
        s = lax.axis_index("seq")
        f = lax.axis_index("fsdp")
        self.s, self.f = s, f
        self.c = lax.rem(s, 2)
        self.x = lax.rem(lax.div(s, 2), 4)
        self.yl = lax.div(s, 8)
        self.yh = lax.div(f, 4)
        self.z = lax.rem(f, 4)
        self.k = lax.div(s, 2)

    def at(self, x=None, yl=None, yh=None, z=None, c=None):
        x = self.x if x is None else x
        yl = self.yl if yl is None else yl
        yh = self.yh if yh is None else yh
        z = self.z if z is None else z
        c = self.c if c is None else c
        return ((yl * 4 + x) * 2 + c, yh * 4 + z)

    def xs(self, d):
        return lax.rem(self.x + d, 4)

    def zs(self, d):
        return lax.rem(self.z + d, 4)


class Net:
    def __init__(self, send, recv, dev):
        self.send, self.recv, self.dev = send, recv, dev
        self.sends, self.recvs, self.drains = 0, 0, []

    def outgoing(self, whole, cond=None):
        sem = self.send.at[self.sends]
        self.sends += 1
        self.drains.append((sem, whole, cond))
        return sem

    def incoming(self):
        self.recvs += 1
        return self.recv.at[self.recvs - 1]

    def copy(self, src, dst, dev, out, into):
        return pltpu.make_async_remote_copy(
            src_ref=src,
            dst_ref=dst,
            send_sem=out,
            recv_sem=into,
            device_id=dev,
            device_id_type=MESH,
        )

    def go(self, src, dst, dev, out, into, cond=None):
        when(cond, self.copy(src, dst, dev, out, into).start)

    def arrived(self, whole, into, cond=None):
        when(cond, self.copy(whole, whole, self.dev, self.send.at[0], into).wait_recv)

    def drain(self):
        for sem, whole, cond in self.drains:
            when(cond, self.copy(whole, whole, self.dev, sem, self.recv.at[0]).wait_send)


def when(cond, fn):
    if cond is None:
        fn()
    else:
        pl.when(cond)(fn)


def greet(partners):
    barrier = pltpu.get_barrier_semaphore()
    for dev in partners:
        pl.semaphore_signal(barrier, inc=1, device_id=dev, device_id_type=MESH)
    pl.semaphore_wait(barrier, len(partners))


def piece_start(i, c, z):
    return ((i // 8) * 8 + ((i // 2) % 4) * 2 + c) * 160 + ((i % 2) * 4 + z) * 20


NSEND = 24
NRECV = 88
WROWS = WIN * TOK
STEP = 4
UNIT = 2 * TOK
CUTS = tuple(pl.ds(g * 48, 48) for g in range(KVH))


def mega_kernel(
    w, hid, q, do, docs_in, qg_in, kg_in,
    att, dq, gh, gw_out, qgo, kgo,
    docs, qg, kg, gw, gsum,
    wbuf, hidv, hT, hpk, hb, kv, kraw, qv, dov, xh, rq, doT, qn, dos, w_s, ds_s, mask,
    attv, dqv, ghv, part, sb, xr, yr, t0, gb, gf, st, rbs, rbr, stf, gacc, kacc, gs1, gr1, gs2, gr2,
    send, recv, loc,
):
    p = Place()
    net = Net(send, recv, p.at(c=1 - p.c))
    c, x, z, k = p.c, p.x, p.z, p.k
    row1 = p.yl == 1
    sib = p.at(c=1 - c)
    near = p.at(yl=1 - p.yl)
    far = p.at(yh=1 - p.yh, yl=1 - p.yl)
    xd = [None] + [p.at(x=p.xs(d)) for d in (1, 2, 3)]
    zd = [None] + [p.at(z=p.zs(d)) for d in (1, 2, 3)]
    fard = [None] + [p.at(yh=1 - p.yh, yl=1 - p.yl, z=p.zs(d)) for d in (1, 2, 3)]
    zgroup = [(p.zs(d), lax.rem(c + e, 2)) for d in range(4) for e in range(2)][1:]
    me16 = (p.yl * 4 + x) * 2 + p.yh
    peers = []
    for i in range(1, 16):
        o = lax.rem(me16 + i, 16)
        peers.append((o, p.at(x=lax.rem(lax.div(o, 2), 4), yl=lax.div(o, 8), yh=lax.rem(o, 2))))
    cj = c * 4
    home, away = p.yh * 4, (1 - p.yh) * 4

    own = pl.ds(cj, 4)
    loads = []
    for n in range(8):
        j = lax.rem(cj + n, 8)
        cols = pl.ds(pl.multiple_of(j * 128, 128), 128)
        loads.append(pltpu.make_async_copy(w.at[:, cols], wbuf.at[p.f, j], loc.at[n]))
    loads.append(pltpu.make_async_copy(hid, hidv.at[c], loc.at[8]))
    loads.append(pltpu.make_async_copy(q, qv, loc.at[9]))
    loads.append(pltpu.make_async_copy(do, dov, loc.at[10]))
    for n, (a, b) in enumerate(((docs_in, docs), (qg_in, qg), (kg_in, kg))):
        loads.append(pltpu.make_async_copy(a, b, loc.at[12 + n]))
    for l in loads:
        l.start()
    for m in range(1, 5):
        @pl.when(k < m)
        def _():
            kv[c, :, pl.ds((4 - m) * UNIT, UNIT), :] = jnp.zeros((KVH, UNIT, HD), BF)
    greet([p.at(z=zz, c=cc) for zz, cc in zgroup] + [d for _, d in peers] + fard[1:])
    for l in loads[:4]:
        l.wait()

    half, fourth = ROWS // 2, ROWS // 4
    mine4 = pl.multiple_of(x * fourth, 16)
    w_out = net.outgoing(wbuf.at[pl.ds(0, 7), pl.ds(0, 4)])
    in_zp, in_zm, in_quarter, in_direct, in_relayed = (
        [net.incoming() for _ in range(KVH)] for _ in range(5)
    )

    def wcopy(f, j, lo, n, dev, into):
        ref = wbuf.at[f, j, pl.ds(lo, n)]
        net.go(ref, ref, dev, w_out, into)

    def push(g):
        j = cj + g
        for d in (1, 2, 3):
            wcopy(p.f, j, mine4, fourth, fard[d], in_quarter[g])
        wcopy(p.f, j, 0, half, zd[1], in_zp[g])
        wcopy(p.f, j, half, half, zd[3], in_zm[g])
        wcopy(p.f, j, 0, ROWS, far, in_direct[g])
        wcopy(p.f, j, half, half, zd[1], in_direct[g])
        wcopy(p.f, j, 0, half, zd[3], in_direct[g])

    def count(rows):
        return part.at[0, 0, pl.ds(0, rows)]

    def relay(g):
        j = cj + g
        net.arrived(count(half), in_zp[g])
        wcopy(home + p.zs(3), j, 0, half, zd[1], in_relayed[g])
        net.arrived(count(half), in_zm[g])
        wcopy(home + p.zs(1), j, half, half, zd[3], in_relayed[g])
        net.arrived(count(3 * fourth), in_quarter[g])
        for d in (1, 3, 2):
            for e in (1, 3, 2):
                wcopy(away + p.zs(4 - d), j, mine4, fourth, xd[e], in_relayed[g])

    push(0)
    loads[8].wait()
    hs_in = net.incoming()
    net.go(hidv.at[c], hidv.at[c], sib, net.outgoing(hidv.at[c]), hs_in)
    push(1)
    for l in loads[4:8] + loads[11:]:
        l.wait()

    gain = jnp.broadcast_to(qg[...], (HD, HD)).T

    def prep(g):
        for h in range(g * GROUP, (g + 1) * GROUP):
            cols = slice(h * HD, (h + 1) * HD)
            t = qv[:, cols].astype(F32).T
            r = lax.rsqrt(jnp.mean(t * t, axis=0, keepdims=True) + EPS)
            xhat = t * r
            xh[:, cols] = xhat
            rq[:, cols] = jnp.broadcast_to(r, (8, HD))
            qn[g, :, (h % GROUP) * HD:(h % GROUP + 1) * HD] = (xhat * gain).astype(BF)
            doT[:, cols] = dov[:, cols].astype(F32).T

    loads[9].wait()
    loads[10].wait()
    prep(0)
    relay(0)
    push(2)
    prep(1)
    relay(1)
    push(3)
    prep(2)

    def window_mask():
        qd = docs[pl.ds(p.s, 1), :].astype(F32)
        tri = (
            lax.broadcasted_iota(jnp.int32, (TOK, TOK), 0)
            <= lax.broadcasted_iota(jnp.int32, (TOK, TOK), 1)
        )
        for d in range(WIN):
            kd = docs[pl.ds(jnp.maximum(p.s - d, 0), 1), :].astype(F32)
            kd = jnp.broadcast_to(kd, (TOK, TOK)).T
            live = jnp.where((kd == qd) & (p.s >= d), 1.0, 0.0)
            if d == 0:
                live = jnp.where(tri, live, 0.0)
            mask[pl.ds((WIN - 1 - d) * TOK, TOK), :] = live

    def clear():
        gacc[...] = jnp.zeros_like(gacc)
        kacc[...] = jnp.zeros_like(kacc)
        st[...] = jnp.zeros_like(st)
        for g in range(KVH):
            for t in range(2):
                part[t, g, pl.ds(pl.multiple_of((1 - c) * WROWS, TOK), TOK), :] = jnp.zeros((TOK, HD), BF)

    mine = z * 2 + c
    h_in = net.incoming()
    own_h = pltpu.make_async_copy(hpk.at[mine], hb.at[mine], loc.at[11])

    def exchange_hidden():
        for b in range(D // 128):
            hT[pl.ds(b * 128, 128), :] = hidv[c, :, b * 128:(b + 1) * 128].astype(F32).T
        for zc in range(4):
            for cc in range(2):
                for i in range(16):
                    hpk[zc * 2 + cc, pl.ds(i * 20, 20), :] = hT[pl.ds(piece_start(i, cc, zc), 20), :].astype(BF)
        out = net.outgoing(hpk.at[pl.ds(0, 7)])
        for zc, cc in zgroup:
            net.go(hpk.at[zc * 2 + cc], hb.at[mine], p.at(z=zc, c=cc), out, h_in)
        own_h.start()

    home_rows = pl.ds(4 * UNIT, UNIT)

    def unit(m):
        return pl.ds((4 - m) * UNIT, UNIT)

    four = kv.at[c, :, pl.ds(0, UNIT)]
    one = kv.at[c, 0, pl.ds(0, UNIT)]
    y_out = net.outgoing(four, p.yl == 0)
    x_out = [None] + [net.outgoing(four, row1 | (x + m <= 3)) for m in (1, 2, 3)]
    b_out = net.outgoing(kv.at[c])
    y_in = [net.incoming() for _ in range(KVH)]
    x_in = [[None] + [net.incoming() for _ in range(3)] for _ in range(KVH)]
    b_in = [net.incoming() for _ in range(KVH)]

    def along_x(g, m, src, cond):
        net.go(kv.at[c, g, src], kv.at[c, g, unit(m)], xd[m], x_out[m], x_in[g][m], cond)


    def project(g):
        if g == 0:
            net.arrived(hidv.at[c], hs_in)
        net.arrived(count(2 * ROWS), in_direct[g])
        net.arrived(count(ROWS + 9 * fourth), in_relayed[g])
        lhs = jnp.concatenate([hidv[0], hidv[1]], axis=0)
        raw = jnp.dot(lhs, wbuf[:, cj + g].reshape(D, 128), preferred_element_type=F32)

        @pl.when(c == 0)
        def _():
            kraw[g] = raw
            r = lax.rsqrt(jnp.mean(raw * raw, axis=1, keepdims=True) + EPS)
            kv[0, g, home_rows, :] = (raw * r * kg[...]).astype(BF)

        @pl.when(c == 1)
        def _():
            kv[1, g, home_rows, :] = raw.astype(BF)

        net.go(kv.at[c, g, unit(0)], kv.at[c, g, unit(4)], near, y_out, y_in[g], p.yl == 0)
        for m in (1, 2, 3):
            along_x(g, m, unit(0), x + m <= 3)

    def spread(g):
        net.arrived(one, y_in[g], row1)
        for m in (1, 2, 3):
            along_x(g, m, unit(4), row1 & (x + m > 3))

    def share(g):
        for m in (1, 2, 3):
            net.arrived(one, x_in[g][m], k >= m)
        net.go(kv.at[c, g], kv.at[c, g], sib, b_out, b_in[g])

    span = pl.ds(pl.multiple_of(c * TOK, TOK), WROWS)

    def open_head(g):
        net.arrived(kv.at[c, g], b_in[g])
        ka = kv[0, g, span, :]
        va = kv[1, g, span, :]
        return ka, va, ka.astype(F32).T.astype(BF), va.astype(F32).T.astype(BF)

    wide_gain = jnp.concatenate([gain] * STEP, axis=1)

    def attend(g, pair, head):
        ka, va, kT, vT = head
        lo = pair * STEP * HD
        cols = slice(lo, lo + STEP * HD)
        full = slice(g * 1024 + lo, g * 1024 + lo + STEP * HD)
        scores = jnp.dot(ka, qn[g, :, cols], preferred_element_type=F32)
        m = mask[...]
        e = jnp.exp2(scores * (SCALE * LOG2E)) * jnp.concatenate([m] * STEP, axis=1)
        total = jnp.sum(e, axis=0, keepdims=True)
        wt = e.astype(BF)
        w_s[:, cols] = wt
        inv = 1.0 / total
        d_out = doT[:, full]
        attT = (jnp.dot(vT, wt, preferred_element_type=F32) * inv).astype(BF).astype(F32)
        delta = jnp.sum(d_out * attT, axis=0, keepdims=True) * inv
        dsc = (d_out * inv).astype(BF)
        dos[:, cols] = dsc
        dp = jnp.dot(va, dsc, preferred_element_type=F32)
        ds = (wt.astype(F32) * (dp - delta)).astype(BF)
        ds_s[:, cols] = ds
        dy = jnp.dot(kT, ds, preferred_element_type=F32) * SCALE
        xhat = xh[:, full]
        r = rq[0:1, full]
        gacc[...] += dy * xhat
        dxh = dy * wide_gain
        dx = r * (dxh - xhat * jnp.mean(xhat * dxh, axis=0, keepdims=True))
        for n in range(STEP):
            at = slice(g * 1024 + lo + n * HD, g * 1024 + lo + (n + 1) * HD)
            attv[:, at] = attT[:, n * HD:(n + 1) * HD].T.astype(BF)
            dqv[:, at] = dx[:, n * HD:(n + 1) * HD].T.astype(BF)

    outs = []

    def close_head(g):
        dvv = lax.dot_general(w_s[...], dos[...], NT, preferred_element_type=F32)
        part[1, g, span, :] = dvv.astype(BF)
        dkk = lax.dot_general(ds_s[...], qn[g], NT, preferred_element_type=F32) * SCALE
        part[0, g, span, :] = dkk.astype(BF)
        cols = pl.ds(g * 1024, 1024)
        for n, (a, b) in enumerate(((attv, att), (dqv, dq))):
            cp = pltpu.make_async_copy(a.at[:, cols], b.at[:, cols], loc.at[g * 2 + n])
            cp.start()
            outs.append(cp)

    s_out, w_out2 = net.outgoing(part.at[1 - c]), net.outgoing(gb.at[c])
    u_out = [None] + [net.outgoing(four, k >= m) for m in (1, 2, 3)]
    v_out = net.outgoing(four, row1)
    z_out = net.outgoing(gb.at[c, :, pl.ds(0, 3)])
    s_in = [net.incoming() for _ in range(KVH)]
    pieces = [(g, h) for g in range(KVH) for h in ((None,) if g < KVH - 1 else (0, 1))]
    v_in, z_in, w_in = ({key: net.incoming() for key in pieces} for _ in range(3))
    u_in = {(g, h, m): net.incoming() for g, h in pieces for m in (1, 2, 3)}

    def part_of(h, start=0):
        return pl.ds(start, UNIT) if h is None else pl.ds(start + h * TOK, TOK)

    def unit_of(m, h):
        return part_of(h, (4 - m) * UNIT)

    def c1(g):
        net.go(part.at[1 - c, g], sb.at[g], sib, s_out, s_in[g])

    def c2(g):
        net.arrived(sb.at[g], s_in[g])
        part[c, g] = (part[c, g].astype(F32) + sb[g].astype(F32)).astype(BF)
        for h in [h for gg, h in pieces if gg == g]:
            for m in (1, 2, 3):
                net.go(
                    part.at[c, g, unit_of(m, h)], xr.at[g, m - 1, part_of(h)], xd[4 - m],
                    u_out[m], u_in[g, h, m], k >= m,
                )

    def c3(g, h=None):
        rows = part_of(h)
        t0[rows] = part[c, g, unit_of(0, h), :].astype(F32)
        for m in (1, 2, 3):
            @pl.when(x + m <= 3)
            def _():
                net.arrived(xr.at[g, m - 1, rows], u_in[g, h, m])
                t0[rows] += xr[g, m - 1, rows].astype(F32)

            @pl.when((x + m > 3) & row1)
            def _():
                net.arrived(xr.at[g, m - 1, rows], u_in[g, h, m])
                part[c, g, unit_of(4, h), :] = (
                    part[c, g, unit_of(4, h), :].astype(F32) + xr[g, m - 1, rows].astype(F32)
                ).astype(BF)

        net.go(part.at[c, g, unit_of(4, h)], yr.at[g, rows], near, v_out, v_in[g, h], row1)
        part[c, g, unit_of(0, h), :] = t0[rows].astype(BF)

    def c4(g, h=None):
        rows = part_of(h)
        t0[rows] = part[c, g, unit_of(0, h), :].astype(F32)

        @pl.when(p.yl == 0)
        def _():
            net.arrived(yr.at[g, rows], v_in[g, h])
            t0[rows] += yr[g, rows].astype(F32)

        @pl.when(c == 0)
        def _():
            raw = kraw[g, rows]
            r = lax.rsqrt(jnp.mean(raw * raw, axis=1, keepdims=True) + EPS)
            xhat = raw * r
            dy = t0[rows]
            kacc[...] += jnp.sum(dy * xhat, axis=0, keepdims=True)
            dxh = dy * kg[...]
            dx = r * (dxh - xhat * jnp.mean(xhat * dxh, axis=1, keepdims=True))
            gb[0, g, z, rows] = dx.astype(BF)

        @pl.when(c == 1)
        def _():
            gb[1, g, z, rows] = t0[rows].astype(BF)

        ref = gb.at[c, g, z, rows]
        for d in (1, 3, 2):
            net.go(ref, ref, zd[d], z_out, z_in[g, h])

    def d1(g, h=None):
        rows = part_of(h)
        net.arrived(gb.at[c, g, pl.ds(0, 3), rows], z_in[g, h])
        ref = gb.at[c, g, :, rows]
        net.go(ref, ref, sib, w_out2, w_in[g, h])

    def offset(g, t):
        return g * 48 + t * 20

    def weight_terms(g):
        for gg, h in pieces:
            if gg == g:
                net.arrived(gb.at[c, g, :, part_of(h)], w_in[g, h])
        lhs = jnp.concatenate([hb[i] for i in range(8)], axis=1)
        rhs = jnp.concatenate([gb[0, g].reshape(8 * TOK, HD), gb[1, g].reshape(8 * TOK, HD)], axis=1)
        gf[...] = jnp.dot(lhs, rhs, preferred_element_type=F32)
        for i in range(16):
            for t in range(2):
                st[i, pl.ds(offset(g, t), 20), :] = gf[pl.ds(i * 20, 20), t * HD:(t + 1) * HD]

    r_in = [net.incoming() for _ in CUTS]

    def scatter(n):
        rows = CUTS[n]
        for i in range(16):
            rbs[i, rows] = st[i, rows].astype(BF)
        out = net.outgoing(rbs.at[pl.ds(0, 15), rows])
        for o, dev in peers:
            net.go(rbs.at[o, rows], rbr.at[me16, rows], dev, out, r_in[n])
        rbr[me16, rows] = rbs[me16, rows]

    def collect(n):
        rows = CUTS[n]
        net.arrived(rbr.at[pl.ds(0, 15), rows], r_in[n])
        total = rbr[0, rows].astype(F32)
        for i in range(1, 16):
            total = total + rbr[i, rows].astype(F32)
        stf[rows] = total
        for t in range(2):
            at = (t * 4 + n) * HD
            gw[:, at:at + HD] = stf[pl.ds(offset(n, t), 20), :].astype(BF)

    w_in_sib = net.incoming()

    share_out = net.outgoing(wbuf.at[pl.ds(0, 7), pl.ds(0, 4)])

    def weight_share(n):
        for f in (home + p.zs(1), home + p.zs(2), home + p.zs(3), away, away + 1, away + 2, away + 3):
            ref = wbuf.at[f, cj + n]
            net.go(ref, ref, sib, share_out, w_in_sib)

    project(0)
    relay(2)
    prep(3)
    project(1)
    spread(0)
    relay(3)
    window_mask()
    clear()
    project(2)
    spread(1)
    share(0)
    exchange_hidden()
    project(3)

    todo = {
        0: [lambda: spread(2), lambda: share(1), lambda: spread(3)],
        1: [lambda: c1(0), lambda: share(2)],
        3: [lambda: c2(0), lambda: share(3), lambda: c1(1), lambda: weight_share(0)],
        5: [lambda: c2(1), lambda: c1(2), lambda: weight_share(1), lambda: weight_share(2)],
        6: [lambda: c3(0), lambda: weight_share(3)],
        7: [lambda: c1(3), lambda: c2(2)],
    }
    for g in range(KVH):
        head = open_head(g)
        for pair in range(GROUP // STEP):
            attend(g, pair, head)
            if pair == GROUP // STEP - 1:
                close_head(g)
            for fn in todo.get(g * (GROUP // STEP) + pair, ()):
                fn()

    c3(1)
    c2(3)
    c4(0)
    c4(1)
    c3(2)
    c3(3, 0)
    c3(3, 1)
    c4(2)
    d1(0)
    c4(3, 0)
    c4(3, 1)
    net.arrived(hpk.at[pl.ds(0, 7)], h_in)
    own_h.wait()
    d1(1)
    weight_terms(0)
    scatter(0)
    a = sum(gacc[:, n * HD:(n + 1) * HD] for n in range(STEP))
    gs1[...] = jnp.concatenate(
        [jnp.sum(a.T, axis=0, keepdims=True), kacc[...], jnp.zeros((6, HD), F32)], axis=0
    )
    g1_in, g2_in = net.incoming(), net.incoming()
    out = net.outgoing(gr1.at[pl.ds(0, 7)])
    for zc, cc in zgroup:
        net.go(gs1, gr1.at[mine], p.at(z=zc, c=cc), out, g1_in)
    gr1[mine] = gs1[...]
    weight_terms(1)
    scatter(1)
    d1(2)
    d1(3, 0)
    d1(3, 1)
    weight_terms(2)
    scatter(2)
    net.arrived(gr1.at[pl.ds(0, 7)], g1_in)
    gs2[...] = jnp.sum(gr1[...], axis=0)
    out = net.outgoing(gr2.at[pl.ds(0, 15)])
    for o, dev in peers:
        net.go(gs2, gr2.at[me16], dev, out, g2_in)
    gr2[me16] = gs2[...]
    weight_terms(3)
    scatter(3)

    net.arrived(wbuf.at[pl.ds(0, 7), pl.ds(0, 4)], w_in_sib)
    tokens = pl.ds(pl.multiple_of(c * TOK, TOK), TOK)
    gkv = jnp.concatenate([gb[t, g, z, tokens, :] for t in range(2) for g in range(KVH)], axis=1)
    for f in range(8):
        wv = jnp.concatenate([wbuf[f, j] for j in range(8)], axis=1)
        ghv[:, f * ROWS:(f + 1) * ROWS] = lax.dot_general(
            gkv, wv, NT, preferred_element_type=F32
        ).astype(BF)
    cp = pltpu.make_async_copy(ghv, gh, loc.at[8])
    cp.start()
    outs.append(cp)
    collect(0)
    collect(1)
    collect(2)
    net.arrived(gr2.at[pl.ds(0, 15)], g2_in)
    gsum[...] = jnp.sum(gr2[...], axis=0)
    collect(3)
    for n, (a, b) in enumerate(((gw, gw_out), (gsum.at[pl.ds(0, 1)], qgo), (gsum.at[pl.ds(1, 1)], kgo))):
        cp = pltpu.make_async_copy(a, b, loc.at[9 + n])
        cp.start()
        outs.append(cp)
    net.drain()
    for cp in outs:
        cp.wait()
    assert net.sends <= NSEND and net.recvs <= NRECV


def finish_kernel(*refs):
    n = (len(refs) - 2) // 3
    ins, outs, held = refs[:n], refs[n:2 * n], refs[2 * n:3 * n]
    sem_in, sem_out = refs[3 * n:]
    jobs = []
    for a, b, h in zip(ins, outs, held):
        parts = 4 if a.shape[0] == TOK else 1
        width = a.shape[1] // parts
        for i in range(parts):
            at = (slice(None), pl.ds(i * width, width))
            j = len(jobs)
            jobs.append((
                pltpu.make_async_copy(a.at[at], h.at[at], sem_in.at[j]),
                pltpu.make_async_copy(h.at[at], b.at[at], sem_out.at[j]),
            ))
    for load, _ in jobs:
        load.start()
    for load, store in jobs:
        load.wait()
        store.start()
    for _, store in jobs:
        store.wait()


def shards(hidden, queries, doc_ids, kv_weight, q_gain, k_gain, grad_out):
    hbm = pl.BlockSpec(memory_space=pl.ANY)
    sds = jax.ShapeDtypeStruct
    vmem = pltpu.VMEM
    wide = 32 * HD
    att, dq, gh, gw, qgo, kgo = pl.pallas_call(
        mega_kernel,
        out_shape=(
            sds((TOK, wide), BF),
            sds((TOK, wide), BF),
            sds((TOK, D), BF),
            sds((20, 1024), BF),
            sds((1, HD), F32),
            sds((1, HD), F32),
        ),
        in_specs=[hbm] * 7,
        out_specs=(hbm,) * 6,
        scratch_shapes=[
            vmem((16, TOK), jnp.int32),
            vmem((1, HD), F32),
            vmem((1, HD), F32),
            vmem((20, 1024), BF),
            vmem((8, HD), F32),
            vmem((8, 8, ROWS, 128), BF),
            vmem((2, TOK, D), BF),
            vmem((D, TOK), F32),
            vmem((8, ROWS, TOK), BF),
            vmem((8, ROWS, TOK), BF),
            vmem((2, KVH, 5 * UNIT, HD), BF),
            vmem((KVH, UNIT, HD), F32),
            vmem((TOK, wide), BF),
            vmem((TOK, wide), BF),
            vmem((HD, wide), F32),
            vmem((8, wide), F32),
            vmem((HD, wide), F32),
            vmem((KVH, HD, GROUP * TOK), BF),
            vmem((HD, GROUP * TOK), BF),
            vmem((WROWS, GROUP * TOK), BF),
            vmem((WROWS, GROUP * TOK), BF),
            vmem((WROWS, TOK), F32),
            vmem((TOK, wide), BF),
            vmem((TOK, wide), BF),
            vmem((TOK, D), BF),
            vmem((2, KVH, 5 * UNIT, HD), BF),
            vmem((KVH, 5 * UNIT, HD), BF),
            vmem((KVH, 3, UNIT, HD), BF),
            vmem((KVH, UNIT, HD), BF),
            vmem((UNIT, HD), F32),
            vmem((2, KVH, 4, UNIT, HD), BF),
            vmem((ROWS, 2 * HD), F32),
            vmem((16, 192, HD), F32),
            vmem((16, 192, HD), BF),
            vmem((16, 192, HD), BF),
            vmem((192, HD), F32),
            vmem((HD, STEP * HD), F32),
            vmem((1, HD), F32),
            vmem((8, HD), F32),
            vmem((8, 8, HD), F32),
            vmem((8, HD), F32),
            vmem((16, 8, HD), F32),
            pltpu.SemaphoreType.DMA((NSEND,)),
            pltpu.SemaphoreType.DMA((NRECV,)),
            pltpu.SemaphoreType.DMA((15,)),
        ],
        compiler_params=pltpu.CompilerParams(
            collective_id=0, has_side_effects=True, vmem_limit_bytes=60 * 1024 * 1024
        ),
        name="mega",
    )(
        kv_weight, hidden[0], queries[0], grad_out[0], doc_ids[0].reshape(16, TOK),
        q_gain.reshape(1, HD), k_gain.reshape(1, HD),
    )
    results = (att, dq, gh, gw, qgo, kgo)
    att, dq, gh, gw, qgo, kgo = pl.pallas_call(
        finish_kernel,
        out_shape=tuple(sds(r.shape, r.dtype) for r in results),
        in_specs=[hbm] * 6,
        out_specs=(hbm,) * 6,
        scratch_shapes=[vmem(r.shape, r.dtype) for r in results]
        + [pltpu.SemaphoreType.DMA((15,))] * 2,
        compiler_params=pltpu.CompilerParams(vmem_limit_bytes=60 * 1024 * 1024),
        name="finish",
    )(*results)
    return (att[None], dq[None], gh[None], gw, qgo.reshape(HD), kgo.reshape(HD))


def solution(mesh):
    return jax.shard_map(
        shards,
        mesh=mesh,
        in_specs=(
            P("fsdp", "seq", None),
            P("fsdp", "seq", None),
            P("fsdp", None),
            P("fsdp", None),
            P(),
            P(),
            P("fsdp", "seq", None),
        ),
        out_specs=(
            P("fsdp", "seq", None),
            P("fsdp", "seq", None),
            P("fsdp", "seq", None),
            P(("seq", "fsdp"), None),
            P(),
            P(),
        ),
        check_vma=False,
    )
```
